32 devices in a mesh: gx: 4 (over z), gy: 4 (over y, x), gz: 2 (over core).
Axes of the slice: x: 2, y: 2, z: 4, core: 2. Of those that a mesh axis runs over, the one named last changes fastest.
Arguments:
- right_side: float32 [192, 192, 256], P('gx', 'gy', 'gz'), may hold values from -6 to 6
- conductance: bfloat16 [192, 192, 256], P('gx', 'gy', 'gz'), may hold values from 0.29882812 to 3
- axis_conductivity: float32 [3], replicated, may hold values from 0.4 to 2.5
- x_vectors: float32 [56, 56], replicated, may hold values from -1 to 2
- y_vectors: float32 [56, 56], replicated, may hold values from -1 to 2
- z_vectors: float32 [72, 72], replicated, may hold values from -1 to 2
- x_values: float32 [56], replicated, may hold values from 0.05 to 4
- y_values: float32 [56], replicated, may hold values from 0.05 to 4
- z_values: float32 [72], replicated, may hold values from 0.05 to 4
- coarse_inverse: float32 [16, 16], replicated, may hold values from -1 to 4
Outputs:
- solution: float32 [192, 192, 256], P('gx', 'gy', 'gz')
- residual: float32 [192, 192, 256], P('gx', 'gy', 'gz')
The draws below stay inside these ranges and needn't reach their ends.
All inputs are finite; a program needn't handle non-finite values.
Results may differ from the reference program's by a relative error of at most 0.0003.
Values may be sent and summed in bfloat16 or wider, within the bound.
No kernel may reach another device: no remote copies, remote signals or barrier semaphores. Data moves between devices by JAX's collectives and lax.ppermute only.
A program may use at most 64 MiB of HBM per device.

```python
import math
import jax
import jax.numpy as jnp
from jax import lax

CX = 48
CY = 48
SZ = 64
OV = 4
ITERS = 1
CZ = 128
EX = 56
EY = 56
EZ = 72
NX = 192
NY = 192
NZ = 256
COARSE = 16
N_GX = 4
N_GY = 4
N_GZ = 2


def near_identity(key, size, spread):
    noise = jax.random.uniform(key, (size, size), jnp.float32, -spread / size, spread / size)
    return jnp.eye(size, dtype=jnp.float32) + noise


def draw_right_side(key, part):
    key = jax.random.fold_in(key, 3)
    rough_key, block_key = jax.random.split(key)
    block_shape = (NX // CX, NY // CY, NZ // SZ)
    rough = jnp.clip(jax.random.normal(rough_key, (NX, NY, NZ), jnp.float32), -4.0, 4.0)
    blocks = jnp.clip(jax.random.normal(block_key, block_shape, jnp.float32), -2.0, 2.0)
    blocks = jnp.repeat(jnp.repeat(jnp.repeat(blocks, CX, 0), CY, 1), SZ, 2)
    return rough + blocks


def draw_x_vectors(key, part):
    key = jax.random.fold_in(key, 11)
    return near_identity(key, EX, 1.2)


def draw_y_vectors(key, part):
    key = jax.random.fold_in(key, 13)
    return near_identity(key, EY, 1.2)


def draw_z_vectors(key, part):
    key = jax.random.fold_in(key, 17)
    return near_identity(key, EZ, 1.2)


def symmetric_dominant(key, size, lowest, highest):
    diag_key, off_key = jax.random.split(key)
    diagonal = jax.random.uniform(diag_key, (size,), jnp.float32, lowest, highest)
    spread = 0.8 / size
    noise = jax.random.uniform(off_key, (size, size), jnp.float32, -spread, spread)
    return (noise + noise.T) * 0.5 + jnp.diag(diagonal)


def draw_coarse_inverse(key, part):
    key = jax.random.fold_in(key, 29)
    return symmetric_dominant(key, COARSE, 1.0, 2.0)


def block_scale(key, extent, pieces, smallest, top_value):
    level, own = 1.0, jax.random.fold_in(key, 6)
    for axis_at, parts in pieces:
        draws = jnp.exp(jax.random.uniform(jax.random.fold_in(own, axis_at), (parts,), jnp.float32, smallest / len(pieces), top_value / len(pieces)))
        level = level * jnp.repeat(draws, extent[axis_at] // parts).reshape([-1 if axis == axis_at else 1 for axis in range(len(extent))])
    return level


def setup_inputs(seed: int = 0) -> dict:
    seeds = jax.random.split(jax.random.key(seed), 11)
    return {
        "right_side": draw_right_side(jax.random.fold_in(seeds[10], 71), 0),
        "conductance": jnp.clip(jnp.exp(math.log(3.0) - 2.306499 * jax.random.uniform(seeds[1], (NX, NY, NZ), jnp.float32) ** block_scale(seeds[1], (NX, NY, NZ), ((0, 4), (1, 4), (2, 2)), -0.2, 0.2)), 0.29882812, 3.0).astype(jnp.bfloat16),
        "axis_conductivity": jnp.clip(jnp.exp(jax.random.uniform(seeds[2], (3,), jnp.float32, math.log(0.4), math.log(2.5))), 0.4, 2.5),
        "x_vectors": draw_x_vectors(jax.random.fold_in(seeds[10], 71), 0),
        "y_vectors": draw_y_vectors(jax.random.fold_in(seeds[10], 71), 0),
        "z_vectors": draw_z_vectors(jax.random.fold_in(seeds[10], 71), 0),
        "x_values": jnp.clip(jnp.exp(jax.random.uniform(seeds[6], (EX,), jnp.float32, math.log(0.05), math.log(4.0))), 0.05, 4.0),
        "y_values": jnp.clip(jnp.exp(jax.random.uniform(seeds[7], (EY,), jnp.float32, math.log(0.05), math.log(4.0))), 0.05, 4.0),
        "z_values": jnp.clip(jnp.exp(jax.random.uniform(seeds[8], (EZ,), jnp.float32, math.log(0.05), math.log(4.0))), 0.05, 4.0),
        "coarse_inverse": draw_coarse_inverse(jax.random.fold_in(seeds[10], 71), 0),
    }


exact_mode = lax.Precision.HIGHEST


def apply_operator(padded_field, padded_scale, axis_conductivity):
    center = padded_field[1:-1, 1:-1, 1:-1]
    own_scale = padded_scale[1:-1, 1:-1, 1:-1]
    summed = jnp.zeros(center.shape, jnp.float32)
    for dimension in range(3):
        for offset in (0, 2):
            selection = [slice(1, -1), slice(1, -1), slice(1, -1)]
            selection[dimension] = slice(offset, offset + center.shape[dimension])
            neighbour = padded_field[tuple(selection)]
            other_scale = padded_scale[tuple(selection)]
            weight = axis_conductivity[dimension] * 0.5 * (own_scale + other_scale)
            summed = summed + weight * (center - neighbour)
    return summed


def split_windows(padded, dimension, core):
    moved = jnp.moveaxis(padded, dimension, 0)
    count = (moved.shape[0] - 2 * OV) // core
    rest = moved.shape[1:]
    lowers = moved[:count * core].reshape((count, core) + rest)[:, :OV]
    middle = moved[OV:OV + count * core].reshape((count, core) + rest)
    uppers = moved[2 * OV:2 * OV + count * core].reshape((count, core) + rest)[:, core - OV:]
    joined = jnp.concatenate([lowers, middle, uppers], axis=1)
    return jnp.moveaxis(joined, (0, 1), (dimension, dimension + 1))


def join_windows(windows, dimension, core):
    moved = jnp.moveaxis(windows, (dimension, dimension + 1), (0, 1))
    count = moved.shape[0]
    rest = moved.shape[2:]
    middle = moved[:, OV:OV + core]
    zero_rim = jnp.zeros_like(moved[:1, :OV])
    previous_high = jnp.concatenate([zero_rim, moved[:-1, OV + core:]], axis=0)
    following_low = jnp.concatenate([moved[1:, :OV], zero_rim], axis=0)
    middle = middle.at[:, :OV].add(previous_high)
    middle = middle.at[:, core - OV:].add(following_low)
    flat = middle.reshape((count * core,) + rest)
    return jnp.moveaxis(flat, 0, dimension)


def local_part(field, x_vectors, y_vectors, z_vectors, denominators):
    padded = jnp.pad(field, OV)

    def one_slab(start):
        slab = lax.dynamic_slice_in_dim(padded, start * CX, CX + 2 * OV, 0)
        window = split_windows(slab, 1, CY)
        window = split_windows(window, 3, SZ)
        first = jnp.einsum("abcde,ai->ibcde", window, x_vectors, precision=exact_mode)
        second = jnp.einsum("ibcde,cj->ibjde", first, y_vectors, precision=exact_mode)
        third = jnp.einsum("ibjde,ek->ibjdk", second, z_vectors, precision=exact_mode)
        scaled = third / denominators[:, None, :, None, :]
        back_z = jnp.einsum("ibjdk,ek->ibjde", scaled, z_vectors, precision=exact_mode)
        back_y = jnp.einsum("ibjde,cj->ibcde", back_z, y_vectors, precision=exact_mode)
        spread = jnp.einsum("ibcde,ai->abcde", back_y, x_vectors, precision=exact_mode)
        return join_windows(join_windows(spread, 3, SZ), 1, CY)

    slabs = lax.map(one_slab, jnp.arange(NX // CX, dtype=jnp.int32))
    return join_windows(slabs, 0, CX)


def reference(right_side, conductance, axis_conductivity, x_vectors, y_vectors, z_vectors, x_values, y_values, z_values, coarse_inverse):
    scale_pad = jnp.pad(conductance.astype(jnp.float32), 1)
    denominators = (axis_conductivity[0] * x_values[:, None, None]
                    + axis_conductivity[1] * y_values[None, :, None]
                    + axis_conductivity[2] * z_values[None, None, :])

    def precondition(field):
        local = local_part(field, x_vectors, y_vectors, z_vectors, denominators)
        blocks = field.reshape(N_GX, CX, N_GY, CY, N_GZ // 2, 2 * CZ)
        sums = jnp.sum(blocks, axis=(1, 3, 5)).reshape(-1)
        coarse_value = jnp.dot(coarse_inverse, sums / (2.0 * CX * CY * CZ), precision=exact_mode)
        lifted = local.reshape(N_GX, CX, N_GY, CY, N_GZ // 2, 2 * CZ) + coarse_value.reshape(N_GX, 1, N_GY, 1, N_GZ // 2, 1)
        return lifted.reshape(NX, NY, NZ)

    solution = jnp.zeros_like(right_side)
    residual = right_side
    shifted = precondition(residual)
    product_now = jnp.sum(residual * shifted)
    direction = shifted
    for number in range(ITERS):
        applied = apply_operator(jnp.pad(direction, 1), scale_pad, axis_conductivity)
        step_size = product_now / jnp.sum(direction * applied)
        solution = solution + step_size * direction
        residual = residual - step_size * applied
        if number + 1 < ITERS:
            shifted = precondition(residual)
            product_next = jnp.sum(residual * shifted)
            direction = shifted + (product_next / product_now) * direction
            product_now = product_next
    return solution, residual
```

```python
import functools

import jax
import jax.numpy as jnp
from jax import lax
from jax.experimental import pallas as pl
from jax.experimental.pallas import tpu as pltpu
from jax.sharding import PartitionSpec as P

SZ = 64
OV = 4
RIM = OV + 1
LANES = 128
SLOT = 8
GROUP = LANES // SLOT
F32 = jnp.float32
BF16 = jnp.bfloat16
MESH_AXES = ("gx", "gy", "gz")

VMEM = pl.BlockSpec(memory_space=pltpu.VMEM)
SMEM = pl.BlockSpec(memory_space=pltpu.SMEM)
ANY = pl.BlockSpec(memory_space=pl.ANY)


def call(kernel, name, outs, args, spaces, scratch=(), limit=8, out_specs=None, aliases=None, flops=0):
    size = sum(o.size * o.dtype.itemsize for o in outs) + sum(a.size * a.dtype.itemsize for a in args)
    return pl.pallas_call(
        kernel,
        out_shape=outs,
        in_specs=spaces,
        out_specs=out_specs or [VMEM] * len(outs),
        scratch_shapes=list(scratch),
        input_output_aliases=aliases or {},
        name=name,
        compiler_params=pltpu.CompilerParams(vmem_limit_bytes=limit * 2**20),
        cost_estimate=pl.CostEstimate(flops=flops, bytes_accessed=size, transcendentals=0),
    )(*args)


def shape(dims, dtype=F32):
    return jax.ShapeDtypeStruct(tuple(dims), dtype)


def halves(value):
    high = value.astype(BF16)
    return high, (value - high.astype(F32)).astype(BF16)


def dot(left, right):
    return jnp.dot(left, right, preferred_element_type=F32)


def iota(dims, axis):
    return lax.broadcasted_iota(jnp.int32, dims, axis)


def one_hot(condition):
    return jnp.where(condition, 1.0, 0.0).astype(BF16)


IX, IY, IZ, SIDE = 0, 1, 2, 3


def place_vector(sizes):
    ix, iy, iz = (lax.axis_index(a) for a in MESH_AXES)
    nz = sizes["gz"]
    if nz == 2:
        sides = [jnp.where(iz == 0, 1, 0), jnp.ones((), jnp.int32)]
    else:
        sides = [jnp.ones((), jnp.int32), jnp.where(iz < nz - 1, 1, 0), jnp.zeros((), jnp.int32), jnp.where(iz > 0, 1, 0)]
    return jnp.stack([ix, iy, iz] + sides).astype(jnp.int32)


def swap_sides(messages, sizes):
    count = sizes["gz"]
    if count == 2:
        return [lax.ppermute(messages[0], "gz", [(0, 1), (1, 0)])]
    up = [(i, (i + 1) % count) for i in range(count)]
    down = [((i + 1) % count, i) for i in range(count)]
    return [lax.ppermute(messages[1], "gz", down), lax.ppermute(messages[0], "gz", up)]


def swap_ends(low, high, axis, sizes):
    count = sizes[axis]
    up = [(i, (i + 1) % count) for i in range(count)]
    down = [((i + 1) % count, i) for i in range(count)]
    return lax.ppermute(high, axis, up), lax.ppermute(low, axis, down)


def prepare_kernel(sides, place, axes, xv, yv, zv, y_row, z_row, fx, bx, fy, by, wz, bz, den, pad, wide, rows):
    ez = zv.shape[0]
    depth = wz.shape[0] // 4

    def stacked(value, out):
        high, low = halves(value[: LANES // 2])
        high, low = high.astype(F32), low.astype(F32)
        half = jnp.where(iota(high.shape, 1) < LANES // 2, high, pltpu.roll(high, LANES // 2, 1))
        out[0 : LANES // 2] = half.astype(BF16)
        out[LANES // 2 :] = low.astype(BF16)

    for vectors, forward, back in ((xv, fx, bx), (yv, fy, by)):
        pad[...] = jnp.zeros_like(pad)
        pad[0 : vectors.shape[0], 0 : vectors.shape[1]] = vectors[...]
        stacked(pad[...], back)
        stacked(pad[...].T, forward)

    wide[...] = jnp.zeros_like(wide)
    wide[0:ez, 0:ez] = zv[...]
    wide[SZ : SZ + ez, LANES : LANES + ez] = zv[...]
    middle = wide[OV : OV + depth]
    high, low = halves(middle)
    wz[0:depth] = high
    wz[depth : 2 * depth] = high
    wz[2 * depth : 3 * depth] = low
    rows[...] = jnp.zeros_like(rows)
    for side in range(sides):
        is_high = place[SIDE + 2 * side] > 0
        for k in range(OV):
            top, bottom = OV + depth + k, OV - 1 - k
            row = jnp.where(is_high, wide[top : top + 1], wide[bottom : bottom + 1])
            row_high, row_low = halves(row)
            at = 3 * SLOT * side + k
            rows[at : at + 1] = row_high.astype(F32)
            rows[at + SLOT : at + SLOT + 1] = row_high.astype(F32)
            rows[at + 2 * SLOT : at + 2 * SLOT + 1] = row_low.astype(F32)
    wz[3 * depth :] = rows[...].astype(BF16)

    rows[...] = jnp.zeros_like(rows)
    for side in range(sides):
        is_high = place[SIDE + 2 * side] > 0
        for k in range(RIM):
            top, bottom = OV + depth - 1 + k, OV - k
            rows[SLOT * side + k : SLOT * side + k + 1] = jnp.where(is_high, wide[top : top + 1], wide[bottom : bottom + 1])
    across = 2 * LANES
    for at, part in ((0, middle), (LANES, rows[...])):
        turned = jnp.concatenate([part[:, 0:LANES].T, part[:, LANES:].T], axis=0)
        high, low = halves(turned)
        bz[0:across, at : at + LANES] = high
        bz[across : 2 * across, at : at + LANES] = high
        bz[2 * across :, at : at + LANES] = low

    ey = yv.shape[0]
    diagonal = iota((ey, ey), 0) == iota((ey, ey), 1)
    y_column = jnp.sum(jnp.where(diagonal, y_row[...], 0.0), axis=1, keepdims=True)
    pad[...] = jnp.ones_like(pad)
    pad[0:1, 0:ez] = axes[2] * z_row[...]
    den[...] = axes[1] * y_column + pad[0:1]


def pack_x_kernel(right, scale, low, high):
    ext_x, ext_y, depth = right.shape
    for out, start, face in ((low, 0, 0), (high, ext_x - OV, ext_x - 1)):
        for t in range(OV):
            out[t * ext_y : (t + 1) * ext_y] = right[start + t]
        out[OV * ext_y :] = scale[face].astype(F32)


def pack_y_kernel(place, sizes, right, scale, x_low, x_high, low, high):
    ext_x, ext_y, depth = right.shape
    from_low = place[IX] > 0
    from_high = place[IX] < sizes["gx"] - 1
    for a in range(ext_x + 2 * OV):
        for out, start in ((low, 0), (high, ext_y - OV)):
            if a < OV:
                rows = jnp.where(from_low, x_low[a * ext_y + start : a * ext_y + start + OV], 0.0)
            elif a < ext_x + OV:
                rows = right[a - OV, start : start + OV]
            else:
                at = (a - OV - ext_x) * ext_y + start
                rows = jnp.where(from_high, x_high[at : at + OV], 0.0)
            out[a * OV : (a + 1) * OV] = rows
    base = (ext_x + 2 * OV) * OV
    for x in range(ext_x):
        low[base + x : base + x + 1] = scale[x, 0:16].astype(F32)[0:1]
        high[base + x : base + x + 1] = scale[x, ext_y - 16 : ext_y].astype(F32)[15:16]


def extend_kernel(sizes, sides, place, right, scale, x_low, x_high, y_low, y_high, ext, *messages):
    ext_x, ext_y, depth = right.shape
    wide_x, wide_y = ext_x + 2 * OV, ext_y + 2 * OV
    x_from_low, x_from_high = place[IX] > 0, place[IX] < sizes["gx"] - 1
    y_from_low, y_from_high = place[IY] > 0, place[IY] < sizes["gy"] - 1
    for a in range(wide_x):
        if a < OV:
            core = jnp.where(x_from_low, x_low[a * ext_y : (a + 1) * ext_y], 0.0)
        elif a < ext_x + OV:
            core = right[a - OV]
        else:
            at = (a - OV - ext_x) * ext_y
            core = jnp.where(x_from_high, x_high[at : at + ext_y], 0.0)
        ext[a * wide_y + OV : a * wide_y + OV + ext_y] = core
        ext[a * wide_y : a * wide_y + OV] = jnp.where(y_from_low, y_low[a * OV : (a + 1) * OV], 0.0)
        ext[a * wide_y + OV + ext_y : (a + 1) * wide_y] = jnp.where(y_from_high, y_high[a * OV : (a + 1) * OV], 0.0)
    lane = iota((depth, LANES), 1)
    cell = iota((depth, LANES), 0)
    slot = lax.rem(lane, SLOT)
    for side in range(sides):
        is_high = place[SIDE + 2 * side] > 0
        target = jnp.where(is_high, depth - 1 - slot, slot)
        face = jnp.where(is_high, depth - 1, 0)
        picks = jnp.where((target == cell) & (slot < OV), 1.0, 0.0)
        face_picks = jnp.where((cell == face) & (slot == OV), 1.0, 0.0)
        for group in range((wide_x + GROUP - 1) // GROUP):
            total = jnp.zeros((wide_y, LANES), F32)
            total_face = jnp.zeros((ext_y, LANES), F32)
            for q in range(GROUP):
                a = group * GROUP + q
                mine = lane // SLOT == q
                if a < wide_x:
                    high, low = halves(ext[a * wide_y : (a + 1) * wide_y])
                    pick = jnp.where(mine, picks, 0.0).astype(BF16)
                    total = total + dot(jnp.concatenate([high, low], axis=1), jnp.concatenate([pick, pick], axis=0))
                if a < ext_x:
                    total_face = total_face + dot(scale[a], jnp.where(mine, face_picks, 0.0).astype(BF16))
            messages[side][group * wide_y : (group + 1) * wide_y] = total
            messages[side][group * wide_y : group * wide_y + ext_y] += total_face


def solve_kernel(sides, place, axes, x_values, ext, *refs):
    received, refs = refs[:sides], refs[sides:]
    fx, bx, fy, by, wz, bz, den, local = refs[:8]
    messages, refs = refs[8 : 8 + sides], refs[8 + sides :]
    first_a, first_b, second_a, second_b = refs
    wide = x_values.shape[0]
    rows = ext.shape[0]
    wide_y = rows // wide
    batch = 8
    lane = iota((wide_y, LANES), 1)

    def along(matrix, pair):
        value = jnp.concatenate(pair, axis=1)
        fill = jnp.zeros((LANES // 2 - value.shape[0], value.shape[1]), F32)
        high, low = halves(jnp.concatenate([value, fill], axis=0))
        out = dot(matrix[...], jnp.concatenate([high, low], axis=0))
        return out[0 : value.shape[0]] + out[LANES // 2 : LANES // 2 + value.shape[0]]

    for start in range(0, wide, batch):
        block = pl.ds(start * wide_y, batch * wide_y)
        high, low = halves(ext[block])
        rims = []
        for a in range(start, start + batch):
            group, q = a // GROUP, a % GROUP
            piece = jnp.zeros((wide_y, LANES), F32)
            for side in range(sides):
                value = received[side][group * wide_y : (group + 1) * wide_y]
                value = jnp.where((lane // SLOT == q) & (place[SIDE + 2 * side + 1] > 0), value, 0.0)
                value_high, value_low = halves(value)
                value_high, value_low = value_high.astype(F32), value_low.astype(F32)
                at = LANES - SLOT * q + 3 * SLOT * side
                piece = piece + pltpu.roll(value_high, at % LANES, 1)
                piece = piece + pltpu.roll(value_low, (at + SLOT) % LANES, 1)
                piece = piece + pltpu.roll(value_high, (at + 2 * SLOT) % LANES, 1)
            rims.append(piece.astype(BF16))
        left = jnp.concatenate([high, low, high, jnp.concatenate(rims, axis=0)], axis=1)
        out = dot(left, wz[...])
        first_a[block] = out[:, 0:LANES]
        first_b[block] = out[:, LANES:]

    def strided(refs_pair, at, count, stride):
        return [ref[pl.ds(at, count, stride=stride), :] for ref in refs_pair]

    def x_forward(y):
        out = along(fx, strided((first_a, first_b), y, wide, wide_y))
        second_a[pl.ds(y * wide, wide)] = out[:, 0:LANES]
        second_b[pl.ds(y * wide, wide)] = out[:, LANES:]

    def y_both(i):
        out = along(fy, strided((second_a, second_b), i, wide_y, wide))
        inverse = 1.0 / (axes[0] * x_values[i] + den[...])
        out = along(by, [out[:, 0:LANES] * inverse, out[:, LANES:] * inverse])
        first_a[pl.ds(i * wide_y, wide_y)] = out[:, 0:LANES]
        first_b[pl.ds(i * wide_y, wide_y)] = out[:, LANES:]

    def x_back(y):
        out = along(bx, strided((first_a, first_b), y, wide, wide_y))
        second_a[pl.ds(y, wide, stride=wide_y), :] = out[:, 0:LANES]
        second_b[pl.ds(y, wide, stride=wide_y), :] = out[:, LANES:]

    for step, count in ((x_forward, wide_y), (y_both, wide), (x_back, wide_y)):

        def several(block, carry, step=step):
            for inner in range(8):
                step(block * 8 + inner)
            return carry

        lax.fori_loop(0, count // 8, several, 0)

    totals = [[jnp.zeros((wide_y, LANES), F32) for _ in range((wide + GROUP - 1) // GROUP)] for _ in range(sides)]
    for start in range(0, wide, batch):
        block = pl.ds(start * wide_y, batch * wide_y)
        high_a, low_a = halves(second_a[block])
        high_b, low_b = halves(second_b[block])
        out = dot(jnp.concatenate([high_a, high_b, low_a, low_b, high_a, high_b], axis=1), bz[...])
        local[block] = out[:, 0:LANES]
        for a in range(start, start + batch):
            group, q = a // GROUP, a % GROUP
            value = out[(a - start) * wide_y : (a - start + 1) * wide_y, LANES:]
            for side in range(sides):
                own = value if sides == 1 else jnp.where(lane // SLOT == side, value, 0.0)
                at = (SLOT * q + LANES - SLOT * side) % LANES
                totals[side][group] = totals[side][group] + (pltpu.roll(own, at, 1) if at else own)
    for side in range(sides):
        for group, total in enumerate(totals[side]):
            messages[side][group * wide_y : (group + 1) * wide_y] = total


def fold_z_kernel(sides, wide, place, local, *refs):
    own, received = refs[:sides], refs[sides : 2 * sides]
    out, refs = refs[2 * sides], refs[2 * sides + 1 :]
    faces, (low_end, high_end) = refs[:sides], refs[sides:]
    rows = local.shape[0]
    wide_y = rows // wide
    groups = (wide + GROUP - 1) // GROUP
    lane = iota((LANES, LANES), 0)
    cell = iota((LANES, LANES), 1)
    slot = lax.rem(lane, SLOT)
    wide_lane = iota((groups * wide_y, LANES), 1)
    pairs = []
    for side in range(sides):
        value = jnp.where(place[SIDE + 2 * side + 1] > 0, received[side][...], 0.0)
        both = value + pltpu.roll(own[side][...], LANES - 1, 1)
        inside = (lax.rem(wide_lane, SLOT) == 0) & (place[SIDE + 2 * side + 1] > 0)
        faces[side][...] = jnp.where(inside, both, 0.0)
        high, low = halves(value)
        pairs.append(jnp.concatenate([high, low], axis=1))
    for a in range(wide):
        group, q = a // GROUP, a % GROUP
        value = local[a * wide_y : (a + 1) * wide_y]
        for side in range(sides):
            is_high = place[SIDE + 2 * side] > 0
            target = jnp.where(is_high, LANES - slot, slot - 1)
            put = one_hot((lane // SLOT == q) & (slot >= 1) & (slot <= OV) & (cell == target))
            value = value + dot(pairs[side][group * wide_y : (group + 1) * wide_y], jnp.concatenate([put, put], axis=0))
        out[a * wide_y : (a + 1) * wide_y] = value
    ends = RIM * wide_y
    low_end[0:ends] = out[0:ends]
    high_end[0:ends] = out[rows - ends : rows]
    for side in range(sides):
        low_end[ends + side * wide_y : ends + (side + 1) * wide_y] = faces[side][0:wide_y]
        high_end[ends + side * wide_y : ends + (side + 1) * wide_y] = faces[side][(groups - 1) * wide_y :]


def fold_x_kernel(sizes, sides, wide, place, field, *refs):
    faces, refs = refs[:sides], refs[sides:]
    x_low, x_high, out = refs[:3]
    out_faces, (low_end, high_end) = refs[3 : 3 + sides], refs[3 + sides :]
    rows = field.shape[0]
    wide_y = rows // wide
    groups = (wide + GROUP - 1) // GROUP
    from_low, from_high = place[IX] > 0, place[IX] < sizes["gx"] - 1
    ends = RIM * wide_y
    low_at, high_at = (OV - 1) * wide_y, (wide - 2 * OV) * wide_y
    out[low_at : low_at + ends] = field[low_at : low_at + ends] + jnp.where(from_low, x_low[0:ends], 0.0)
    out[high_at : high_at + ends] = field[high_at : high_at + ends] + jnp.where(from_high, x_high[0:ends], 0.0)
    lane = iota((wide_y, LANES), 1)
    high_lane = (wide - 2 * OV) % GROUP * SLOT
    for side in range(sides):
        out_faces[side][...] = faces[side][...]
        part = slice(ends + side * wide_y, ends + (side + 1) * wide_y)
        inside = (lane >= (OV - 1) * SLOT) & (lane < 2 * OV * SLOT) & from_low
        out_faces[side][0:wide_y] += jnp.where(inside, x_low[part], 0.0)
        inside = (lane >= high_lane) & (lane < high_lane + RIM * SLOT) & from_high
        out_faces[side][(groups - 1) * wide_y :] += jnp.where(inside, x_high[part], 0.0)
    planes = wide - 2 * OV + 2
    for end, start in ((low_end, 0), (high_end, wide_y - RIM)):
        for p in range(planes):
            at = (p + OV - 1) * wide_y + start
            end[p * RIM : (p + 1) * RIM] = out[at : at + RIM]
        for side in range(sides):
            for group in range(groups):
                at = planes * RIM + (side * groups + group) * RIM
                end[at : at + RIM] = out_faces[side][group * wide_y + start : group * wide_y + start + RIM]


def operator_kernel(sizes, sides, wide, place, axes, field, *refs):
    faces, refs = refs[:sides], refs[sides:]
    y_low, y_high, right, scale, sx_low, sx_high, sy_low, sy_high = refs[:8]
    scale_faces, refs = refs[8 : 8 + sides], refs[8 + sides :]
    direction, applied, z_weight, wx, wy, sums, values, scales, edges = refs
    ext_x, ext_y, depth = right.shape
    wide_y = ext_y + 2 * OV
    groups = (wide + GROUP - 1) // GROUP
    planes = ext_x + 2
    core = slice(8, 8 + ext_y)
    inside = [
        (place[IX] > 0, place[IX] < sizes["gx"] - 1),
        (place[IY] > 0, place[IY] < sizes["gy"] - 1),
        (place[IZ] > 0, place[IZ] < sizes["gz"] - 1),
    ]
    for p in range(planes):
        at = (p + OV - 1) * wide_y
        values[p, 7 : 9 + ext_y] = field[at + OV - 1 : at + OV + ext_y + 1]
        values[p, 7 : 7 + RIM] += jnp.where(inside[1][0], y_low[p * RIM : (p + 1) * RIM], 0.0)
        values[p, 4 + ext_y : 4 + ext_y + RIM] += jnp.where(inside[1][1], y_high[p * RIM : (p + 1) * RIM], 0.0)
    for (axis_low, axis_high), low_at, high_at in (
        (inside[0], (0, slice(None)), (planes - 1, slice(None))),
        (inside[1], (slice(None), slice(7, 8)), (slice(None), slice(8 + ext_y, 9 + ext_y))),
    ):
        values[low_at] = jnp.where(axis_low, values[low_at], 0.0)
        values[high_at] = jnp.where(axis_high, values[high_at], 0.0)
    for side in range(sides):
        for group in range(groups):
            at = side * groups * wide_y + group * wide_y
            edges[at : at + wide_y] = faces[side][group * wide_y : (group + 1) * wide_y]
            row = (ext_x + 2) * RIM + (side * groups + group) * RIM
            edges[at + OV - 1 : at + OV - 1 + RIM] += jnp.where(inside[1][0], y_low[row : row + RIM], 0.0)
            edges[at + ext_y : at + ext_y + RIM] += jnp.where(inside[1][1], y_high[row : row + RIM], 0.0)
    x_rows, y_rows = OV * ext_y, wide * OV
    scales[0, core] = jnp.where(inside[0][0], sx_low[x_rows : x_rows + ext_y], 0.0)
    scales[planes - 1, core] = jnp.where(inside[0][1], sx_high[x_rows : x_rows + ext_y], 0.0)
    for x in range(ext_x):
        scales[x + 1, core] = scale[x].astype(F32)
        scales[x + 1, 7:8] = jnp.where(inside[1][0], sy_low[y_rows + x : y_rows + x + 1], 0.0)
        scales[x + 1, 8 + ext_y : 9 + ext_y] = jnp.where(inside[1][1], sy_high[y_rows + x : y_rows + x + 1], 0.0)

    hx, hy, hz = (0.5 * axes[d] for d in range(3))
    lane = iota((ext_y, depth), 1)
    row_lane = iota((LANES, depth), 0)
    row_cell = iota((LANES, depth), 1)
    zero = jnp.zeros((ext_y, depth), F32)
    sum_right, sum_product, sum_energy, sum_applied, sum_z = zero, zero, zero, zero, zero
    wx[0] = hx * (scales[1, core] + scales[0, core])
    wx[1] = hx * (scales[planes - 2, core] + scales[planes - 1, core])
    x_flux = wx[0] * (values[1, core] - values[0, core])
    for x in range(ext_x):
        mid, own = values[x + 1, core], scales[x + 1, core]
        next_flux = hx * (scales[x + 2, core] + own) * (values[x + 2, core] - mid)
        total = x_flux - next_flux
        x_flux = next_flux
        below, above = slice(7, 7 + ext_y), slice(9, 9 + ext_y)
        weight_below = hy * (own + scales[x + 1, below])
        weight_above = hy * (own + scales[x + 1, above])
        total = total + weight_below * (mid - values[x + 1, below]) + weight_above * (mid - values[x + 1, above])
        wy[0, x : x + 1] = weight_below[0:1]
        wy[1, x : x + 1] = weight_above[ext_y - 1 : ext_y]
        edge_value, edge_scale = zero, zero
        for side in range(sides):
            is_high, valid = place[SIDE + 2 * side] > 0, place[SIDE + 2 * side + 1] > 0
            target = jnp.where(is_high, depth - 1, 0)
            a = x + OV
            at = (side * groups + a // GROUP) * wide_y + OV
            high, low = halves(edges[at : at + ext_y])
            put = one_hot((row_lane == a % GROUP * SLOT) & (row_cell == target))
            edge_value = edge_value + dot(jnp.concatenate([high, low], axis=1), jnp.concatenate([put, put], axis=0))
            at = x // GROUP * wide_y
            face = jnp.where(valid, scale_faces[side][at : at + ext_y], 0.0).astype(BF16)
            put = one_hot((row_lane == x % GROUP * SLOT + OV) & (row_cell == target))
            edge_scale = edge_scale + dot(face, put)
        lower = jnp.where(lane == 0, edge_value, pltpu.roll(mid, 1, 1))
        lower_scale = jnp.where(lane == 0, edge_scale, pltpu.roll(own, 1, 1))
        flux = hz * (own + lower_scale) * (mid - lower)
        ends = (lane == 0) | (lane == depth - 1)
        end_weight = jnp.where(ends, hz * (own + edge_scale), 0.0)
        upper = jnp.where(lane == depth - 1, end_weight * (mid - edge_value), -pltpu.roll(flux, depth - 1, 1))
        total = total + flux + upper
        here = right[x]
        direction[x] = mid
        applied[x] = total
        z_weight[x] = end_weight
        sum_right = sum_right + here
        sum_product = sum_product + here * mid
        sum_energy = sum_energy + mid * total
        sum_applied = sum_applied + total
        sum_z = sum_z + end_weight

    def whole(value):
        return jnp.sum(jnp.sum(value, axis=0, keepdims=True), axis=1, keepdims=True)

    x_high_sum, y_high_sum = whole(wx[1]), whole(wy[1])
    z_high_sum = whole(jnp.where(lane == depth - 1, sum_z, 0.0))
    faces_sum = whole(wx[0]) + x_high_sum + whole(wy[0]) + y_high_sum + whole(sum_z)
    columns = [
        whole(sum_right),
        whole(sum_product),
        whole(sum_energy),
        whole(sum_applied),
        faces_sum,
        jnp.where(inside[0][1], x_high_sum, 0.0),
        jnp.where(inside[1][1], y_high_sum, 0.0),
        jnp.where(inside[2][1], z_high_sum, 0.0),
    ]
    at = iota((1, LANES), 1)
    row = jnp.zeros((1, LANES), F32)
    for number, value in enumerate(columns):
        row = jnp.where(at == number, value, row)
    sums[...] = jnp.broadcast_to(row, sums.shape)


def finish_kernel(sizes, place, sums, inverse, direction, applied, z_weight, wx, wy, right, solution, residual, held_s, held_r, sems):
    ext_x, ext_y, depth = right.shape
    nx, ny, nz = (sizes[a] for a in MESH_AXES)
    count, blocks = nx * ny * nz, nx * ny * nz // 2
    table = sums[...]
    part = [table[:, k : k + 1] for k in range(8)]
    member = iota((count, blocks), 0) // 2 == iota((count, blocks), 1)
    means = jnp.sum(jnp.where(member, part[0], 0.0), axis=0, keepdims=True) / (2.0 * ext_x * ext_y * depth)
    coarse = jnp.sum(inverse[...] * means, axis=1, keepdims=True)
    diagonal = iota((blocks, blocks), 0) == iota((blocks, blocks), 1)
    coarse_row = jnp.sum(jnp.where(diagonal, coarse, 0.0), axis=0, keepdims=True)
    level = jnp.sum(jnp.where(member, coarse_row, 0.0), axis=1, keepdims=True)

    def shifted(by):
        return jnp.concatenate([level[by:], level[:by]], axis=0)

    def whole(value):
        return jnp.sum(value, axis=0, keepdims=True)

    product = whole(part[1] + level * part[0])
    neighbours = part[5] * shifted(ny * nz) + part[6] * shifted(nz) + part[7] * shifted(1)
    curvature = whole(part[2] + 2.0 * level * part[3] + level * (level * part[4] - 2.0 * neighbours))
    step = product / curvature
    device = iota((count, 1), 0)
    mine = (place[IX] * ny + place[IY]) * nz + place[IZ]

    def level_at(number, inside):
        return whole(jnp.where((device == number) & inside, level, 0.0))

    own = level_at(mine, True)
    drops = []
    for axis, stride, size in ((IX, ny * nz, nx), (IY, nz, ny), (IZ, 1, nz)):
        drops.append(step * (own - level_at(mine - stride, place[axis] > 0)))
        drops.append(step * (own - level_at(mine + stride, place[axis] < size - 1)))
    z_drop = jnp.where(iota((1, depth), 1) < depth // 2, drops[4], drops[5])
    chunk = 12
    for x in range(ext_x):
        held_s[x] = step * (direction[x] + own)
        value = right[x] - step * applied[x] - z_drop * z_weight[x]
        if x == 0:
            value = value - drops[0] * wx[0]
        if x == ext_x - 1:
            value = value - drops[1] * wx[1]
        held_r[x] = value
        held_r[x, 0:1] = value[0:1] - drops[2] * wy[0, x : x + 1]
        held_r[x, ext_y - 1 : ext_y] = value[ext_y - 1 : ext_y] - drops[3] * wy[1, x : x + 1]
        if (x + 1) % chunk == 0:
            part_x = pl.ds(x + 1 - chunk, chunk)
            number = (x + 1) // chunk - 1
            pltpu.make_async_copy(held_s.at[part_x], solution.at[part_x], sems.at[0, number]).start()
            pltpu.make_async_copy(held_r.at[part_x], residual.at[part_x], sems.at[1, number]).start()
    for number in range(ext_x // chunk):
        part_x = pl.ds(number * chunk, chunk)
        pltpu.make_async_copy(held_s.at[part_x], solution.at[part_x], sems.at[0, number]).wait()
        pltpu.make_async_copy(held_r.at[part_x], residual.at[part_x], sems.at[1, number]).wait()


def body(sizes, right, scale, axes, xv, yv, zv, x_values, y_values, z_values, inverse):
    ext_x, ext_y, depth = right.shape
    wide_x, wide_y, ez = xv.shape[0], yv.shape[0], zv.shape[0]
    sides = 1 if sizes["gz"] == 2 else 2
    groups = (wide_x + GROUP - 1) // GROUP
    count = sizes["gx"] * sizes["gy"] * sizes["gz"]
    place = place_vector(sizes)
    bind = functools.partial

    x_message = shape([RIM * ext_y, depth])
    low, high = call(pack_x_kernel, "pack_x", [x_message] * 2, [right, scale], [VMEM] * 2)
    x_low, x_high = swap_ends(low, high, "gx", sizes)

    square = shape([LANES, LANES], BF16)
    mats = call(
        bind(prepare_kernel, sides),
        "prepare",
        [square] * 4 + [shape([4 * depth, 2 * LANES], BF16), shape([6 * LANES, 2 * LANES], BF16), shape([wide_y, LANES])],
        [place, axes, xv, yv, zv, y_values.reshape(1, -1), z_values.reshape(1, -1)],
        [SMEM] * 2 + [VMEM] * 5,
        [pltpu.VMEM((LANES, LANES), F32), pltpu.VMEM((depth + 2 * OV, 2 * LANES), F32), pltpu.VMEM((LANES, 2 * LANES), F32)],
    )

    y_message = shape([wide_x * OV + ext_x, depth])
    low, high = call(
        lambda place, *refs: pack_y_kernel(place, sizes, *refs),
        "pack_y",
        [y_message] * 2,
        [place, right, scale, x_low, x_high],
        [SMEM] + [VMEM] * 4,
    )
    y_low, y_high = swap_ends(low, high, "gy", sizes)

    rim_message = shape([groups * wide_y, LANES])
    field = shape([wide_x * wide_y, depth])
    ext, *rims = call(
        bind(extend_kernel, sizes, sides),
        "extend",
        [field] + [rim_message] * sides,
        [place, right, scale, x_low, x_high, y_low, y_high],
        [SMEM] + [VMEM] * 6,
    )
    rims = swap_sides(rims, sizes)

    tall = pltpu.VMEM((wide_x * wide_y, LANES), F32)
    local, *own_rims = call(
        bind(solve_kernel, sides),
        "solve",
        [field] + [rim_message] * sides,
        [place, axes, x_values, ext, *rims, *mats],
        [SMEM] * 3 + [VMEM] * (1 + sides + len(mats)),
        [tall] * 4,
        limit=20,
    )
    other_rims = swap_sides(own_rims, sizes)

    x_message = shape([(RIM + sides) * wide_y, depth])
    field_z, *refs = call(
        bind(fold_z_kernel, sides, wide_x),
        "fold_z",
        [field] + [rim_message] * sides + [x_message] * 2,
        [place, local, *own_rims, *other_rims],
        [SMEM] + [VMEM] * (1 + 2 * sides),
    )
    faces, (low, high) = refs[:sides], refs[sides:]
    xs_low, xs_high = swap_ends(low, high, "gx", sizes)

    y_message = shape([(ext_x + 2 + groups * sides) * RIM, depth])
    field_x, *refs = call(
        bind(fold_x_kernel, sizes, sides, wide_x),
        "fold_x",
        [field] + [rim_message] * sides + [y_message] * 2,
        [place, field_z, *faces, xs_low, xs_high],
        [SMEM] + [VMEM] * (3 + sides),
        aliases={1: 0},
    )
    faces, (low, high) = refs[:sides], refs[sides:]
    ys_low, ys_high = swap_ends(low, high, "gy", sizes)

    block = shape(right.shape)
    padded = pltpu.VMEM((ext_x + 2, ext_y + 16, depth), F32)
    direction, applied, z_weight, wx, wy, sums = call(
        bind(operator_kernel, sizes, sides, wide_x),
        "operator",
        [block] * 3 + [shape([2, ext_y, depth]), shape([2, ext_x, depth]), shape([count, LANES])],
        [place, axes, field_x, *faces, ys_low, ys_high, right, scale, x_low, x_high, y_low, y_high, *rims],
        [SMEM] * 2 + [VMEM] * (9 + 2 * sides),
        [padded, padded, pltpu.VMEM((sides * groups * wide_y, LANES), F32)],
        limit=12,
    )
    sums = lax.all_to_all(sums, MESH_AXES, 0, 0, tiled=True)

    held = pltpu.VMEM(right.shape, F32)
    return tuple(
        call(
            bind(finish_kernel, sizes),
            "finish",
            [block] * 2,
            [place, sums, inverse, direction, applied, z_weight, wx, wy, right],
            [SMEM] + [VMEM] * 8,
            [held, held, pltpu.SemaphoreType.DMA((2, ext_x // 12))],
            out_specs=[ANY] * 2,
        )
    )


def solution(mesh):
    sizes = dict(mesh.shape)
    in_specs = (P(*MESH_AXES), P(*MESH_AXES), P(), P(), P(), P(), P(), P(), P(), P())
    out_specs = (P(*MESH_AXES), P(*MESH_AXES))
    return jax.shard_map(functools.partial(body, sizes), mesh=mesh, in_specs=in_specs, out_specs=out_specs, check_vma=False)
```

```python
import functools

import jax
import jax.numpy as jnp
from jax import lax
from jax.experimental import pallas as pl
from jax.experimental.pallas import tpu as pltpu
from jax.sharding import PartitionSpec as P

SZ = 64
OV = 4
RIM = OV + 1
LANES = 128
SLOT = 8
GROUP = LANES // SLOT
F32 = jnp.float32
BF16 = jnp.bfloat16
MESH_AXES = ("gx", "gy", "gz")

VMEM = pl.BlockSpec(memory_space=pltpu.VMEM)
ANY = pl.BlockSpec(memory_space=pl.ANY)
HBM = pl.BlockSpec(memory_space=pltpu.HBM)


def call(sizes, kernel, name, outs, args, spaces, scratch=(), limit=8, out_specs=None, aliases=None, flops=0):
    size = sum(o.size * o.dtype.itemsize for o in outs) + sum(a.size * a.dtype.itemsize for a in args)

    def placed(*refs):
        return kernel(place_values(sizes), *refs)

    return pl.pallas_call(
        placed,
        out_shape=outs,
        in_specs=spaces,
        out_specs=out_specs or [VMEM] * len(outs),
        scratch_shapes=list(scratch),
        input_output_aliases=aliases or {},
        name=name,
        compiler_params=pltpu.CompilerParams(vmem_limit_bytes=limit * 2**20),
        cost_estimate=pl.CostEstimate(flops=flops, bytes_accessed=size, transcendentals=0),
    )(*args)


def shape(dims, dtype=F32):
    return jax.ShapeDtypeStruct(tuple(dims), dtype)


def halves(value):
    high = value.astype(BF16)
    return high, (value - high.astype(F32)).astype(BF16)


def dot(left, right):
    return jnp.dot(left, right, preferred_element_type=F32)


def iota(dims, axis):
    return lax.broadcasted_iota(jnp.int32, dims, axis)


IX, IY, IZ, SIDE = 0, 1, 2, 3


def place_values(sizes):
    ix, iy, iz = (lax.axis_index(a) for a in MESH_AXES)
    nz = sizes["gz"]
    if nz == 2:
        sides = [1 - iz, 1]
    else:
        sides = [1, jnp.where(iz < nz - 1, 1, 0), 0, jnp.where(iz > 0, 1, 0)]
    return [ix, iy, iz] + sides


def swap_sides(messages, sizes):
    count = sizes["gz"]
    if count == 2:
        return [lax.ppermute(messages[0], "gz", [(0, 1), (1, 0)])]
    up = [(i, (i + 1) % count) for i in range(count)]
    down = [((i + 1) % count, i) for i in range(count)]
    return [lax.ppermute(messages[1], "gz", down), lax.ppermute(messages[0], "gz", up)]


def swap_ends(first, second, axis, sizes):
    count = sizes[axis]
    received = []
    for message, start in ((first, 0), (second, 1)):
        partner = list(range(count))
        for i in range(start, count - 1, 2):
            partner[i], partner[i + 1] = i + 1, i
        received.append(lax.ppermute(message, axis, list(enumerate(partner))))
    return received


def is_even(place, axis):
    return lax.rem(place[axis], 2) == 0


def from_ends(place, axis, sizes, first, second):
    even = is_even(place, axis)
    inside_low = place[axis] > 0
    inside_high = place[axis] < sizes[MESH_AXES[axis]] - 1

    def low(at):
        return jnp.where(inside_low, jnp.where(even, second[at], first[at]), 0.0)

    def high(at):
        return jnp.where(inside_high, jnp.where(even, first[at], second[at]), 0.0)

    return low, high


def prepare_kernel(sides, place, axes, xv, yv, zv, y_row, z_row, fx, bx, fy, by, wz, bz, den, pad, wide, rows):
    ez = zv.shape[0]
    depth = wz.shape[0] // 4

    def stacked(value, out):
        high, low = halves(value[: LANES // 2])
        high = high.astype(F32)
        twice = jnp.where(iota(high.shape, 1) < LANES // 2, high, pltpu.roll(high, LANES // 2, 1))
        out[:, 0:LANES] = twice.astype(BF16)
        out[:, LANES:] = low[:, 0 : LANES // 2]

    for vectors, forward, back in ((xv, fx, bx), (yv, fy, by)):
        pad[...] = jnp.zeros_like(pad)
        pad[0 : vectors.shape[0], 0 : vectors.shape[1]] = vectors[...]
        stacked(pad[...], back)
        stacked(pad[...].T, forward)

    wide[...] = jnp.zeros_like(wide)
    wide[0:ez, 0:ez] = zv[...]
    wide[SZ : SZ + ez, LANES : LANES + ez] = zv[...]
    middle = wide[OV : OV + depth]
    high, low = halves(middle)
    wz[0:depth] = high
    wz[depth : 2 * depth] = high
    wz[2 * depth : 3 * depth] = low
    rows[...] = jnp.zeros_like(rows)
    for side in range(sides):
        is_high = place[SIDE + 2 * side] > 0
        for k in range(OV):
            top, bottom = OV + depth + k, k
            row = jnp.where(is_high, wide[top : top + 1], wide[bottom : bottom + 1])
            row_high, row_low = halves(row)
            at = 3 * SLOT * side + k
            rows[at : at + 1] = row_high.astype(F32)
            rows[at + SLOT : at + SLOT + 1] = row_high.astype(F32)
            rows[at + 2 * SLOT : at + 2 * SLOT + 1] = row_low.astype(F32)
    wz[3 * depth :] = rows[...].astype(BF16)

    rows[...] = jnp.zeros_like(rows)
    for side in range(sides):
        is_high = place[SIDE + 2 * side] > 0
        for k in range(RIM):
            top, bottom = OV + depth - 1 + k, k
            rows[SLOT * side + k : SLOT * side + k + 1] = jnp.where(is_high, wide[top : top + 1], wide[bottom : bottom + 1])
    across = 2 * LANES
    for at, part in ((0, middle), (LANES, rows[...])):
        turned = jnp.concatenate([part[:, 0:LANES].T, part[:, LANES:].T], axis=0)
        high, low = halves(turned)
        bz[0:across, at : at + LANES] = high
        bz[across : 2 * across, at : at + LANES] = high
        bz[2 * across :, at : at + LANES] = low

    ey = yv.shape[0]
    diagonal = iota((ey, ey), 0) == iota((ey, ey), 1)
    y_column = jnp.sum(jnp.where(diagonal, y_row[...], 0.0), axis=1, keepdims=True)
    pad[...] = jnp.ones_like(pad)
    pad[0:1, 0:ez] = axes[:, 2:3] * z_row[...]
    den[...] = axes[:, 1:2] * y_column + pad[0:1]


def pack_x_kernel(place, right, scale, first, second, faces, sems):
    ext_x = right.shape[0]
    even = is_even(place, IX)
    copies = []
    for number, (out, high) in enumerate(((first, even), (second, jnp.logical_not(even)))):
        start = jnp.where(high, ext_x - OV, 0)
        face = jnp.where(high, ext_x - 1, 0)
        copies.append(pltpu.make_async_copy(right.at[pl.ds(start, OV)], out.at[pl.ds(0, OV)], sems.at[0, number]))
        copies.append(pltpu.make_async_copy(scale.at[face], faces.at[number], sems.at[1, number]))
    for copy in copies:
        copy.start()
    for copy in copies:
        copy.wait()
    for number, out in enumerate((first, second)):
        out[OV] = faces[number].astype(F32)


def pack_y_own_kernel(place, right, scale, first, second):
    ext_x, ext_y, depth = right.shape
    even = is_even(place, IY)
    base = (ext_x + 2 * OV) * OV
    for x in range(ext_x):
        low, high = right[x, 0:OV], right[x, ext_y - OV : ext_y]
        at = (x + OV) * OV
        first[at : at + OV] = jnp.where(even, high, low)
        second[at : at + OV] = jnp.where(even, low, high)
        low, high = scale[x, 0:16].astype(F32)[0:1], scale[x, ext_y - 16 : ext_y].astype(F32)[15:16]
        first[base + x : base + x + 1] = jnp.where(even, high, low)
        second[base + x : base + x + 1] = jnp.where(even, low, high)


def pack_y_rest_kernel(sizes, place, x_first, x_second, own_first, own_second, first, second):
    ext_y = x_first.shape[1]
    even = is_even(place, IY)
    x_low, x_high = from_ends(place, IX, sizes, x_first, x_second)
    last = (own_first.shape[0] - 2 * OV * OV) // (OV + 1) * OV
    for t in range(OV):
        for source, at in ((x_low, t * OV), (x_high, last + OV * OV + t * OV)):
            low, high = source((t, slice(0, OV))), source((t, slice(ext_y - OV, ext_y)))
            first[at : at + OV] = jnp.where(even, high, low)
            second[at : at + OV] = jnp.where(even, low, high)


def pack_rims(place, side, depth, wide_x, wide_y, ext, message, starts):
    lane = iota((8, LANES), 1)
    start = jnp.where(place[SIDE + 2 * side] > 0, depth - OV, 0)
    for row in starts:
        for group in range((wide_x + GROUP - 1) // GROUP):
            total = jnp.zeros((8, LANES), F32)
            for q in range(min(GROUP, wide_x - group * GROUP)):
                at = (group * GROUP + q) * wide_y + row
                moved = pltpu.roll(ext[at : at + 8], lax.rem(SLOT * q + depth - start, depth), 1)
                total = jnp.where((lane >= SLOT * q) & (lane < SLOT * q + OV), moved, total)
            message[group * wide_y + row : group * wide_y + row + 8] += total


def extend_own_kernel(sizes, sides, place, right, scale, x_first, x_second, ext, *messages):
    ext_x, ext_y, depth = right.shape
    wide_x, wide_y = ext_x + 2 * OV, ext_y + 2 * OV
    x_low, x_high = from_ends(place, IX, sizes, x_first, x_second)
    for a in range(wide_x):
        if a < OV:
            core = x_low(a)
        elif a < ext_x + OV:
            core = right[a - OV]
        else:
            core = x_high(a - OV - ext_x)
        ext[a * wide_y + OV : a * wide_y + OV + ext_y] = core
    lane = iota((ext_y, LANES), 1)
    for side in range(sides):
        face = jnp.where(place[SIDE + 2 * side] > 0, depth - 1, 0)
        messages[side][...] = jnp.zeros_like(messages[side])
        for group in range((ext_x + GROUP - 1) // GROUP):
            total = jnp.zeros((ext_y, LANES), F32)
            for q in range(min(GROUP, ext_x - group * GROUP)):
                at = SLOT * q + OV
                moved = pltpu.roll(scale[group * GROUP + q].astype(F32), lax.rem(at + depth - face, depth), 1)
                total = jnp.where(lane == at, moved, total)
            messages[side][group * wide_y : group * wide_y + ext_y] = total
        pack_rims(place, side, depth, wide_x, wide_y, ext, messages[side], range(8, wide_y - 8, 8))


def extend_rest_kernel(sizes, sides, wide_x, place, y_first, y_second, own_ext, *refs):
    refs = refs[sides:]
    ext, messages = refs[0], refs[1:]
    rows, depth = ext.shape
    wide_y = rows // wide_x
    y_low, y_high = from_ends(place, IY, sizes, y_first, y_second)
    for a in range(wide_x):
        part = slice(a * OV, (a + 1) * OV)
        ext[a * wide_y : a * wide_y + OV] = y_low(part)
        ext[(a + 1) * wide_y - OV : (a + 1) * wide_y] = y_high(part)
    for side in range(sides):
        pack_rims(place, side, depth, wide_x, wide_y, ext, messages[side], (0, wide_y - 8))


def solve_kernel(sides, place, axes, x_values, ext, *refs):
    received, refs = refs[:sides], refs[sides:]
    fx, bx, fy, by, wz, bz, den, local = refs[:8]
    messages, refs = refs[8 : 8 + sides], refs[8 + sides :]
    first_a, first_b, second_a, second_b = refs
    wide = x_values.shape[1]
    rows = ext.shape[0]
    wide_y = rows // wide
    batch = 8
    lane = iota((wide_y, LANES), 1)

    def along(matrix, pair):
        value = jnp.concatenate(pair, axis=1)
        fill = jnp.zeros((LANES // 2 - value.shape[0], value.shape[1]), F32)
        high, low = halves(jnp.concatenate([value, fill], axis=0))
        return dot(matrix[...], jnp.concatenate([high, low, high], axis=0))[0 : value.shape[0]]

    for start in range(0, wide, batch):
        block = pl.ds(start * wide_y, batch * wide_y)
        high, low = halves(ext[block])
        rims = []
        for a in range(start, start + batch):
            group, q = a // GROUP, a % GROUP
            piece = jnp.zeros((wide_y, LANES), F32)
            for side in range(sides):
                value = received[side][group * wide_y : (group + 1) * wide_y]
                value = jnp.where((lane // SLOT == q) & (place[SIDE + 2 * side + 1] > 0), value, 0.0)
                value_high, value_low = halves(value)
                value_high, value_low = value_high.astype(F32), value_low.astype(F32)
                at = LANES - SLOT * q + 3 * SLOT * side
                piece = piece + pltpu.roll(value_high, at % LANES, 1)
                piece = piece + pltpu.roll(value_low, (at + SLOT) % LANES, 1)
                piece = piece + pltpu.roll(value_high, (at + 2 * SLOT) % LANES, 1)
            rims.append(piece.astype(BF16))
        left = jnp.concatenate([high, low, high, jnp.concatenate(rims, axis=0)], axis=1)
        out = dot(left, wz[...])
        first_a[block] = out[:, 0:LANES]
        first_b[block] = out[:, LANES:]

    def strided(refs_pair, at, count, stride):
        return [ref[pl.ds(at, count, stride=stride), :] for ref in refs_pair]

    def x_forward(y):
        out = along(fx, strided((first_a, first_b), y, wide, wide_y))
        second_a[pl.ds(y * wide, wide)] = out[:, 0:LANES]
        second_b[pl.ds(y * wide, wide)] = out[:, LANES:]

    def y_both(i):
        out = along(fy, strided((second_a, second_b), i, wide_y, wide))
        inverse = 1.0 / (axes[:, 0:1] * x_values[:, i : i + 1] + den[...])
        out = along(by, [out[:, 0:LANES] * inverse, out[:, LANES:] * inverse])
        first_a[pl.ds(i * wide_y, wide_y)] = out[:, 0:LANES]
        first_b[pl.ds(i * wide_y, wide_y)] = out[:, LANES:]

    def x_back(y):
        out = along(bx, strided((first_a, first_b), y, wide, wide_y))
        second_a[pl.ds(y, wide, stride=wide_y), :] = out[:, 0:LANES]
        second_b[pl.ds(y, wide, stride=wide_y), :] = out[:, LANES:]

    for step, count in ((x_forward, wide_y), (y_both, wide), (x_back, wide_y)):
        for number in range(count):
            step(number)

    totals = [[jnp.zeros((wide_y, LANES), F32) for _ in range((wide + GROUP - 1) // GROUP)] for _ in range(sides)]
    for start in range(0, wide, batch):
        block = pl.ds(start * wide_y, batch * wide_y)
        high_a, low_a = halves(second_a[block])
        high_b, low_b = halves(second_b[block])
        out = dot(jnp.concatenate([high_a, high_b, low_a, low_b, high_a, high_b], axis=1), bz[...])
        local[block] = out[:, 0:LANES]
        for a in range(start, start + batch):
            group, q = a // GROUP, a % GROUP
            value = out[(a - start) * wide_y : (a - start + 1) * wide_y, LANES:]
            for side in range(sides):
                own = value if sides == 1 else jnp.where(lane // SLOT == side, value, 0.0)
                at = (SLOT * q + LANES - SLOT * side) % LANES
                totals[side][group] = totals[side][group] + (pltpu.roll(own, at, 1) if at else own)
    for side in range(sides):
        for group, total in enumerate(totals[side]):
            messages[side][group * wide_y : (group + 1) * wide_y] = total


def with_z_rims(place, sides, wide_y, local, received, a):
    lane = iota((wide_y, LANES), 1)
    group, q = a // GROUP, a % GROUP
    value = local[a * wide_y : (a + 1) * wide_y]
    for side in range(sides):
        is_high, valid = place[SIDE + 2 * side] > 0, place[SIDE + 2 * side + 1] > 0
        start = jnp.where(is_high, LANES - OV, 0)
        shift = lax.rem(jnp.where(is_high, LANES - OV, LANES - 1) + LANES - SLOT * q, LANES)
        moved = pltpu.roll(received[side][group * wide_y : (group + 1) * wide_y], shift, 1)
        value = value + jnp.where((lane >= start) & (lane < start + OV) & valid, moved, 0.0)
    return value


def pack_back_x_kernel(sides, wide, place, local, *refs):
    own, received = refs[:sides], refs[sides : 2 * sides]
    refs = refs[2 * sides :]
    faces, (first, second) = refs[:sides], refs[sides:]
    wide_y = local.shape[0] // wide
    groups = (wide + GROUP - 1) // GROUP
    even = is_even(place, IX)
    wide_lane = iota((groups * wide_y, LANES), 1)
    for side in range(sides):
        is_high, valid = place[SIDE + 2 * side] > 0, place[SIDE + 2 * side + 1] > 0
        other = pltpu.roll(received[side][...], jnp.where(is_high, LANES - OV, 0), 1)
        mine = pltpu.roll(own[side][...], jnp.where(is_high, LANES - 1, LANES - OV + 1), 1)
        faces[side][...] = jnp.where((lax.rem(wide_lane, SLOT) == 0) & valid, other + mine, 0.0)
        low, high = faces[side][0:wide_y], faces[side][(groups - 1) * wide_y :]
        at = (RIM + side) * wide_y
        first[at : at + wide_y] = jnp.where(even, high, low)
        second[at : at + wide_y] = jnp.where(even, low, high)
    for t in range(RIM):
        low = with_z_rims(place, sides, wide_y, local, received, t)
        high = with_z_rims(place, sides, wide_y, local, received, wide - RIM + t)
        first[t * wide_y : (t + 1) * wide_y] = jnp.where(even, high, low)
        second[t * wide_y : (t + 1) * wide_y] = jnp.where(even, low, high)


def fold_z_kernel(sides, wide, place, local, *refs):
    faces, received = refs[:sides], refs[sides : 2 * sides]
    out, first, second = refs[2 * sides :]
    wide_y = local.shape[0] // wide
    groups = (wide + GROUP - 1) // GROUP
    planes = wide - 2 * OV + 2
    even = is_even(place, IY)
    for a in range(wide):
        value = with_z_rims(place, sides, wide_y, local, received, a)
        out[a * wide_y : (a + 1) * wide_y] = value
        p = a - OV + 1
        if 0 <= p < planes:
            low, high = value[0:RIM], value[wide_y - RIM :]
            first[p * RIM : (p + 1) * RIM] = jnp.where(even, high, low)
            second[p * RIM : (p + 1) * RIM] = jnp.where(even, low, high)
    for side in range(sides):
        for group in range(groups):
            at = planes * RIM + (side * groups + group) * RIM
            low = faces[side][group * wide_y : group * wide_y + RIM]
            high = faces[side][(group + 1) * wide_y - RIM : (group + 1) * wide_y]
            first[at : at + RIM] = jnp.where(even, high, low)
            second[at : at + RIM] = jnp.where(even, low, high)


def x_received(sizes, wide, wide_y, place, x_first, x_second):
    low, high = from_ends(place, IX, sizes, x_first, x_second)
    high_lane = (wide - 2 * OV) % GROUP * SLOT

    def plane(a, rows):
        if OV - 1 <= a < OV - 1 + RIM:
            at, source = (a - OV + 1) * wide_y, low
        elif wide - 2 * OV <= a < wide - 2 * OV + RIM:
            at, source = (a - wide + 2 * OV) * wide_y, high
        else:
            return None
        return source(slice(at + rows.start, at + rows.stop))

    def faces(side, group, rows):
        lane = iota((rows.stop - rows.start, LANES), 1)
        at = (RIM + side) * wide_y
        rows = slice(at + rows.start, at + rows.stop)
        if group == 0:
            return jnp.where((lane >= (OV - 1) * SLOT) & (lane < 2 * OV * SLOT), low(rows), 0.0)
        if group == (wide + GROUP - 1) // GROUP - 1:
            return jnp.where((lane >= high_lane) & (lane < high_lane + RIM * SLOT), high(rows), 0.0)
        return None

    return plane, faces


def pack_back_y_kernel(sizes, sides, wide, wide_y, place, x_first, x_second, own_first, own_second, first, second):
    groups = (wide + GROUP - 1) // GROUP
    planes = wide - 2 * OV + 2
    even = is_even(place, IY)
    plane, faces = x_received(sizes, wide, wide_y, place, x_first, x_second)
    low_rows, high_rows = slice(0, RIM), slice(wide_y - RIM, wide_y)

    def add(at, low, high):
        first[at : at + RIM] += jnp.where(even, high, low)
        second[at : at + RIM] += jnp.where(even, low, high)

    for p in range(planes):
        low = plane(p + OV - 1, low_rows)
        if low is not None:
            add(p * RIM, low, plane(p + OV - 1, high_rows))
    for side in range(sides):
        for group in range(groups):
            low = faces(side, group, low_rows)
            if low is not None:
                add(planes * RIM + (side * groups + group) * RIM, low, faces(side, group, high_rows))


def weights_kernel(sizes, sides, place, axes, right, scale, x_first, x_second, y_first, y_second, *refs):
    scale_faces = refs[:sides]
    wx, wy, wz, z_weight, sums, scales = refs[sides:]
    ext_x, ext_y, depth = right.shape
    wide_y = ext_y + 2 * OV
    core = slice(8, 8 + ext_y)
    x_low, x_high = from_ends(place, IX, sizes, x_first, x_second)
    y_low, y_high = from_ends(place, IY, sizes, y_first, y_second)
    y_rows = (ext_x + 2 * OV) * OV
    scales[0, core] = x_low(OV)
    scales[ext_x + 1, core] = x_high(OV)
    for x in range(ext_x):
        scales[x + 1, core] = scale[x].astype(F32)
        part = slice(y_rows + x, y_rows + x + 1)
        scales[x + 1, 7:8] = y_low(part)
        scales[x + 1, 8 + ext_y : 9 + ext_y] = y_high(part)
    hx, hy, hz = (0.5 * axes[:, d : d + 1] for d in range(3))
    lane = iota((8, depth), 1)
    ends = (lane == 0) | (lane == depth - 1)
    zero = jnp.zeros((8, depth), F32)
    sum_right, sum_z = zero, zero
    for x in range(ext_x + 1):
        wx[x] = hx * (scales[x, core] + scales[x + 1, core])
    for x in range(ext_x):
        wy[x, 0 : ext_y + 1] = hy * (scales[x + 1, 7 : 8 + ext_y] + scales[x + 1, 8 : 9 + ext_y])
        for row in range(0, ext_y, 8):
            own = scales[x + 1, 8 + row : 16 + row]
            edge = zero
            for side in range(sides):
                is_high, valid = place[SIDE + 2 * side] > 0, place[SIDE + 2 * side + 1] > 0
                target = jnp.where(is_high, depth - 1, 0)
                at = x // GROUP * wide_y + row
                shift = lax.rem(target + depth - (x % GROUP * SLOT + OV), depth)
                edge = jnp.where((lane == target) & valid, pltpu.roll(scale_faces[side][at : at + 8], shift, 1), edge)
            wz[x, row : row + 8] = hz * (own + jnp.where(lane == 0, edge, pltpu.roll(own, 1, 1)))
            end_weight = jnp.where(ends, hz * (own + edge), 0.0)
            z_weight[x, row : row + 8] = end_weight
            sum_z = sum_z + end_weight
            sum_right = sum_right + right[x, row : row + 8]

    def whole(value):
        return jnp.sum(jnp.sum(value, axis=0, keepdims=True), axis=1, keepdims=True)

    def y_sum(row):
        total = jnp.zeros((1, depth), F32)
        for x in range(ext_x):
            total = total + wy[x, row : row + 1]
        return whole(total)

    x_high_sum, y_high_sum = whole(wx[ext_x]), y_sum(ext_y)
    z_high_sum = whole(jnp.where(lane == depth - 1, sum_z, 0.0))
    faces_sum = whole(wx[0]) + x_high_sum + y_sum(0) + y_high_sum + whole(sum_z)
    columns = {
        0: whole(sum_right),
        4: faces_sum,
        5: jnp.where(place[IX] < sizes["gx"] - 1, x_high_sum, 0.0),
        6: jnp.where(place[IY] < sizes["gy"] - 1, y_high_sum, 0.0),
        7: jnp.where(place[IZ] < sizes["gz"] - 1, z_high_sum, 0.0),
    }
    sums[...] = in_columns(columns, jnp.zeros((1, LANES), F32))


def in_columns(columns, row):
    at = iota((1, LANES), 1)
    for number, value in columns.items():
        row = jnp.where(at == number, value, row)
    return row


def operator_tile(place, sides, groups, values, edges, wx, wy, wz, z_weight, block, inner, row):
    depth = values.shape[2]
    ext_y = z_weight.shape[1]
    lane = iota((8, depth), 1)
    at = slice(8 + row, 16 + row)
    x = block * GROUP + inner
    mid = values[x + 1, at]
    total = wx[x, row : row + 8] * (mid - values[x, at]) + wx[x + 1, row : row + 8] * (mid - values[x + 2, at])
    total = total + wy[x, row : row + 8] * (mid - values[x + 1, 7 + row : 15 + row])
    total = total + wy[x, row + 1 : row + 9] * (mid - values[x + 1, 9 + row : 17 + row])
    edge = jnp.zeros((8, depth), F32)
    for side in range(sides):
        is_high, valid = place[SIDE + 2 * side] > 0, place[SIDE + 2 * side + 1] > 0
        target = jnp.where(is_high, depth - 1, 0)
        start = (side * groups + block + (inner + OV) // GROUP) * ext_y + row
        moved = edges[pl.ds(pl.multiple_of(start, 8), 8)]
        q = (inner + OV) % GROUP
        if q:
            moved = pltpu.roll(moved, depth - q * SLOT, 1)
        edge = jnp.where((lane == target) & valid, moved, edge)
    flux = wz[x, row : row + 8] * (mid - jnp.where(lane == 0, edge, pltpu.roll(mid, 1, 1)))
    above = z_weight[x, row : row + 8] * (mid - edge)
    total = total + flux + jnp.where(lane == depth - 1, above, -pltpu.roll(flux, depth - 1, 1))
    return mid, total


def operator_tiles(place, sides, groups, right, values, edges, weights, applied, sums, rows):
    def several(block, totals):
        product, energy, whole = totals
        for inner in range(GROUP):
            x = block * GROUP + inner
            for row in rows:
                mid, total = operator_tile(place, sides, groups, values, edges, *weights, block, inner, row)
                applied[x, row : row + 8] = total
                product = product + right[x, row : row + 8] * mid
                energy = energy + mid * total
                whole = whole + total
        return product, energy, whole

    totals = lax.fori_loop(0, right.shape[0] // GROUP, several, (jnp.zeros((8, values.shape[2]), F32),) * 3)
    for number, value in enumerate(totals):
        sums[number * 8 : (number + 1) * 8] = value


def to_face(place, side, value):
    return pltpu.roll(value, jnp.where(place[SIDE + 2 * side] > 0, LANES - 1, 0), 1)


def inner_kernel(sizes, sides, wide, place, right, field, x_first, x_second, *refs):
    faces, weights, refs = refs[:sides], refs[sides : sides + 4], refs[sides + 4 :]
    values, edges, applied, sums = refs
    ext_x, ext_y, depth = right.shape
    wide_y = ext_y + 2 * OV
    groups = (wide + GROUP - 1) // GROUP
    plane, face = x_received(sizes, wide, wide_y, place, x_first, x_second)
    inside_low, inside_high = place[IX] > 0, place[IX] < sizes["gx"] - 1
    rows = slice(OV - 1, wide_y - OV + 1)
    for p in range(ext_x + 2):
        a = p + OV - 1
        value = field[a * wide_y + rows.start : a * wide_y + rows.stop]
        more = plane(a, rows)
        if more is not None:
            value = value + more
        if p == 0:
            value = jnp.where(inside_low, value, 0.0)
        if p == ext_x + 1:
            value = jnp.where(inside_high, value, 0.0)
        values[p, 7 : 9 + ext_y] = value
    for side in range(sides):
        for group in range(groups):
            value = faces[side][group * wide_y : (group + 1) * wide_y]
            more = face(side, group, slice(0, wide_y))
            value = value if more is None else value + more
            at = (side * groups + group) * ext_y
            edges[at : at + ext_y] = to_face(place, side, value)[OV : OV + ext_y]
    operator_tiles(place, sides, groups, right, values, edges, weights, applied, sums, range(8, ext_y - 8, 8))


def outer_kernel(sizes, sides, wide, place, right, y_first, y_second, *refs):
    weights, fixed, refs = refs[:4], refs[4], refs[5:]
    inner_sums, refs = refs[3], refs[4:]
    values, edges, applied, out, sums = refs
    ext_x, ext_y, depth = right.shape
    wide_y = ext_y + 2 * OV
    groups = (wide + GROUP - 1) // GROUP
    low, high = from_ends(place, IY, sizes, y_first, y_second)
    inside_low, inside_high = place[IY] > 0, place[IY] < sizes["gy"] - 1
    for p in range(ext_x + 2):
        part = slice(p * RIM, (p + 1) * RIM)
        low_rows, high_rows = low(part), high(part)
        if p == 0 or p == ext_x + 1:
            inside = place[IX] > 0 if p == 0 else place[IX] < sizes["gx"] - 1
            low_rows, high_rows = (jnp.where(inside, rows, 0.0) for rows in (low_rows, high_rows))
        values[p, 7 : 7 + RIM] += low_rows
        values[p, 4 + ext_y : 4 + ext_y + RIM] += high_rows
        values[p, 7:8] = jnp.where(inside_low, values[p, 7:8], 0.0)
        values[p, 8 + ext_y : 9 + ext_y] = jnp.where(inside_high, values[p, 8 + ext_y : 9 + ext_y], 0.0)
    for number in range(sides * groups):
        at = (ext_x + 2 + number) * RIM
        start = number * ext_y
        side = number // groups
        edges[start : start + OV] += to_face(place, side, low(slice(at, at + RIM)))[1:]
        edges[start + ext_y - OV : start + ext_y] += to_face(place, side, high(slice(at, at + RIM)))[:OV]
    operator_tiles(place, sides, groups, right, values, edges, weights, applied, sums, (0, ext_y - 8))
    columns = {}
    for number in range(3):
        part = slice(number * 8, (number + 1) * 8)
        value = inner_sums[part] + sums[part]
        columns[number + 1] = jnp.sum(jnp.sum(value, axis=0, keepdims=True), axis=1, keepdims=True)
    out[...] = jnp.broadcast_to(in_columns(columns, fixed[...]), out.shape)


def finish_kernel(sizes, place, sums, inverse, values, applied, wx, wy, z_weight, right, solution, residual, held_s, held_r, sems):
    ext_x, ext_y, depth = right.shape
    nx, ny, nz = (sizes[a] for a in MESH_AXES)
    count, blocks = nx * ny * nz, nx * ny * nz // 2
    table = sums[...]
    part = [table[:, k : k + 1] for k in range(8)]
    member = iota((count, blocks), 0) // 2 == iota((count, blocks), 1)
    means = jnp.sum(jnp.where(member, part[0], 0.0), axis=0, keepdims=True) / (2.0 * ext_x * ext_y * depth)
    coarse = jnp.sum(inverse[...] * means, axis=1, keepdims=True)
    diagonal = iota((blocks, blocks), 0) == iota((blocks, blocks), 1)
    coarse_row = jnp.sum(jnp.where(diagonal, coarse, 0.0), axis=0, keepdims=True)
    level = jnp.sum(jnp.where(member, coarse_row, 0.0), axis=1, keepdims=True)

    def shifted(by):
        return jnp.concatenate([level[by:], level[:by]], axis=0)

    def whole(value):
        return jnp.sum(value, axis=0, keepdims=True)

    product = whole(part[1] + level * part[0])
    neighbours = part[5] * shifted(ny * nz) + part[6] * shifted(nz) + part[7] * shifted(1)
    curvature = whole(part[2] + 2.0 * level * part[3] + level * (level * part[4] - 2.0 * neighbours))
    step = product / curvature
    device = iota((count, 1), 0)
    mine = (place[IX] * ny + place[IY]) * nz + place[IZ]

    def level_at(number, inside):
        return whole(jnp.where((device == number) & inside, level, 0.0))

    own = level_at(mine, True)
    drops = []
    for axis, stride, size in ((IX, ny * nz, nx), (IY, nz, ny), (IZ, 1, nz)):
        drops.append(step * (own - level_at(mine - stride, place[axis] > 0)))
        drops.append(step * (own - level_at(mine + stride, place[axis] < size - 1)))
    z_drop = jnp.where(iota((1, depth), 1) < depth // 2, drops[4], drops[5])
    chunk = 12
    for x in range(ext_x):
        held_s[x] = step * (values[x + 1, 8 : 8 + ext_y] + own)
        value = right[x] - step * applied[x] - z_drop * z_weight[x]
        if x == 0:
            value = value - drops[0] * wx[0]
        if x == ext_x - 1:
            value = value - drops[1] * wx[ext_x]
        held_r[x] = value
        held_r[x, 0:1] = value[0:1] - drops[2] * wy[x, 0:1]
        held_r[x, ext_y - 1 : ext_y] = value[ext_y - 1 : ext_y] - drops[3] * wy[x, ext_y : ext_y + 1]
        if (x + 1) % chunk == 0:
            part_x = pl.ds(x + 1 - chunk, chunk)
            number = (x + 1) // chunk - 1
            pltpu.make_async_copy(held_s.at[part_x], solution.at[part_x], sems.at[0, number]).start()
            pltpu.make_async_copy(held_r.at[part_x], residual.at[part_x], sems.at[1, number]).start()
    for number in range(ext_x // chunk):
        part_x = pl.ds(number * chunk, chunk)
        pltpu.make_async_copy(held_s.at[part_x], solution.at[part_x], sems.at[0, number]).wait()
        pltpu.make_async_copy(held_r.at[part_x], residual.at[part_x], sems.at[1, number]).wait()


def body(sizes, right, scale, axes, xv, yv, zv, x_values, y_values, z_values, inverse):
    ext_x, ext_y, depth = right.shape
    wide_x, wide_y = xv.shape[0], yv.shape[0]
    sides = 1 if sizes["gz"] == 2 else 2
    groups = (wide_x + GROUP - 1) // GROUP
    count = sizes["gx"] * sizes["gy"] * sizes["gz"]
    bind = functools.partial
    run = bind(call, sizes)
    block = shape(right.shape)
    axes_row = axes.reshape(1, -1)
    beside = 2 * 10**9

    xs = run(
        pack_x_kernel,
        "pack_x",
        [shape([RIM, ext_y, depth])] * 2,
        [right, scale],
        [HBM] * 2,
        [pltpu.VMEM((2, ext_y, depth), BF16), pltpu.SemaphoreType.DMA((2, 2))],
        limit=60,
    )
    xs = swap_ends(*xs, "gx", sizes)

    thin = shape([LANES // 2, 3 * LANES // 2], BF16)
    mats = run(
        bind(prepare_kernel, sides),
        "prepare",
        [thin] * 4 + [shape([4 * depth, 2 * LANES], BF16), shape([6 * LANES, 2 * LANES], BF16), shape([wide_y, LANES])],
        [axes_row, xv, yv, zv, y_values.reshape(1, -1), z_values.reshape(1, -1)],
        [VMEM] * 6,
        [pltpu.VMEM((LANES, LANES), F32), pltpu.VMEM((depth + 2 * OV, 2 * LANES), F32), pltpu.VMEM((LANES, 2 * LANES), F32)],
        flops=beside,
    )
    y_message = [shape([wide_x * OV + ext_x, depth])] * 2
    ys = run(pack_y_own_kernel, "pack_y_own", y_message, [right, scale], [VMEM] * 2, flops=beside)
    ys, mats = lax.optimization_barrier((ys, mats))
    ys = run(
        bind(pack_y_rest_kernel, sizes),
        "pack_y_rest",
        y_message,
        [*xs, *ys],
        [VMEM] * 4,
        aliases={2: 0, 3: 1},
    )
    ys = swap_ends(*ys, "gy", sizes)

    rim_message = shape([groups * wide_y, LANES])
    field = shape([wide_x * wide_y, depth])
    ext, *rims = run(
        bind(extend_own_kernel, sizes, sides),
        "extend_own",
        [field] + [rim_message] * sides,
        [right, scale, *xs],
        [VMEM] * 4,
        flops=beside,
    )
    ext, *rims = run(
        bind(extend_rest_kernel, sizes, sides, wide_x),
        "extend_rest",
        [field] + [rim_message] * sides,
        [*ys, ext, *rims],
        [VMEM] * (3 + sides),
        aliases={2 + k: k for k in range(1 + sides)},
    )
    rims = swap_sides(rims, sizes)

    tall = pltpu.VMEM((wide_x * wide_y, LANES), F32)
    local, *own_rims = run(
        bind(solve_kernel, sides),
        "solve",
        [field] + [rim_message] * sides,
        [axes_row, x_values.reshape(1, -1), ext, *rims, *mats],
        [VMEM] * (3 + sides + len(mats)),
        [tall] * 4,
        limit=20,
    )
    other_rims = swap_sides(own_rims, sizes)

    *faces, low, high = run(
        bind(pack_back_x_kernel, sides, wide_x),
        "pack_back_x",
        [rim_message] * sides + [shape([(RIM + sides) * wide_y, depth])] * 2,
        [local, *own_rims, *other_rims],
        [VMEM] * (1 + 2 * sides),
    )
    back_xs = swap_ends(low, high, "gx", sizes)

    y_message = [shape([(ext_x + 2 + groups * sides) * RIM, depth])] * 2
    field_z, *back_ys = run(
        bind(fold_z_kernel, sides, wide_x),
        "fold_z",
        [field] + y_message,
        [local, *faces, *other_rims],
        [VMEM] * (1 + 2 * sides),
        flops=beside,
    )
    low, late_rims = lax.optimization_barrier((low, rims))
    scale_block = pltpu.VMEM((ext_x + 2, ext_y + 16, depth), F32)
    *weights, fixed = run(
        bind(weights_kernel, sizes, sides),
        "weights",
        [shape([ext_x + 1, ext_y, depth]), shape([ext_x, ext_y + 8, depth]), block, block, shape([1, LANES])],
        [axes_row, right, scale, *xs, *ys, *late_rims],
        [VMEM] * (7 + sides),
        [scale_block],
        flops=beside,
    )
    back_ys = run(
        bind(pack_back_y_kernel, sizes, sides, wide_x, wide_y),
        "pack_back_y",
        y_message,
        [*back_xs, *back_ys],
        [VMEM] * 4,
        aliases={2: 0, 3: 1},
    )
    back_ys = swap_ends(*back_ys, "gy", sizes)

    parts = [shape([ext_x + 2, ext_y + 16, depth]), shape([sides * groups * ext_y, LANES]), block]
    inner = run(
        bind(inner_kernel, sizes, sides, wide_x),
        "inner",
        parts + [shape([24, depth])],
        [right, field_z, *back_xs, *faces, *weights],
        [VMEM] * (8 + sides),
        flops=beside,
    )
    values, edges, applied, sums = run(
        bind(outer_kernel, sizes, sides, wide_x),
        "outer",
        parts + [shape([count, LANES])],
        [right, *back_ys, *weights, fixed, *inner],
        [VMEM] * 12,
        [pltpu.VMEM((24, depth), F32)],
        aliases={8: 0, 9: 1, 10: 2},
    )
    sums = lax.all_to_all(sums, MESH_AXES, 0, 0, tiled=True)

    held = pltpu.VMEM(right.shape, F32)
    wx, wy, _, z_weight = weights
    return tuple(
        run(
            bind(finish_kernel, sizes),
            "finish",
            [block] * 2,
            [sums, inverse, values, applied, wx, wy, z_weight, right],
            [VMEM] * 8,
            [held, held, pltpu.SemaphoreType.DMA((2, ext_x // 12))],
            out_specs=[ANY] * 2,
        )
    )


def solution(mesh):
    sizes = dict(mesh.shape)
    in_specs = (P(*MESH_AXES), P(*MESH_AXES), P(), P(), P(), P(), P(), P(), P(), P())
    out_specs = (P(*MESH_AXES), P(*MESH_AXES))
    return jax.shard_map(functools.partial(body, sizes), mesh=mesh, in_specs=in_specs, out_specs=out_specs, check_vma=False)
```

```python
import functools

import jax
import jax.numpy as jnp
from jax import lax
from jax.experimental import pallas as pl
from jax.experimental.pallas import tpu as pltpu
from jax.sharding import PartitionSpec as P

SZ = 64
OV = 4
RIM = OV + 1
LANES = 128
SLOT = 8
GROUP = LANES // SLOT
F32 = jnp.float32
BF16 = jnp.bfloat16
MESH_AXES = ("gx", "gy", "gz")

VMEM = pl.BlockSpec(memory_space=pltpu.VMEM)
ANY = pl.BlockSpec(memory_space=pl.ANY)
HBM = pl.BlockSpec(memory_space=pltpu.HBM)


def call(sizes, kernel, name, outs, args, spaces, scratch=(), limit=8, out_specs=None, aliases=None, flops=0):
    size = sum(o.size * o.dtype.itemsize for o in outs) + sum(a.size * a.dtype.itemsize for a in args)

    def placed(*refs):
        return kernel(place_values(sizes), *refs)

    return pl.pallas_call(
        placed,
        out_shape=outs,
        in_specs=spaces,
        out_specs=out_specs or [VMEM] * len(outs),
        scratch_shapes=list(scratch),
        input_output_aliases=aliases or {},
        name=name,
        compiler_params=pltpu.CompilerParams(vmem_limit_bytes=limit * 2**20),
        cost_estimate=pl.CostEstimate(flops=flops, bytes_accessed=size, transcendentals=0),
    )(*args)


def shape(dims, dtype=F32):
    return jax.ShapeDtypeStruct(tuple(dims), dtype)


def halves(value):
    high = value.astype(BF16)
    return high, (value - high.astype(F32)).astype(BF16)


def dot(left, right):
    return jnp.dot(left, right, preferred_element_type=F32)


def iota(dims, axis):
    return lax.broadcasted_iota(jnp.int32, dims, axis)


IX, IY, IZ, SIDE = 0, 1, 2, 3


def place_values(sizes):
    ix, iy, iz = (lax.axis_index(a) for a in MESH_AXES)
    nz = sizes["gz"]
    if nz == 2:
        sides = [1 - iz, 1]
    else:
        sides = [1, jnp.where(iz < nz - 1, 1, 0), 0, jnp.where(iz > 0, 1, 0)]
    return [ix, iy, iz] + sides


def swap_sides(messages, sizes):
    count = sizes["gz"]
    if count == 2:
        return [lax.ppermute(messages[0], "gz", [(0, 1), (1, 0)])]
    up = [(i, (i + 1) % count) for i in range(count)]
    down = [((i + 1) % count, i) for i in range(count)]
    return [lax.ppermute(messages[1], "gz", down), lax.ppermute(messages[0], "gz", up)]


def swap_ends(first, second, axis, sizes):
    count = sizes[axis]
    received = []
    for message, start in ((first, 0), (second, 1)):
        partner = list(range(count))
        for i in range(start, count - 1, 2):
            partner[i], partner[i + 1] = i + 1, i
        received.append(lax.ppermute(message, axis, list(enumerate(partner))))
    return received


def is_even(place, axis):
    return lax.rem(place[axis], 2) == 0


def from_ends(place, axis, sizes, first, second):
    even = is_even(place, axis)
    inside_low = place[axis] > 0
    inside_high = place[axis] < sizes[MESH_AXES[axis]] - 1

    def low(at):
        return jnp.where(inside_low, jnp.where(even, second[at], first[at]), 0.0)

    def high(at):
        return jnp.where(inside_high, jnp.where(even, first[at], second[at]), 0.0)

    return low, high


def prepare_kernel(sides, cells, place, axes, xv, yv, zv, y_row, z_row, inverse, fx, bx, fy, by, wz, bz, den, spread, pad, wide, rows):
    ez = zv.shape[0]
    depth = wz.shape[0] // 4

    def stacked(value, out):
        size = out.shape[1] // 3
        high, low = (part.astype(F32) for part in halves(value[: LANES // 2]))
        spread = jnp.concatenate([high, jnp.zeros_like(high)], axis=1)
        wide_low = jnp.concatenate([low, jnp.zeros_like(low)], axis=1)
        out[...] = (spread + pltpu.roll(spread, size, 1) + pltpu.roll(wide_low, 2 * size, 1)).astype(BF16)[:, : 3 * size]

    for vectors, forward, back in ((xv, fx, bx), (yv, fy, by)):
        size = vectors.shape[0]
        pad[...] = jnp.zeros_like(pad)
        pad[0:size, 0:size] = vectors[...]
        stacked(pad[...], back)
        if vectors is yv:
            pad[0 : size - OV, 0:size] = vectors[OV:size]
            pad[size - OV : size, 0:size] = vectors[0:OV]
        stacked(pad[...].T, forward)

    wide[...] = jnp.zeros_like(wide)
    wide[0:ez, 0:ez] = zv[...]
    wide[SZ : SZ + ez, LANES : LANES + ez] = zv[...]
    middle = wide[OV : OV + depth]
    high, low = halves(middle)
    wz[0:depth] = high
    wz[depth : 2 * depth] = high
    wz[2 * depth : 3 * depth] = low
    rows[...] = jnp.zeros_like(rows)
    for side in range(sides):
        is_high = place[SIDE + 2 * side] > 0
        for k in range(OV):
            top, bottom = OV + depth + k, k
            row = jnp.where(is_high, wide[top : top + 1], wide[bottom : bottom + 1])
            row_high, row_low = halves(row)
            at = 3 * SLOT * side + k
            rows[at : at + 1] = row_high.astype(F32)
            rows[at + SLOT : at + SLOT + 1] = row_high.astype(F32)
            rows[at + 2 * SLOT : at + 2 * SLOT + 1] = row_low.astype(F32)
    wz[3 * depth :] = rows[...].astype(BF16)

    rows[...] = jnp.zeros_like(rows)
    for side in range(sides):
        is_high = place[SIDE + 2 * side] > 0
        for k in range(RIM):
            top, bottom = OV + depth - 1 + k, k
            rows[SLOT * side + k : SLOT * side + k + 1] = jnp.where(is_high, wide[top : top + 1], wide[bottom : bottom + 1])
    across = 2 * LANES
    for at, part in ((0, middle), (LANES, rows[...])):
        turned = jnp.concatenate([part[:, 0:LANES].T, part[:, LANES:].T], axis=0)
        high, low = halves(turned)
        bz[0:across, at : at + LANES] = high
        bz[across : 2 * across, at : at + LANES] = high
        bz[2 * across :, at : at + LANES] = low

    ey = yv.shape[0]
    diagonal = iota((ey, ey), 0) == iota((ey, ey), 1)
    y_column = jnp.sum(jnp.where(diagonal, y_row[...], 0.0), axis=1, keepdims=True)
    pad[...] = jnp.ones_like(pad)
    pad[0:1, 0:ez] = axes[:, 2:3] * z_row[...]
    den[...] = axes[:, 1:2] * y_column + pad[0:1]
    count, blocks = spread.shape[0], inverse.shape[0]
    member = jnp.where(iota((count, blocks), 0) // 2 == iota((count, blocks), 1), 1.0, 0.0)
    from_block = jnp.where(iota((blocks, count), 0) == iota((blocks, count), 1) // 2, 1.0, 0.0)
    exact = functools.partial(jnp.dot, preferred_element_type=F32, precision=lax.Precision.HIGHEST)
    spread[...] = exact(exact(member, inverse[...]), from_block) / cells


def pack_y_own_kernel(place, right, scale, first, second):
    ext_x, ext_y, depth = right.shape
    even = is_even(place, IY)
    base = (ext_x + 2 * OV) * OV
    for x in range(ext_x):
        low, high = right[x, 0:OV], right[x, ext_y - OV : ext_y]
        at = (x + OV) * OV
        first[at : at + OV] = jnp.where(even, high, low)
        second[at : at + OV] = jnp.where(even, low, high)
        low, high = scale[x, 0:16].astype(F32)[0:1], scale[x, ext_y - 16 : ext_y].astype(F32)[15:16]
        first[base + x : base + x + 1] = jnp.where(even, high, low)
        second[base + x : base + x + 1] = jnp.where(even, low, high)


def pack_y_rest_kernel(sizes, sides, wide_x, place, x_first, x_second, *refs):
    rims, (first, second) = refs[:sides], refs[sides + 2 :]
    ext_y = x_first.shape[1]
    even = is_even(place, IY)
    x_low, x_high = from_ends(place, IX, sizes, x_first, x_second)
    last = (wide_x - 2 * OV) * OV
    groups = (wide_x + GROUP - 1) // GROUP
    for side in range(sides):
        for group in range(groups):
            start = group * ext_y
            low, high = rims[side][start : start + OV], rims[side][start + ext_y - OV : start + ext_y]
            at = wide_x * OV + wide_x - 2 * OV + (side * groups + group) * OV
            first[at : at + OV] = jnp.where(even, high, low)
            second[at : at + OV] = jnp.where(even, low, high)
    for t in range(OV):
        for source, at in ((x_low, t * OV), (x_high, last + OV * OV + t * OV)):
            low, high = source((t, slice(0, OV))), source((t, slice(ext_y - OV, ext_y)))
            first[at : at + OV] = jnp.where(even, high, low)
            second[at : at + OV] = jnp.where(even, low, high)


def pack_z_kernel(planes, faces, sides, place, *refs):
    if faces:
        right, scale, *messages = refs
        sources = {a + OV: right.at[a] for a in range(right.shape[0])}
        ext_x, ext_y, depth = right.shape
    else:
        x_first, x_second, *messages = refs
        messages = messages[sides:]
        low, high = from_ends(place, IX, planes, x_first, x_second)
        ext_y, depth = x_first.shape[1:]
        ext_x = messages[0].shape[0] // ext_y * GROUP - 2 * OV
        ext_x = ext_x // GROUP * GROUP
        sources = {}
    lane = iota((ext_y, LANES), 1)
    for side in range(sides):
        is_high = place[SIDE + 2 * side] > 0
        start, face = jnp.where(is_high, depth - OV, 0), jnp.where(is_high, depth - 1, 0)
        for group in range(messages[side].shape[0] // ext_y):
            at = slice(group * ext_y, (group + 1) * ext_y)
            total = jnp.zeros((ext_y, LANES), F32) if faces else messages[side][at]
            for q in range(GROUP):
                a = group * GROUP + q
                if faces and a in sources:
                    cells = sources[a][...]
                elif not faces and a < OV:
                    cells = low(a)
                elif not faces and ext_x + OV <= a < ext_x + 2 * OV:
                    cells = high(a - OV - ext_x)
                else:
                    cells = None
                if cells is not None:
                    moved = pltpu.roll(cells, lax.rem(SLOT * q + depth - start, depth), 1)
                    total = jnp.where((lane >= SLOT * q) & (lane < SLOT * q + OV), moved, total)
                if faces and a < ext_x:
                    moved = pltpu.roll(scale[a].astype(F32), lax.rem(SLOT * q + OV + depth - face, depth), 1)
                    total = jnp.where(lane == SLOT * q + OV, moved, total)
            messages[side][at] = total


def rim_columns(place, sides, values, q):
    lane = iota(values[0].shape, 1)
    piece = jnp.zeros(values[0].shape, F32)
    for side in range(sides):
        value = jnp.where((lane // SLOT == q) & (place[SIDE + 2 * side + 1] > 0), values[side], 0.0)
        high = value.astype(BF16).astype(F32)
        at = LANES - SLOT * q + 3 * SLOT * side
        for number, part in enumerate((high, value - high, high)):
            shift = (at + number * SLOT) % LANES
            piece = piece + (pltpu.roll(part, shift, 1) if shift else part)
    return piece.astype(BF16)


def z_forward(cells, rims, wz):
    high, low = halves(cells)
    return dot(jnp.concatenate([high, low, high, rims], axis=1), wz[...])


def along(matrix, pair):
    value = jnp.concatenate(pair, axis=1)
    high = value.astype(BF16).astype(F32)
    stack = jnp.concatenate([high, value - high, high], axis=0).astype(BF16)
    return dot(matrix[...], stack)[0 : value.shape[0]]


def strided(pair, at, count, stride):
    return [ref[pl.ds(at, count, stride=stride), :] for ref in pair]


def solve_own_kernel(sizes, sides, place, right, x_first, x_second, *refs):
    received, (fx, wz, out_a, out_b, first_a, first_b) = refs[:sides], refs[sides:]
    ext_x, ext_y, depth = right.shape
    wide = ext_x + 2 * OV
    low, high = from_ends(place, IX, sizes, x_first, x_second)
    batch = 8
    for start in range(0, wide, batch):
        cells, rims = [], []
        for a in range(start, start + batch):
            if a < OV:
                cells.append(low(a))
            elif a < ext_x + OV:
                cells.append(right[a - OV])
            else:
                cells.append(high(a - OV - ext_x))
            at = slice(a // GROUP * ext_y, (a // GROUP + 1) * ext_y)
            rims.append(rim_columns(place, sides, [ref[at] for ref in received], a % GROUP))
        out = z_forward(jnp.concatenate(cells, axis=0), jnp.concatenate(rims, axis=0), wz)
        block = pl.ds(start * ext_y, batch * ext_y)
        first_a[block] = out[:, 0:LANES]
        first_b[block] = out[:, LANES:]
    for y in range(ext_y):
        out = along(fx, strided((first_a, first_b), y, wide, ext_y))
        out_a[y * wide : (y + 1) * wide] = out[:, 0:LANES]
        out_b[y * wide : (y + 1) * wide] = out[:, LANES:]


def solve_rest_kernel(sizes, sides, place, axes, x_values, scale, y_first, y_second, own_a, own_b, *refs):
    fx, bx, fy, by, wz, bz, den, back_a, back_b, first, second = refs[:11]
    edge_a, edge_b, halo_a, halo_b, mode_a, mode_b = refs[11:]
    wide = x_values.shape[1]
    rows = back_a.shape[0]
    wide_y = rows // wide
    ext_y = wide_y - 2 * OV
    groups = (wide + GROUP - 1) // GROUP
    low, high = from_ends(place, IY, sizes, y_first, y_second)
    both = []
    for side in range(sides):
        values = []
        for group in range(groups):
            at = wide * OV + wide - 2 * OV + (side * groups + group) * OV
            values.append(jnp.concatenate([high(slice(at, at + OV)), low(slice(at, at + OV))], axis=0))
        both.append(values)
    cells, rims = [], []
    for a in range(wide):
        part = slice(a * OV, (a + 1) * OV)
        cells.append(jnp.concatenate([high(part), low(part)], axis=0))
        rims.append(rim_columns(place, sides, [values[a // GROUP] for values in both], a % GROUP))
    out = z_forward(jnp.concatenate(cells, axis=0), jnp.concatenate(rims, axis=0), wz)
    edge_a[...] = out[:, 0:LANES]
    edge_b[...] = out[:, LANES:]
    for t in range(2 * OV):
        out = along(fx, strided((edge_a, edge_b), t, wide, 2 * OV))
        halo_a[t * wide : (t + 1) * wide] = out[:, 0:LANES]
        halo_b[t * wide : (t + 1) * wide] = out[:, LANES:]
    for i in range(wide):
        pair = []
        for inside, outside in ((own_a, halo_a), (own_b, halo_b)):
            parts = strided((inside,), i, ext_y, wide) + strided((outside,), i, 2 * OV, wide)
            pair.append(jnp.concatenate(parts, axis=0))
        out = along(fy, pair)
        inverse = 1.0 / (axes[:, 0:1] * x_values[:, i : i + 1] + den[...])
        out = along(by, [out[:, 0:LANES] * inverse, out[:, LANES:] * inverse])
        mode_a[pl.ds(i * wide_y, wide_y)] = out[:, 0:LANES]
        mode_b[pl.ds(i * wide_y, wide_y)] = out[:, LANES:]
    for y in range(wide_y):
        out = along(bx, strided((mode_a, mode_b), y, wide, wide_y))
        back_a[pl.ds(y, wide, stride=wide_y), :] = out[:, 0:LANES]
        back_b[pl.ds(y, wide, stride=wide_y), :] = out[:, LANES:]
    even = is_even(place, IX)
    ends = RIM * wide_y
    low, low_rims = z_back(sides, wide_y, back_a, back_b, bz, 0, RIM)
    high, high_rims = z_back(sides, wide_y, back_a, back_b, bz, wide - RIM, RIM)
    first[0:ends] = jnp.where(even, high, low)
    second[0:ends] = jnp.where(even, low, high)
    for side in range(sides):
        low = sum(low_rims[side].values())
        high = sum(high_rims[side].values())
        at = ends + side * wide_y
        first[at : at + wide_y] = jnp.where(even, high, low)
        second[at : at + wide_y] = jnp.where(even, low, high)
    low, high = scale[0].astype(F32), scale[scale.shape[0] - 1].astype(F32)
    at = ends + sides * wide_y
    first[at : at + ext_y] = jnp.where(even, high, low)
    second[at : at + ext_y] = jnp.where(even, low, high)


def z_back(sides, wide_y, back_a, back_b, bz, start, count):
    lane = iota((wide_y, LANES), 1)
    block = pl.ds(start * wide_y, count * wide_y)
    high_a, low_a = halves(back_a[block])
    high_b, low_b = halves(back_b[block])
    out = dot(jnp.concatenate([high_a, high_b, low_a, low_b, high_a, high_b], axis=1), bz[...])
    rims = [{} for _ in range(sides)]
    for a in range(start, start + count):
        group, q = a // GROUP, a % GROUP
        value = out[(a - start) * wide_y : (a - start + 1) * wide_y, LANES:]
        for side in range(sides):
            own = value if sides == 1 else jnp.where(lane // SLOT == side, value, 0.0)
            at = (SLOT * q + LANES - SLOT * side) % LANES
            moved = pltpu.roll(own, at, 1) if at else own
            rims[side][group] = rims[side][group] + moved if group in rims[side] else moved
    return out[:, 0:LANES], rims


def solve_tail_kernel(sides, wide, place, back_a, back_b, bz, local, *rims):
    wide_y = back_a.shape[0] // wide
    for side in range(sides):
        rims[side][...] = jnp.zeros_like(rims[side])
    count = 10
    for start in range(OV - 1, wide - OV + 1, count):
        out, more = z_back(sides, wide_y, back_a, back_b, bz, start, count)
        at = start - OV + 1
        local[at * wide_y : (at + count) * wide_y] = out
        for side in range(sides):
            for group, value in more[side].items():
                rims[side][group * wide_y : (group + 1) * wide_y] += value


def placed_rims(place, sides, received, a, rows):
    total = None
    for side in range(sides):
        is_high, valid = place[SIDE + 2 * side] > 0, place[SIDE + 2 * side + 1] > 0
        start = jnp.where(is_high, LANES - OV, 0)
        shift = lax.rem(jnp.where(is_high, LANES - OV, LANES - 1) + LANES - SLOT * (a % GROUP), LANES)
        value = received[side][rows]
        lane = iota(value.shape, 1)
        value = jnp.where((lane >= start) & (lane < start + OV) & valid, pltpu.roll(value, shift, 1), 0.0)
        total = value if total is None else total + value
    return total


def pack_back_z_kernel(sizes, sides, wide, wide_y, place, x_first, x_second, *refs):
    own, out = refs[:sides], refs[sides:]
    _, faces = x_received(sizes, wide, wide_y, place, x_first, x_second)
    for side in range(sides):
        for group in range((wide + GROUP - 1) // GROUP):
            part = slice(group * wide_y, (group + 1) * wide_y)
            more = faces(side, group, slice(0, wide_y))
            out[side][part] = own[side][part] if more is None else own[side][part] + more


def fold_x_kernel(sizes, wide, wide_y, place, x_first, x_second, local, out):
    plane, _ = x_received(sizes, wide, wide_y, place, x_first, x_second)
    for p in range(wide - 2 * OV + 2):
        part = slice(p * wide_y, (p + 1) * wide_y)
        more = plane(p + OV - 1, slice(0, wide_y))
        out[part] = local[part] if more is None else local[part] + more


def pack_back_y_kernel(sides, wide, wide_y, place, field, *refs):
    own, received = refs[:sides], refs[sides : 2 * sides]
    faces, (first, second) = refs[2 * sides : 3 * sides], refs[3 * sides :]
    groups = (wide + GROUP - 1) // GROUP
    planes = wide - 2 * OV + 2
    even = is_even(place, IY)

    def put(at, low, high):
        first[at : at + RIM] = jnp.where(even, high, low)
        second[at : at + RIM] = jnp.where(even, low, high)

    lane = iota((groups * wide_y, LANES), 1)
    for side in range(sides):
        is_high, valid = place[SIDE + 2 * side] > 0, place[SIDE + 2 * side + 1] > 0
        other = pltpu.roll(received[side][...], jnp.where(is_high, LANES - OV, 0), 1)
        mine = pltpu.roll(own[side][...], jnp.where(is_high, LANES - 1, LANES - OV + 1), 1)
        faces[side][...] = jnp.where((lax.rem(lane, SLOT) == 0) & valid, other + mine, 0.0)
        for group in range(groups):
            low = faces[side][group * wide_y : group * wide_y + 8]
            high = faces[side][(group + 1) * wide_y - 8 : (group + 1) * wide_y]
            put(planes * RIM + (side * groups + group) * RIM, low[0:RIM], high[8 - RIM :])
    for p in range(planes):
        a = p + OV - 1
        ends = []
        for start in (0, wide_y - 8):
            at = a // GROUP * wide_y + start
            value = placed_rims(place, sides, received, a, slice(at, at + 8))
            ends.append(field[p * wide_y + start : p * wide_y + start + 8] + value)
        put(p * RIM, ends[0][0:RIM], ends[1][8 - RIM :])


def x_received(sizes, wide, wide_y, place, x_first, x_second):
    low, high = from_ends(place, IX, sizes, x_first, x_second)
    high_lane = (wide - 2 * OV) % GROUP * SLOT

    def plane(a, rows):
        if OV - 1 <= a < OV - 1 + RIM:
            at, source = (a - OV + 1) * wide_y, low
        elif wide - 2 * OV <= a < wide - 2 * OV + RIM:
            at, source = (a - wide + 2 * OV) * wide_y, high
        else:
            return None
        return source(slice(at + rows.start, at + rows.stop))

    def faces(side, group, rows):
        lane = iota((rows.stop - rows.start, LANES), 1)
        at = (RIM + side) * wide_y
        rows = slice(at + rows.start, at + rows.stop)
        if group == 0:
            return jnp.where((lane >= (OV - 1) * SLOT) & (lane < 2 * OV * SLOT), low(rows), 0.0)
        if group == (wide + GROUP - 1) // GROUP - 1:
            return jnp.where((lane >= high_lane) & (lane < high_lane + RIM * SLOT), high(rows), 0.0)
        return None

    return plane, faces


def weights_kernel(sizes, sides, place, axes, right, scale, x_first, x_second, y_first, y_second, *refs):
    scale_faces = refs[:sides]
    wx, wy, wz, z_weight, sums, scales = refs[sides:]
    ext_x, ext_y, depth = right.shape
    core = slice(8, 8 + ext_y)
    x_low, x_high = from_ends(place, IX, sizes, x_first, x_second)
    y_low, y_high = from_ends(place, IY, sizes, y_first, y_second)
    y_rows = (ext_x + 2 * OV) * OV
    x_rows = slice(x_first.shape[0] - ext_y, x_first.shape[0])
    scales[0, core] = x_low(x_rows)
    scales[ext_x + 1, core] = x_high(x_rows)
    for x in range(ext_x):
        scales[x + 1, core] = scale[x].astype(F32)
        part = slice(y_rows + x, y_rows + x + 1)
        scales[x + 1, 7:8] = y_low(part)
        scales[x + 1, 8 + ext_y : 9 + ext_y] = y_high(part)
    hx, hy, hz = (0.5 * axes[:, d : d + 1] for d in range(3))
    lane = iota((8, depth), 1)
    ends = (lane == 0) | (lane == depth - 1)
    zero = jnp.zeros((8, depth), F32)
    sum_right, sum_z = zero, zero
    for x in range(ext_x + 1):
        wx[x] = hx * (scales[x, core] + scales[x + 1, core])
    for x in range(ext_x):
        wy[x, 0 : ext_y + 1] = hy * (scales[x + 1, 7 : 8 + ext_y] + scales[x + 1, 8 : 9 + ext_y])
        for row in range(0, ext_y, 8):
            own = scales[x + 1, 8 + row : 16 + row]
            edge = zero
            for side in range(sides):
                is_high, valid = place[SIDE + 2 * side] > 0, place[SIDE + 2 * side + 1] > 0
                target = jnp.where(is_high, depth - 1, 0)
                at = x // GROUP * ext_y + row
                shift = lax.rem(target + depth - (x % GROUP * SLOT + OV), depth)
                edge = jnp.where((lane == target) & valid, pltpu.roll(scale_faces[side][at : at + 8], shift, 1), edge)
            wz[x, row : row + 8] = hz * (own + jnp.where(lane == 0, edge, pltpu.roll(own, 1, 1)))
            end_weight = jnp.where(ends, hz * (own + edge), 0.0)
            z_weight[x, row : row + 8] = end_weight
            sum_z = sum_z + end_weight
            sum_right = sum_right + right[x, row : row + 8]

    def whole(value):
        return jnp.sum(jnp.sum(value, axis=0, keepdims=True), axis=1, keepdims=True)

    def y_sum(row):
        total = jnp.zeros((1, depth), F32)
        for x in range(ext_x):
            total = total + wy[x, row : row + 1]
        return whole(total)

    x_high_sum, y_high_sum = whole(wx[ext_x]), y_sum(ext_y)
    z_high_sum = whole(jnp.where(lane == depth - 1, sum_z, 0.0))
    faces_sum = whole(wx[0]) + x_high_sum + y_sum(0) + y_high_sum + whole(sum_z)
    columns = {
        0: whole(sum_right),
        4: faces_sum,
        5: jnp.where(place[IX] < sizes["gx"] - 1, x_high_sum, 0.0),
        6: jnp.where(place[IY] < sizes["gy"] - 1, y_high_sum, 0.0),
        7: jnp.where(place[IZ] < sizes["gz"] - 1, z_high_sum, 0.0),
    }
    sums[...] = in_columns(columns, jnp.zeros((1, LANES), F32))


def in_columns(columns, row):
    at = iota((1, LANES), 1)
    for number, value in columns.items():
        row = jnp.where(at == number, value, row)
    return row


def operator_tile(place, sides, groups, values, edges, wx, wy, wz, z_weight, block, inner, row):
    depth = values.shape[2]
    ext_y = z_weight.shape[1]
    lane = iota((8, depth), 1)
    at = slice(8 + row, 16 + row)
    x = block * GROUP + inner
    mid = values[x + 1, at]
    total = wx[x, row : row + 8] * (mid - values[x, at]) + wx[x + 1, row : row + 8] * (mid - values[x + 2, at])
    total = total + wy[x, row : row + 8] * (mid - values[x + 1, 7 + row : 15 + row])
    total = total + wy[x, row + 1 : row + 9] * (mid - values[x + 1, 9 + row : 17 + row])
    edge = jnp.zeros((8, depth), F32)
    for side in range(sides):
        is_high, valid = place[SIDE + 2 * side] > 0, place[SIDE + 2 * side + 1] > 0
        target = jnp.where(is_high, depth - 1, 0)
        start = (side * groups + block + (inner + OV) // GROUP) * ext_y + row
        moved = edges[pl.ds(pl.multiple_of(start, 8), 8)]
        q = (inner + OV) % GROUP
        if q:
            moved = pltpu.roll(moved, depth - q * SLOT, 1)
        edge = jnp.where((lane == target) & valid, moved, edge)
    flux = wz[x, row : row + 8] * (mid - jnp.where(lane == 0, edge, pltpu.roll(mid, 1, 1)))
    above = z_weight[x, row : row + 8] * (mid - edge)
    total = total + flux + jnp.where(lane == depth - 1, above, -pltpu.roll(flux, depth - 1, 1))
    return mid, total


def operator_tiles(place, sides, groups, right, values, edges, weights, applied, sums, rows):
    def several(block, totals):
        product, energy, whole = totals
        for inner in range(GROUP):
            x = block * GROUP + inner
            for row in rows:
                mid, total = operator_tile(place, sides, groups, values, edges, *weights, block, inner, row)
                applied[x, row : row + 8] = total
                product = product + right[x, row : row + 8] * mid
                energy = energy + mid * total
                whole = whole + total
        return product, energy, whole

    totals = lax.fori_loop(0, right.shape[0] // GROUP, several, (jnp.zeros((8, values.shape[2]), F32),) * 3)
    for number, value in enumerate(totals):
        sums[number * 8 : (number + 1) * 8] = value


def to_face(place, side, value):
    return pltpu.roll(value, jnp.where(place[SIDE + 2 * side] > 0, LANES - 1, 0), 1)


def inner_kernel(sizes, sides, wide, place, right, field, *refs):
    received, faces, weights = refs[:sides], refs[sides : 2 * sides], refs[2 * sides : 2 * sides + 4]
    values, edges, applied, sums = refs[2 * sides + 4 :]
    ext_x, ext_y, depth = right.shape
    wide_y = ext_y + 2 * OV
    groups = (wide + GROUP - 1) // GROUP
    inside_low, inside_high = place[IX] > 0, place[IX] < sizes["gx"] - 1
    for p in range(ext_x + 2):
        a = p + OV - 1
        at = a // GROUP * wide_y
        value = placed_rims(place, sides, received, a, slice(at, at + wide_y))
        value = value + field[p * wide_y : (p + 1) * wide_y]
        if p == 0:
            value = jnp.where(inside_low, value, 0.0)
        if p == ext_x + 1:
            value = jnp.where(inside_high, value, 0.0)
        values[p, 8 - OV : 8 - OV + wide_y] = value
    for side in range(sides):
        for group in range(groups):
            value = faces[side][group * wide_y : (group + 1) * wide_y]
            at = (side * groups + group) * ext_y
            edges[at : at + ext_y] = to_face(place, side, value)[OV : OV + ext_y]
    operator_tiles(place, sides, groups, right, values, edges, weights, applied, sums, range(8, ext_y - 8, 8))


def outer_kernel(sizes, sides, wide, place, right, y_first, y_second, *refs):
    weights, fixed, refs = refs[:4], refs[4], refs[5:]
    inner_sums, refs = refs[3], refs[4:]
    values, edges, applied, out, sums = refs
    ext_x, ext_y, depth = right.shape
    wide_y = ext_y + 2 * OV
    groups = (wide + GROUP - 1) // GROUP
    low, high = from_ends(place, IY, sizes, y_first, y_second)
    inside_low, inside_high = place[IY] > 0, place[IY] < sizes["gy"] - 1
    for p in range(ext_x + 2):
        part = slice(p * RIM, (p + 1) * RIM)
        low_rows, high_rows = low(part), high(part)
        if p == 0 or p == ext_x + 1:
            inside = place[IX] > 0 if p == 0 else place[IX] < sizes["gx"] - 1
            low_rows, high_rows = (jnp.where(inside, rows, 0.0) for rows in (low_rows, high_rows))
        values[p, 7 : 7 + RIM] += low_rows
        values[p, 4 + ext_y : 4 + ext_y + RIM] += high_rows
        values[p, 7:8] = jnp.where(inside_low, values[p, 7:8], 0.0)
        values[p, 8 + ext_y : 9 + ext_y] = jnp.where(inside_high, values[p, 8 + ext_y : 9 + ext_y], 0.0)
    for number in range(sides * groups):
        at = (ext_x + 2 + number) * RIM
        start = number * ext_y
        side = number // groups
        edges[start : start + OV] += to_face(place, side, low(slice(at, at + RIM)))[1:]
        edges[start + ext_y - OV : start + ext_y] += to_face(place, side, high(slice(at, at + RIM)))[:OV]
    operator_tiles(place, sides, groups, right, values, edges, weights, applied, sums, (0, ext_y - 8))
    columns = {}
    for number in range(3):
        part = slice(number * 8, (number + 1) * 8)
        value = inner_sums[part] + sums[part]
        columns[number + 1] = jnp.sum(jnp.sum(value, axis=0, keepdims=True), axis=1, keepdims=True)
    out[...] = jnp.broadcast_to(in_columns(columns, fixed[...]), out.shape)


def finish_kernel(sizes, place, sums, spread, values, applied, wx, wy, z_weight, right, solution, residual, held_s, held_r, sems):
    ext_x, ext_y, depth = right.shape
    nx, ny, nz = (sizes[a] for a in MESH_AXES)
    count = nx * ny * nz
    table = sums[...]
    part = [table[:, k : k + 1] for k in range(8)]
    from_device = iota((count, count), 0) == iota((count, count), 1)
    sums_row = jnp.sum(jnp.where(from_device, part[0], 0.0), axis=0, keepdims=True)
    level = jnp.sum(spread[...] * sums_row, axis=1, keepdims=True)

    def shifted(by):
        return jnp.concatenate([level[by:], level[:by]], axis=0)

    def whole(value):
        return jnp.sum(value, axis=0, keepdims=True)

    product = whole(part[1] + level * part[0])
    neighbours = part[5] * shifted(ny * nz) + part[6] * shifted(nz) + part[7] * shifted(1)
    curvature = whole(part[2] + 2.0 * level * part[3] + level * (level * part[4] - 2.0 * neighbours))
    step = product / curvature
    device = iota((count, 1), 0)
    mine = (place[IX] * ny + place[IY]) * nz + place[IZ]

    def level_at(number, inside):
        return whole(jnp.where((device == number) & inside, level, 0.0))

    own = level_at(mine, True)
    drops = []
    for axis, stride, size in ((IX, ny * nz, nx), (IY, nz, ny), (IZ, 1, nz)):
        drops.append(step * (own - level_at(mine - stride, place[axis] > 0)))
        drops.append(step * (own - level_at(mine + stride, place[axis] < size - 1)))
    z_drop = jnp.where(iota((1, depth), 1) < depth // 2, drops[4], drops[5])
    chunk = 12
    for x in range(ext_x):
        held_s[x] = step * (values[x + 1, 8 : 8 + ext_y] + own)
        value = right[x] - step * applied[x] - z_drop * z_weight[x]
        if x == 0:
            value = value - drops[0] * wx[0]
        if x == ext_x - 1:
            value = value - drops[1] * wx[ext_x]
        held_r[x] = value
        held_r[x, 0:1] = value[0:1] - drops[2] * wy[x, 0:1]
        held_r[x, ext_y - 1 : ext_y] = value[ext_y - 1 : ext_y] - drops[3] * wy[x, ext_y : ext_y + 1]
        if (x + 1) % chunk == 0:
            part_x = pl.ds(x + 1 - chunk, chunk)
            number = (x + 1) // chunk - 1
            pltpu.make_async_copy(held_s.at[part_x], solution.at[part_x], sems.at[0, number]).start()
            pltpu.make_async_copy(held_r.at[part_x], residual.at[part_x], sems.at[1, number]).start()
    for number in range(ext_x // chunk):
        part_x = pl.ds(number * chunk, chunk)
        pltpu.make_async_copy(held_s.at[part_x], solution.at[part_x], sems.at[0, number]).wait()
        pltpu.make_async_copy(held_r.at[part_x], residual.at[part_x], sems.at[1, number]).wait()


def body(sizes, right, scale, axes, xv, yv, zv, x_values, y_values, z_values, inverse):
    ext_x, ext_y, depth = right.shape
    wide_x, wide_y = xv.shape[0], yv.shape[0]
    sides = 1 if sizes["gz"] == 2 else 2
    groups = (wide_x + GROUP - 1) // GROUP
    count = sizes["gx"] * sizes["gy"] * sizes["gz"]
    bind = functools.partial
    run = bind(call, sizes)
    block = shape(right.shape)
    axes_row = axes.reshape(1, -1)
    beside = 2 * 10**9

    up = lax.rem(lax.axis_index("gx"), 2) == 0
    starts = jnp.where(up, ext_x - OV, 0), jnp.where(up, 0, ext_x - OV)
    xs = [lax.dynamic_slice_in_dim(right, start, OV, 0) for start in starts]
    xs = swap_ends(*xs, "gx", sizes)

    thin = [shape([LANES // 2, 3 * size], BF16) for size in (wide_x, wide_x, wide_y, wide_y)]
    mats = run(
        bind(prepare_kernel, sides, 2.0 * ext_x * ext_y * depth),
        "prepare",
        thin + [shape([4 * depth, 2 * LANES], BF16), shape([6 * LANES, 2 * LANES], BF16), shape([wide_y, LANES]), shape([count, count])],
        [axes_row, xv, yv, zv, y_values.reshape(1, -1), z_values.reshape(1, -1), inverse],
        [VMEM] * 7,
        [pltpu.VMEM((LANES, LANES), F32), pltpu.VMEM((depth + 2 * OV, 2 * LANES), F32), pltpu.VMEM((LANES, 2 * LANES), F32)],
        flops=beside,
    )
    rim_message = [shape([groups * ext_y, LANES])] * sides
    rims = run(
        bind(pack_z_kernel, None, True, sides),
        "pack_z_own",
        rim_message,
        [right, scale],
        [VMEM] * 2,
        flops=beside,
    )
    y_message = [shape([wide_x * OV + ext_x + sides * groups * OV, depth])] * 2
    ys = run(pack_y_own_kernel, "pack_y_own", y_message, [right, scale], [VMEM] * 2, flops=beside)
    rims, ys, mats = lax.optimization_barrier((rims, ys, mats))
    *mats, spread = mats
    rims = run(
        bind(pack_z_kernel, sizes, False, sides),
        "pack_z_rest",
        rim_message,
        [*xs, *rims],
        [VMEM] * (2 + sides),
        aliases={2 + k: k for k in range(sides)},
    )
    rims = swap_sides(rims, sizes)

    ys = run(
        bind(pack_y_rest_kernel, sizes, sides, wide_x),
        "pack_y_rest",
        y_message,
        [*xs, *rims, *ys],
        [VMEM] * (4 + sides),
        aliases={2 + sides: 0, 3 + sides: 1},
    )
    ys = swap_ends(*ys, "gy", sizes)

    fx, _, _, _, wz, _, _ = mats
    tall = pltpu.VMEM((wide_x * wide_y, LANES), F32)
    core = pltpu.VMEM((wide_x * ext_y, LANES), F32)
    owns = run(
        bind(solve_own_kernel, sizes, sides),
        "solve_own",
        [shape([wide_x * ext_y, LANES])] * 2,
        [right, *xs, *rims, fx, wz],
        [VMEM] * (5 + sides),
        [core] * 2,
        limit=16,
        flops=2 * beside,
    )
    field = shape([wide_x * wide_y, depth])
    rim_message = shape([groups * wide_y, LANES])
    edge = pltpu.VMEM((wide_x * 2 * OV, LANES), F32)
    *back, low, high = run(
        bind(solve_rest_kernel, sizes, sides),
        "solve_rest",
        [field] * 2 + [shape([(RIM + sides) * wide_y + ext_y, depth])] * 2,
        [axes_row, x_values.reshape(1, -1), scale, *ys, *owns, *mats],
        [VMEM] * (7 + len(mats)),
        [edge] * 4 + [tall] * 2,
        limit=20,
    )
    back_xs = swap_ends(low, high, "gx", sizes)

    planes = ext_x + 2
    field = shape([planes * wide_y, depth])
    local, *own_rims = run(
        bind(solve_tail_kernel, sides, wide_x),
        "solve_tail",
        [field] + [rim_message] * sides,
        [*back, mats[5]],
        [VMEM] * 3,
        flops=beside,
    )
    own_rims = run(
        bind(pack_back_z_kernel, sizes, sides, wide_x, wide_y),
        "pack_back_z",
        [rim_message] * sides,
        [*back_xs, *own_rims],
        [VMEM] * (2 + sides),
    )
    late_rims, own_rims = lax.optimization_barrier((rims, own_rims))
    other_rims = swap_sides(own_rims, sizes)
    field_x = run(
        bind(fold_x_kernel, sizes, wide_x, wide_y),
        "fold_x",
        [field],
        [*back_xs, local],
        [VMEM] * 3,
        flops=beside,
    )[0]
    scale_block = pltpu.VMEM((planes, ext_y + 16, depth), F32)
    *weights, fixed = run(
        bind(weights_kernel, sizes, sides),
        "weights",
        [shape([ext_x + 1, ext_y, depth]), shape([ext_x, ext_y + 8, depth]), block, block, shape([1, LANES])],
        [axes_row, right, scale, *back_xs, *ys, *late_rims],
        [VMEM] * (7 + sides),
        [scale_block],
        flops=beside,
    )
    *faces, low, high = run(
        bind(pack_back_y_kernel, sides, wide_x, wide_y),
        "pack_back_y",
        [rim_message] * sides + [shape([(planes + groups * sides) * RIM, depth])] * 2,
        [field_x, *own_rims, *other_rims],
        [VMEM] * (1 + 2 * sides),
    )
    back_ys = swap_ends(low, high, "gy", sizes)

    parts = [shape([planes, ext_y + 16, depth]), shape([sides * groups * ext_y, LANES]), block]
    inner = run(
        bind(inner_kernel, sizes, sides, wide_x),
        "inner",
        parts + [shape([24, depth])],
        [right, field_x, *other_rims, *faces, *weights],
        [VMEM] * (6 + 2 * sides),
        flops=beside,
    )
    values, edges, applied, sums = run(
        bind(outer_kernel, sizes, sides, wide_x),
        "outer",
        parts + [shape([count, LANES])],
        [right, *back_ys, *weights, fixed, *inner],
        [VMEM] * 12,
        [pltpu.VMEM((24, depth), F32)],
        aliases={8: 0, 9: 1, 10: 2},
    )
    sums = lax.all_to_all(sums, MESH_AXES, 0, 0, tiled=True)

    held = pltpu.VMEM(right.shape, F32)
    wx, wy, _, z_weight = weights
    return tuple(
        run(
            bind(finish_kernel, sizes),
            "finish",
            [block] * 2,
            [sums, spread, values, applied, wx, wy, z_weight, right],
            [VMEM] * 8,
            [held, held, pltpu.SemaphoreType.DMA((2, ext_x // 12))],
            out_specs=[ANY] * 2,
        )
    )


def solution(mesh):
    sizes = dict(mesh.shape)
    in_specs = (P(*MESH_AXES), P(*MESH_AXES), P(), P(), P(), P(), P(), P(), P(), P())
    out_specs = (P(*MESH_AXES), P(*MESH_AXES))
    return jax.shard_map(functools.partial(body, sizes), mesh=mesh, in_specs=in_specs, out_specs=out_specs, check_vma=False)
```

```python
import functools

import jax
import jax.numpy as jnp
from jax import lax
from jax.experimental import pallas as pl
from jax.experimental.pallas import tpu as pltpu
from jax.sharding import PartitionSpec as P

SZ = 64
OV = 4
RIM = OV + 1
LANES = 128
SLOT = 8
GROUP = LANES // SLOT
F32 = jnp.float32
BF16 = jnp.bfloat16
MESH_AXES = ("gx", "gy", "gz")

VMEM = pl.BlockSpec(memory_space=pltpu.VMEM)
ANY = pl.BlockSpec(memory_space=pl.ANY)
HBM = pl.BlockSpec(memory_space=pltpu.HBM)


def call(sizes, kernel, name, outs, args, spaces, scratch=(), limit=8, out_specs=None, aliases=None, flops=0):
    size = sum(o.size * o.dtype.itemsize for o in outs) + sum(a.size * a.dtype.itemsize for a in args)

    def placed(*refs):
        return kernel(place_values(sizes), *refs)

    return pl.pallas_call(
        placed,
        out_shape=outs,
        in_specs=spaces,
        out_specs=out_specs or [VMEM] * len(outs),
        scratch_shapes=list(scratch),
        input_output_aliases=aliases or {},
        name=name,
        compiler_params=pltpu.CompilerParams(vmem_limit_bytes=limit * 2**20),
        cost_estimate=pl.CostEstimate(flops=flops, bytes_accessed=size, transcendentals=0),
    )(*args)


def shape(dims, dtype=F32):
    return jax.ShapeDtypeStruct(tuple(dims), dtype)


def halves(value):
    high = value.astype(BF16)
    return high, (value - high.astype(F32)).astype(BF16)


def dot(left, right):
    return jnp.dot(left, right, preferred_element_type=F32)


def iota(dims, axis):
    return lax.broadcasted_iota(jnp.int32, dims, axis)


IX, IY, IZ, SIDE = 0, 1, 2, 3


def place_values(sizes):
    ix, iy, iz = (lax.axis_index(a) for a in MESH_AXES)
    nz = sizes["gz"]
    if nz == 2:
        sides = [1 - iz, 1]
    else:
        sides = [1, jnp.where(iz < nz - 1, 1, 0), 0, jnp.where(iz > 0, 1, 0)]
    return [ix, iy, iz] + sides


def swap_sides(messages, sizes):
    count = sizes["gz"]
    if count == 2:
        return [lax.ppermute(messages[0], "gz", [(0, 1), (1, 0)])]
    up = [(i, (i + 1) % count) for i in range(count)]
    down = [((i + 1) % count, i) for i in range(count)]
    return [lax.ppermute(messages[1], "gz", down), lax.ppermute(messages[0], "gz", up)]


def swap_ends(first, second, axis, sizes):
    count = sizes[axis]
    received = []
    for message, start in ((first, 0), (second, 1)):
        partner = list(range(count))
        for i in range(start, count - 1, 2):
            partner[i], partner[i + 1] = i + 1, i
        received.append(lax.ppermute(message, axis, list(enumerate(partner))))
    return received


def is_even(place, axis):
    return lax.rem(place[axis], 2) == 0


def from_ends(place, axis, sizes, first, second):
    even = is_even(place, axis)
    inside_low = place[axis] > 0
    inside_high = place[axis] < sizes[MESH_AXES[axis]] - 1

    def low(at):
        return jnp.where(inside_low, jnp.where(even, second[at], first[at]), 0.0)

    def high(at):
        return jnp.where(inside_high, jnp.where(even, first[at], second[at]), 0.0)

    return low, high


def prepare_kernel(sides, cells, place, axes, xv, yv, zv, y_row, z_row, inverse, fx, bx, fy, by, wz, bz, den, spread, pad, wide, rows):
    ez = zv.shape[0]
    depth = wz.shape[0] // 4

    def stacked(value, out):
        size = out.shape[1] // 3
        high, low = (part.astype(F32) for part in halves(value[: LANES // 2]))
        spread = jnp.concatenate([high, jnp.zeros_like(high)], axis=1)
        wide_low = jnp.concatenate([low, jnp.zeros_like(low)], axis=1)
        out[...] = (spread + pltpu.roll(spread, size, 1) + pltpu.roll(wide_low, 2 * size, 1)).astype(BF16)[:, : 3 * size]

    for vectors, forward, back in ((xv, fx, bx), (yv, fy, by)):
        size = vectors.shape[0]
        pad[...] = jnp.zeros_like(pad)
        pad[0:size, 0:size] = vectors[...]
        stacked(pad[...], back)
        if vectors is yv:
            pad[0 : size - OV, 0:size] = vectors[OV:size]
            pad[size - OV : size, 0:size] = vectors[0:OV]
        stacked(pad[...].T, forward)

    wide[...] = jnp.zeros_like(wide)
    wide[0:ez, 0:ez] = zv[...]
    wide[SZ : SZ + ez, LANES : LANES + ez] = zv[...]
    middle = wide[OV : OV + depth]
    high, low = halves(middle)
    wz[0:depth] = high
    wz[depth : 2 * depth] = high
    wz[2 * depth : 3 * depth] = low
    rows[...] = jnp.zeros_like(rows)
    for side in range(sides):
        is_high = place[SIDE + 2 * side] > 0
        for k in range(OV):
            top, bottom = OV + depth + k, k
            row = jnp.where(is_high, wide[top : top + 1], wide[bottom : bottom + 1])
            row_high, row_low = halves(row)
            at = 3 * SLOT * side + k
            rows[at : at + 1] = row_high.astype(F32)
            rows[at + SLOT : at + SLOT + 1] = row_high.astype(F32)
            rows[at + 2 * SLOT : at + 2 * SLOT + 1] = row_low.astype(F32)
    wz[3 * depth :] = rows[...].astype(BF16)

    rows[...] = jnp.zeros_like(rows)
    for side in range(sides):
        is_high = place[SIDE + 2 * side] > 0
        for k in range(RIM):
            top, bottom = OV + depth - 1 + k, k
            rows[SLOT * side + k : SLOT * side + k + 1] = jnp.where(is_high, wide[top : top + 1], wide[bottom : bottom + 1])
    across = 2 * LANES
    for at, part in ((0, middle), (LANES, rows[...])):
        turned = jnp.concatenate([part[:, 0:LANES].T, part[:, LANES:].T], axis=0)
        high, low = halves(turned)
        bz[0:across, at : at + LANES] = high
        bz[across : 2 * across, at : at + LANES] = high
        bz[2 * across :, at : at + LANES] = low

    ey = yv.shape[0]
    diagonal = iota((ey, ey), 0) == iota((ey, ey), 1)
    y_column = jnp.sum(jnp.where(diagonal, y_row[...], 0.0), axis=1, keepdims=True)
    pad[...] = jnp.ones_like(pad)
    pad[0:1, 0:ez] = axes[:, 2:3] * z_row[...]
    den[...] = axes[:, 1:2] * y_column + pad[0:1]
    count, blocks = spread.shape[0], inverse.shape[0]
    member = jnp.where(iota((count, blocks), 0) // 2 == iota((count, blocks), 1), 1.0, 0.0)
    from_block = jnp.where(iota((blocks, count), 0) == iota((blocks, count), 1) // 2, 1.0, 0.0)
    exact = functools.partial(jnp.dot, preferred_element_type=F32, precision=lax.Precision.HIGHEST)
    spread[...] = exact(exact(member, inverse[...]), from_block) / cells


def pack_y_own_kernel(place, right, scale, first, second):
    ext_x, ext_y, depth = right.shape
    even = is_even(place, IY)
    base = (ext_x + 2 * OV) * OV
    for x in range(ext_x):
        low, high = right[x, 0:OV], right[x, ext_y - OV : ext_y]
        at = (x + OV) * OV
        first[at : at + OV] = jnp.where(even, high, low)
        second[at : at + OV] = jnp.where(even, low, high)
        low, high = scale[x, 0:16].astype(F32)[0:1], scale[x, ext_y - 16 : ext_y].astype(F32)[15:16]
        first[base + x : base + x + 1] = jnp.where(even, high, low)
        second[base + x : base + x + 1] = jnp.where(even, low, high)


def pack_y_rest_kernel(sizes, sides, wide_x, place, x_first, x_second, *refs):
    rims, (first, second) = refs[:sides], refs[sides + 2 :]
    ext_y = x_first.shape[1]
    even = is_even(place, IY)
    x_low, x_high = from_ends(place, IX, sizes, x_first, x_second)
    last = (wide_x - 2 * OV) * OV
    groups = (wide_x + GROUP - 1) // GROUP
    for side in range(sides):
        for group in range(groups):
            start = group * ext_y
            low, high = rims[side][start : start + OV], rims[side][start + ext_y - OV : start + ext_y]
            at = wide_x * OV + wide_x - 2 * OV + (side * groups + group) * OV
            first[at : at + OV] = jnp.where(even, high, low)
            second[at : at + OV] = jnp.where(even, low, high)
    for t in range(OV):
        for source, at in ((x_low, t * OV), (x_high, last + OV * OV + t * OV)):
            low, high = source((t, slice(0, OV))), source((t, slice(ext_y - OV, ext_y)))
            first[at : at + OV] = jnp.where(even, high, low)
            second[at : at + OV] = jnp.where(even, low, high)


def pack_z_kernel(planes, faces, sides, place, *refs):
    if faces:
        right, scale, *messages = refs
        sources = {a + OV: right.at[a] for a in range(right.shape[0])}
        ext_x, ext_y, depth = right.shape
    else:
        x_first, x_second, *messages = refs
        messages = messages[sides:]
        low, high = from_ends(place, IX, planes, x_first, x_second)
        ext_y, depth = x_first.shape[1:]
        ext_x = messages[0].shape[0] // ext_y * GROUP - 2 * OV
        ext_x = ext_x // GROUP * GROUP
        sources = {}
    lane = iota((ext_y, LANES), 1)
    for side in range(sides):
        is_high = place[SIDE + 2 * side] > 0
        start, face = jnp.where(is_high, depth - OV, 0), jnp.where(is_high, depth - 1, 0)
        for group in range(messages[side].shape[0] // ext_y):
            at = slice(group * ext_y, (group + 1) * ext_y)
            total = jnp.zeros((ext_y, LANES), F32) if faces else messages[side][at]
            for q in range(GROUP):
                a = group * GROUP + q
                if faces and a in sources:
                    cells = sources[a][...]
                elif not faces and a < OV:
                    cells = low(a)
                elif not faces and ext_x + OV <= a < ext_x + 2 * OV:
                    cells = high(a - OV - ext_x)
                else:
                    cells = None
                if cells is not None:
                    moved = pltpu.roll(cells, lax.rem(SLOT * q + depth - start, depth), 1)
                    total = jnp.where((lane >= SLOT * q) & (lane < SLOT * q + OV), moved, total)
                if faces and a < ext_x:
                    moved = pltpu.roll(scale[a].astype(F32), lax.rem(SLOT * q + OV + depth - face, depth), 1)
                    total = jnp.where(lane == SLOT * q + OV, moved, total)
            messages[side][at] = total


def rim_columns(place, sides, values, q):
    lane = iota(values[0].shape, 1)
    piece = jnp.zeros(values[0].shape, F32)
    for side in range(sides):
        value = jnp.where((lane // SLOT == q) & (place[SIDE + 2 * side + 1] > 0), values[side], 0.0)
        high = value.astype(BF16).astype(F32)
        at = LANES - SLOT * q + 3 * SLOT * side
        for number, part in enumerate((high, value - high, high)):
            shift = (at + number * SLOT) % LANES
            piece = piece + (pltpu.roll(part, shift, 1) if shift else part)
    return piece.astype(BF16)


def z_forward(cells, rims, wz):
    high, low = halves(cells)
    return dot(jnp.concatenate([high, low, high, rims], axis=1), wz[...])


def along(matrix, pair):
    value = jnp.concatenate(pair, axis=1)
    high = value.astype(BF16).astype(F32)
    stack = jnp.concatenate([high, value - high, high], axis=0).astype(BF16)
    return dot(matrix[...], stack)[0 : value.shape[0]]


def strided(pair, at, count, stride):
    return [ref[pl.ds(at, count, stride=stride), :] for ref in pair]


def solve_own_kernel(sizes, sides, place, right, x_first, x_second, *refs):
    received, (fx, wz, out_a, out_b, first_a, first_b) = refs[:sides], refs[sides:]
    ext_x, ext_y, depth = right.shape
    wide = ext_x + 2 * OV
    low, high = from_ends(place, IX, sizes, x_first, x_second)
    batch = 8
    for start in range(0, wide, batch):
        cells, rims = [], []
        for a in range(start, start + batch):
            if a < OV:
                cells.append(low(a))
            elif a < ext_x + OV:
                cells.append(right[a - OV])
            else:
                cells.append(high(a - OV - ext_x))
            at = slice(a // GROUP * ext_y, (a // GROUP + 1) * ext_y)
            rims.append(rim_columns(place, sides, [ref[at] for ref in received], a % GROUP))
        out = z_forward(jnp.concatenate(cells, axis=0), jnp.concatenate(rims, axis=0), wz)
        block = pl.ds(start * ext_y, batch * ext_y)
        first_a[block] = out[:, 0:LANES]
        first_b[block] = out[:, LANES:]
    for y in range(ext_y):
        out = along(fx, strided((first_a, first_b), y, wide, ext_y))
        out_a[y * wide : (y + 1) * wide] = out[:, 0:LANES]
        out_b[y * wide : (y + 1) * wide] = out[:, LANES:]


def solve_rest_kernel(sizes, sides, place, axes, x_values, scale, y_first, y_second, own_a, own_b, *refs):
    fx, bx, fy, by, wz, bz, den, back_a, back_b, first, second = refs[:11]
    edge_a, edge_b, halo_a, halo_b, mode_a, mode_b = refs[11:]
    wide = x_values.shape[1]
    rows = back_a.shape[0]
    wide_y = rows // wide
    ext_y = wide_y - 2 * OV
    groups = (wide + GROUP - 1) // GROUP
    low, high = from_ends(place, IY, sizes, y_first, y_second)
    both = []
    for side in range(sides):
        values = []
        for group in range(groups):
            at = wide * OV + wide - 2 * OV + (side * groups + group) * OV
            values.append(jnp.concatenate([high(slice(at, at + OV)), low(slice(at, at + OV))], axis=0))
        both.append(values)
    cells, rims = [], []
    for a in range(wide):
        part = slice(a * OV, (a + 1) * OV)
        cells.append(jnp.concatenate([high(part), low(part)], axis=0))
        rims.append(rim_columns(place, sides, [values[a // GROUP] for values in both], a % GROUP))
    out = z_forward(jnp.concatenate(cells, axis=0), jnp.concatenate(rims, axis=0), wz)
    edge_a[...] = out[:, 0:LANES]
    edge_b[...] = out[:, LANES:]
    for t in range(2 * OV):
        out = along(fx, strided((edge_a, edge_b), t, wide, 2 * OV))
        halo_a[t * wide : (t + 1) * wide] = out[:, 0:LANES]
        halo_b[t * wide : (t + 1) * wide] = out[:, LANES:]
    for i in range(wide):
        pair = []
        for inside, outside in ((own_a, halo_a), (own_b, halo_b)):
            parts = strided((inside,), i, ext_y, wide) + strided((outside,), i, 2 * OV, wide)
            pair.append(jnp.concatenate(parts, axis=0))
        out = along(fy, pair)
        inverse = 1.0 / (axes[:, 0:1] * x_values[:, i : i + 1] + den[...])
        out = along(by, [out[:, 0:LANES] * inverse, out[:, LANES:] * inverse])
        mode_a[pl.ds(i * wide_y, wide_y)] = out[:, 0:LANES]
        mode_b[pl.ds(i * wide_y, wide_y)] = out[:, LANES:]
    for y in range(wide_y):
        out = along(bx, strided((mode_a, mode_b), y, wide, wide_y))
        back_a[pl.ds(y, wide, stride=wide_y), :] = out[:, 0:LANES]
        back_b[pl.ds(y, wide, stride=wide_y), :] = out[:, LANES:]
    even = is_even(place, IX)
    ends = RIM * wide_y
    low, low_rims = z_back(sides, wide_y, back_a, back_b, bz, 0, RIM)
    high, high_rims = z_back(sides, wide_y, back_a, back_b, bz, wide - RIM, RIM)
    first[0:ends] = jnp.where(even, high, low)
    second[0:ends] = jnp.where(even, low, high)
    for side in range(sides):
        low = sum(low_rims[side].values())
        high = sum(high_rims[side].values())
        at = ends + side * wide_y
        first[at : at + wide_y] = jnp.where(even, high, low)
        second[at : at + wide_y] = jnp.where(even, low, high)
    low, high = scale[0].astype(F32), scale[scale.shape[0] - 1].astype(F32)
    at = ends + sides * wide_y
    first[at : at + ext_y] = jnp.where(even, high, low)
    second[at : at + ext_y] = jnp.where(even, low, high)


def z_back(sides, wide_y, back_a, back_b, bz, start, count):
    lane = iota((wide_y, LANES), 1)
    block = pl.ds(start * wide_y, count * wide_y)
    high_a, low_a = halves(back_a[block])
    high_b, low_b = halves(back_b[block])
    out = dot(jnp.concatenate([high_a, high_b, low_a, low_b, high_a, high_b], axis=1), bz[...])
    rims = [{} for _ in range(sides)]
    for a in range(start, start + count):
        group, q = a // GROUP, a % GROUP
        value = out[(a - start) * wide_y : (a - start + 1) * wide_y, LANES:]
        for side in range(sides):
            own = value if sides == 1 else jnp.where(lane // SLOT == side, value, 0.0)
            at = (SLOT * q + LANES - SLOT * side) % LANES
            moved = pltpu.roll(own, at, 1) if at else own
            rims[side][group] = rims[side][group] + moved if group in rims[side] else moved
    return out[:, 0:LANES], rims


def solve_tail_kernel(sides, wide, place, back_a, back_b, bz, local, *rims):
    wide_y = back_a.shape[0] // wide
    for side in range(sides):
        rims[side][...] = jnp.zeros_like(rims[side])
    count = 10
    for start in range(OV - 1, wide - OV + 1, count):
        out, more = z_back(sides, wide_y, back_a, back_b, bz, start, count)
        at = start - OV + 1
        local[at * wide_y : (at + count) * wide_y] = out
        for side in range(sides):
            for group, value in more[side].items():
                rims[side][group * wide_y : (group + 1) * wide_y] += value


def placed_rims(place, sides, received, a, rows):
    total = None
    for side in range(sides):
        is_high, valid = place[SIDE + 2 * side] > 0, place[SIDE + 2 * side + 1] > 0
        start = jnp.where(is_high, LANES - OV, 0)
        shift = lax.rem(jnp.where(is_high, LANES - OV, LANES - 1) + LANES - SLOT * (a % GROUP), LANES)
        value = received[side][rows]
        lane = iota(value.shape, 1)
        value = jnp.where((lane >= start) & (lane < start + OV) & valid, pltpu.roll(value, shift, 1), 0.0)
        total = value if total is None else total + value
    return total


def pack_back_z_kernel(sizes, sides, wide, wide_y, place, x_first, x_second, *refs):
    own, out = refs[:sides], refs[sides:]
    _, faces = x_received(sizes, wide, wide_y, place, x_first, x_second)
    for side in range(sides):
        for group in range((wide + GROUP - 1) // GROUP):
            part = slice(group * wide_y, (group + 1) * wide_y)
            more = faces(side, group, slice(0, wide_y))
            out[side][part] = own[side][part] if more is None else own[side][part] + more


def fold_x_kernel(sizes, wide, wide_y, place, x_first, x_second, local, out):
    plane, _ = x_received(sizes, wide, wide_y, place, x_first, x_second)
    for p in range(wide - 2 * OV + 2):
        part = slice(p * wide_y, (p + 1) * wide_y)
        more = plane(p + OV - 1, slice(0, wide_y))
        out[part] = local[part] if more is None else local[part] + more


def pack_back_y_kernel(sides, wide, wide_y, place, field, *refs):
    own, received = refs[:sides], refs[sides : 2 * sides]
    faces, (first, second) = refs[2 * sides : 3 * sides], refs[3 * sides :]
    groups = (wide + GROUP - 1) // GROUP
    planes = wide - 2 * OV + 2
    even = is_even(place, IY)

    def put(at, low, high):
        first[at : at + RIM] = jnp.where(even, high, low)
        second[at : at + RIM] = jnp.where(even, low, high)

    lane = iota((groups * wide_y, LANES), 1)
    for side in range(sides):
        is_high, valid = place[SIDE + 2 * side] > 0, place[SIDE + 2 * side + 1] > 0
        other = pltpu.roll(received[side][...], jnp.where(is_high, LANES - OV, 0), 1)
        mine = pltpu.roll(own[side][...], jnp.where(is_high, LANES - 1, LANES - OV + 1), 1)
        faces[side][...] = jnp.where((lax.rem(lane, SLOT) == 0) & valid, other + mine, 0.0)
        for group in range(groups):
            low = faces[side][group * wide_y : group * wide_y + 8]
            high = faces[side][(group + 1) * wide_y - 8 : (group + 1) * wide_y]
            put(planes * RIM + (side * groups + group) * RIM, low[0:RIM], high[8 - RIM :])
    for p in range(planes):
        a = p + OV - 1
        ends = []
        for start in (0, wide_y - 8):
            at = a // GROUP * wide_y + start
            value = placed_rims(place, sides, received, a, slice(at, at + 8))
            ends.append(field[p * wide_y + start : p * wide_y + start + 8] + value)
        put(p * RIM, ends[0][0:RIM], ends[1][8 - RIM :])


def x_received(sizes, wide, wide_y, place, x_first, x_second):
    low, high = from_ends(place, IX, sizes, x_first, x_second)
    high_lane = (wide - 2 * OV) % GROUP * SLOT

    def plane(a, rows):
        if OV - 1 <= a < OV - 1 + RIM:
            at, source = (a - OV + 1) * wide_y, low
        elif wide - 2 * OV <= a < wide - 2 * OV + RIM:
            at, source = (a - wide + 2 * OV) * wide_y, high
        else:
            return None
        return source(slice(at + rows.start, at + rows.stop))

    def faces(side, group, rows):
        lane = iota((rows.stop - rows.start, LANES), 1)
        at = (RIM + side) * wide_y
        rows = slice(at + rows.start, at + rows.stop)
        if group == 0:
            return jnp.where((lane >= (OV - 1) * SLOT) & (lane < 2 * OV * SLOT), low(rows), 0.0)
        if group == (wide + GROUP - 1) // GROUP - 1:
            return jnp.where((lane >= high_lane) & (lane < high_lane + RIM * SLOT), high(rows), 0.0)
        return None

    return plane, faces


def weights_kernel(sizes, sides, place, axes, right, scale, x_first, x_second, y_first, y_second, *refs):
    scale_faces = refs[:sides]
    wx, wy, wz, z_weight, sums, scales = refs[sides:]
    ext_x, ext_y, depth = right.shape
    core = slice(8, 8 + ext_y)
    x_low, x_high = from_ends(place, IX, sizes, x_first, x_second)
    y_low, y_high = from_ends(place, IY, sizes, y_first, y_second)
    y_rows = (ext_x + 2 * OV) * OV
    x_rows = slice(x_first.shape[0] - ext_y, x_first.shape[0])
    scales[0, core] = x_low(x_rows)
    scales[ext_x + 1, core] = x_high(x_rows)
    for x in range(ext_x):
        scales[x + 1, core] = scale[x].astype(F32)
        part = slice(y_rows + x, y_rows + x + 1)
        scales[x + 1, 7:8] = y_low(part)
        scales[x + 1, 8 + ext_y : 9 + ext_y] = y_high(part)
    hx, hy, hz = (0.5 * axes[:, d : d + 1] for d in range(3))
    lane = iota((8, depth), 1)
    ends = (lane == 0) | (lane == depth - 1)
    zero = jnp.zeros((8, depth), F32)
    sum_right, sum_z = zero, zero
    for x in range(ext_x + 1):
        wx[x] = hx * (scales[x, core] + scales[x + 1, core])
    for x in range(ext_x):
        wy[x, 0 : ext_y + 1] = hy * (scales[x + 1, 7 : 8 + ext_y] + scales[x + 1, 8 : 9 + ext_y])
        for row in range(0, ext_y, 8):
            own = scales[x + 1, 8 + row : 16 + row]
            edge = zero
            for side in range(sides):
                is_high, valid = place[SIDE + 2 * side] > 0, place[SIDE + 2 * side + 1] > 0
                target = jnp.where(is_high, depth - 1, 0)
                at = x // GROUP * ext_y + row
                shift = lax.rem(target + depth - (x % GROUP * SLOT + OV), depth)
                edge = jnp.where((lane == target) & valid, pltpu.roll(scale_faces[side][at : at + 8], shift, 1), edge)
            wz[x, row : row + 8] = hz * (own + jnp.where(lane == 0, edge, pltpu.roll(own, 1, 1)))
            end_weight = jnp.where(ends, hz * (own + edge), 0.0)
            z_weight[x, row : row + 8] = end_weight
            sum_z = sum_z + end_weight
            sum_right = sum_right + right[x, row : row + 8]

    def whole(value):
        return jnp.sum(jnp.sum(value, axis=0, keepdims=True), axis=1, keepdims=True)

    def y_sum(row):
        total = jnp.zeros((1, depth), F32)
        for x in range(ext_x):
            total = total + wy[x, row : row + 1]
        return whole(total)

    x_high_sum, y_high_sum = whole(wx[ext_x]), y_sum(ext_y)
    z_high_sum = whole(jnp.where(lane == depth - 1, sum_z, 0.0))
    faces_sum = whole(wx[0]) + x_high_sum + y_sum(0) + y_high_sum + whole(sum_z)
    columns = {
        0: whole(sum_right),
        4: faces_sum,
        5: jnp.where(place[IX] < sizes["gx"] - 1, x_high_sum, 0.0),
        6: jnp.where(place[IY] < sizes["gy"] - 1, y_high_sum, 0.0),
        7: jnp.where(place[IZ] < sizes["gz"] - 1, z_high_sum, 0.0),
    }
    sums[...] = in_columns(columns, jnp.zeros((1, LANES), F32))


def in_columns(columns, row):
    at = iota((1, LANES), 1)
    for number, value in columns.items():
        row = jnp.where(at == number, value, row)
    return row


def operator_tile(place, sides, groups, values, edges, wx, wy, wz, z_weight, block, inner, row):
    depth = values.shape[2]
    ext_y = z_weight.shape[1]
    lane = iota((8, depth), 1)
    at = slice(8 + row, 16 + row)
    x = block * GROUP + inner
    mid = values[x + 1, at]
    total = wx[x, row : row + 8] * (mid - values[x, at]) + wx[x + 1, row : row + 8] * (mid - values[x + 2, at])
    total = total + wy[x, row : row + 8] * (mid - values[x + 1, 7 + row : 15 + row])
    total = total + wy[x, row + 1 : row + 9] * (mid - values[x + 1, 9 + row : 17 + row])
    edge = jnp.zeros((8, depth), F32)
    for side in range(sides):
        is_high, valid = place[SIDE + 2 * side] > 0, place[SIDE + 2 * side + 1] > 0
        target = jnp.where(is_high, depth - 1, 0)
        start = (side * groups + block + (inner + OV) // GROUP) * ext_y + row
        moved = edges[pl.ds(pl.multiple_of(start, 8), 8)]
        q = (inner + OV) % GROUP
        if q:
            moved = pltpu.roll(moved, depth - q * SLOT, 1)
        edge = jnp.where((lane == target) & valid, moved, edge)
    flux = wz[x, row : row + 8] * (mid - jnp.where(lane == 0, edge, pltpu.roll(mid, 1, 1)))
    above = z_weight[x, row : row + 8] * (mid - edge)
    total = total + flux + jnp.where(lane == depth - 1, above, -pltpu.roll(flux, depth - 1, 1))
    return mid, total


def operator_tiles(place, sides, groups, right, values, edges, weights, applied, sums, rows):
    def several(block, totals):
        product, energy, whole = totals
        for inner in range(GROUP):
            x = block * GROUP + inner
            for row in rows:
                mid, total = operator_tile(place, sides, groups, values, edges, *weights, block, inner, row)
                applied[x, row : row + 8] = total
                product = product + right[x, row : row + 8] * mid
                energy = energy + mid * total
                whole = whole + total
        return product, energy, whole

    totals = lax.fori_loop(0, right.shape[0] // GROUP, several, (jnp.zeros((8, values.shape[2]), F32),) * 3)
    for number, value in enumerate(totals):
        sums[number * 8 : (number + 1) * 8] = value


def to_face(place, side, value):
    return pltpu.roll(value, jnp.where(place[SIDE + 2 * side] > 0, LANES - 1, 0), 1)


def inner_kernel(sizes, sides, wide, place, right, field, *refs):
    received, faces, weights = refs[:sides], refs[sides : 2 * sides], refs[2 * sides : 2 * sides + 4]
    values, edges, applied, sums = refs[2 * sides + 4 :]
    ext_x, ext_y, depth = right.shape
    wide_y = ext_y + 2 * OV
    groups = (wide + GROUP - 1) // GROUP
    inside_low, inside_high = place[IX] > 0, place[IX] < sizes["gx"] - 1
    for p in range(ext_x + 2):
        a = p + OV - 1
        at = a // GROUP * wide_y
        value = placed_rims(place, sides, received, a, slice(at, at + wide_y))
        value = value + field[p * wide_y : (p + 1) * wide_y]
        if p == 0:
            value = jnp.where(inside_low, value, 0.0)
        if p == ext_x + 1:
            value = jnp.where(inside_high, value, 0.0)
        values[p, 8 - OV : 8 - OV + wide_y] = value
    for side in range(sides):
        for group in range(groups):
            value = faces[side][group * wide_y : (group + 1) * wide_y]
            at = (side * groups + group) * ext_y
            edges[at : at + ext_y] = to_face(place, side, value)[OV : OV + ext_y]
    operator_tiles(place, sides, groups, right, values, edges, weights, applied, sums, range(8, ext_y - 8, 8))


def outer_kernel(sizes, sides, wide, place, right, y_first, y_second, *refs):
    weights, fixed, refs = refs[:4], refs[4], refs[5:]
    inner_sums, refs = refs[3], refs[4:]
    values, edges, applied, out, sums = refs
    ext_x, ext_y, depth = right.shape
    wide_y = ext_y + 2 * OV
    groups = (wide + GROUP - 1) // GROUP
    low, high = from_ends(place, IY, sizes, y_first, y_second)
    inside_low, inside_high = place[IY] > 0, place[IY] < sizes["gy"] - 1
    for p in range(ext_x + 2):
        part = slice(p * RIM, (p + 1) * RIM)
        low_rows, high_rows = low(part), high(part)
        if p == 0 or p == ext_x + 1:
            inside = place[IX] > 0 if p == 0 else place[IX] < sizes["gx"] - 1
            low_rows, high_rows = (jnp.where(inside, rows, 0.0) for rows in (low_rows, high_rows))
        values[p, 7 : 7 + RIM] += low_rows
        values[p, 4 + ext_y : 4 + ext_y + RIM] += high_rows
        values[p, 7:8] = jnp.where(inside_low, values[p, 7:8], 0.0)
        values[p, 8 + ext_y : 9 + ext_y] = jnp.where(inside_high, values[p, 8 + ext_y : 9 + ext_y], 0.0)
    for number in range(sides * groups):
        at = (ext_x + 2 + number) * RIM
        start = number * ext_y
        side = number // groups
        edges[start : start + OV] += to_face(place, side, low(slice(at, at + RIM)))[1:]
        edges[start + ext_y - OV : start + ext_y] += to_face(place, side, high(slice(at, at + RIM)))[:OV]
    operator_tiles(place, sides, groups, right, values, edges, weights, applied, sums, (0, ext_y - 8))
    columns = {}
    for number in range(3):
        part = slice(number * 8, (number + 1) * 8)
        value = inner_sums[part] + sums[part]
        columns[number + 1] = jnp.sum(jnp.sum(value, axis=0, keepdims=True), axis=1, keepdims=True)
    out[...] = jnp.broadcast_to(in_columns(columns, fixed[...]), out.shape)


def finish_kernel(sizes, place, sums, spread, values, applied, wx, wy, z_weight, right, solution, residual, held_s, held_r, sems):
    ext_x, ext_y, depth = right.shape
    nx, ny, nz = (sizes[a] for a in MESH_AXES)
    count = nx * ny * nz
    table = sums[...]
    part = [table[:, k : k + 1] for k in range(8)]
    from_device = iota((count, count), 0) == iota((count, count), 1)
    sums_row = jnp.sum(jnp.where(from_device, part[0], 0.0), axis=0, keepdims=True)
    level = jnp.sum(spread[...] * sums_row, axis=1, keepdims=True)

    def shifted(by):
        return jnp.concatenate([level[by:], level[:by]], axis=0)

    def whole(value):
        return jnp.sum(value, axis=0, keepdims=True)

    product = whole(part[1] + level * part[0])
    neighbours = part[5] * shifted(ny * nz) + part[6] * shifted(nz) + part[7] * shifted(1)
    curvature = whole(part[2] + 2.0 * level * part[3] + level * (level * part[4] - 2.0 * neighbours))
    step = product / curvature
    device = iota((count, 1), 0)
    mine = (place[IX] * ny + place[IY]) * nz + place[IZ]

    def level_at(number, inside):
        return whole(jnp.where((device == number) & inside, level, 0.0))

    own = level_at(mine, True)
    drops = []
    for axis, stride, size in ((IX, ny * nz, nx), (IY, nz, ny), (IZ, 1, nz)):
        drops.append(step * (own - level_at(mine - stride, place[axis] > 0)))
        drops.append(step * (own - level_at(mine + stride, place[axis] < size - 1)))
    z_drop = jnp.where(iota((1, depth), 1) < depth // 2, drops[4], drops[5])
    chunk = 12
    for x in range(ext_x):
        held_s[x] = step * (values[x + 1, 8 : 8 + ext_y] + own)
        value = right[x] - step * applied[x] - z_drop * z_weight[x]
        if x == 0:
            value = value - drops[0] * wx[0]
        if x == ext_x - 1:
            value = value - drops[1] * wx[ext_x]
        held_r[x] = value
        held_r[x, 0:1] = value[0:1] - drops[2] * wy[x, 0:1]
        held_r[x, ext_y - 1 : ext_y] = value[ext_y - 1 : ext_y] - drops[3] * wy[x, ext_y : ext_y + 1]
        if (x + 1) % chunk == 0:
            part_x = pl.ds(x + 1 - chunk, chunk)
            number = (x + 1) // chunk - 1
            pltpu.make_async_copy(held_s.at[part_x], solution.at[part_x], sems.at[0, number]).start()
            pltpu.make_async_copy(held_r.at[part_x], residual.at[part_x], sems.at[1, number]).start()
    for number in range(ext_x // chunk):
        part_x = pl.ds(number * chunk, chunk)
        pltpu.make_async_copy(held_s.at[part_x], solution.at[part_x], sems.at[0, number]).wait()
        pltpu.make_async_copy(held_r.at[part_x], residual.at[part_x], sems.at[1, number]).wait()


def body(sizes, right, scale, axes, xv, yv, zv, x_values, y_values, z_values, inverse):
    ext_x, ext_y, depth = right.shape
    wide_x, wide_y = xv.shape[0], yv.shape[0]
    sides = 1 if sizes["gz"] == 2 else 2
    groups = (wide_x + GROUP - 1) // GROUP
    count = sizes["gx"] * sizes["gy"] * sizes["gz"]
    bind = functools.partial
    run = bind(call, sizes)
    block = shape(right.shape)
    axes_row = axes.reshape(1, -1)
    beside = 2 * 10**9

    up = lax.rem(lax.axis_index("gx"), 2) == 0
    starts = jnp.where(up, ext_x - OV, 0), jnp.where(up, 0, ext_x - OV)
    xs = [lax.dynamic_slice_in_dim(right, start, OV, 0) for start in starts]
    xs = swap_ends(*xs, "gx", sizes)

    rim_message = [shape([groups * ext_y, LANES])] * sides
    rims = run(
        bind(pack_z_kernel, None, True, sides),
        "pack_z_own",
        rim_message,
        [right, scale],
        [VMEM] * 2,
        flops=beside,
    )
    y_message = [shape([wide_x * OV + ext_x + sides * groups * OV, depth])] * 2
    ys = run(pack_y_own_kernel, "pack_y_own", y_message, [right, scale], [VMEM] * 2, flops=beside)
    rims, ys = lax.optimization_barrier((rims, ys))
    rims = run(
        bind(pack_z_kernel, sizes, False, sides),
        "pack_z_rest",
        rim_message,
        [*xs, *rims],
        [VMEM] * (2 + sides),
        aliases={2 + k: k for k in range(sides)},
    )
    rims, late_zv = lax.optimization_barrier((rims, zv))
    rims = swap_sides(rims, sizes)
    thin = [shape([LANES // 2, 3 * size], BF16) for size in (wide_x, wide_x, wide_y, wide_y)]
    *mats, spread = run(
        bind(prepare_kernel, sides, 2.0 * ext_x * ext_y * depth),
        "prepare",
        thin + [shape([4 * depth, 2 * LANES], BF16), shape([6 * LANES, 2 * LANES], BF16), shape([wide_y, LANES]), shape([count, count])],
        [axes_row, xv, yv, late_zv, y_values.reshape(1, -1), z_values.reshape(1, -1), inverse],
        [VMEM] * 7,
        [pltpu.VMEM((LANES, LANES), F32), pltpu.VMEM((depth + 2 * OV, 2 * LANES), F32), pltpu.VMEM((LANES, 2 * LANES), F32)],
        flops=beside,
    )

    ys = run(
        bind(pack_y_rest_kernel, sizes, sides, wide_x),
        "pack_y_rest",
        y_message,
        [*xs, *rims, *ys],
        [VMEM] * (4 + sides),
        aliases={2 + sides: 0, 3 + sides: 1},
    )
    ys = swap_ends(*ys, "gy", sizes)

    fx, _, _, _, wz, _, _ = mats
    tall = pltpu.VMEM((wide_x * wide_y, LANES), F32)
    core = pltpu.VMEM((wide_x * ext_y, LANES), F32)
    owns = run(
        bind(solve_own_kernel, sizes, sides),
        "solve_own",
        [shape([wide_x * ext_y, LANES])] * 2,
        [right, *xs, *rims, fx, wz],
        [VMEM] * (5 + sides),
        [core] * 2,
        limit=16,
        flops=2 * beside,
    )
    field = shape([wide_x * wide_y, depth])
    rim_message = shape([groups * wide_y, LANES])
    edge = pltpu.VMEM((wide_x * 2 * OV, LANES), F32)
    *back, low, high = run(
        bind(solve_rest_kernel, sizes, sides),
        "solve_rest",
        [field] * 2 + [shape([(RIM + sides) * wide_y + ext_y, depth])] * 2,
        [axes_row, x_values.reshape(1, -1), scale, *ys, *owns, *mats],
        [VMEM] * (7 + len(mats)),
        [edge] * 4 + [tall] * 2,
        limit=20,
    )
    back_xs = swap_ends(low, high, "gx", sizes)

    planes = ext_x + 2
    field = shape([planes * wide_y, depth])
    local, *own_rims = run(
        bind(solve_tail_kernel, sides, wide_x),
        "solve_tail",
        [field] + [rim_message] * sides,
        [*back, mats[5]],
        [VMEM] * 3,
        flops=beside,
    )
    own_rims = run(
        bind(pack_back_z_kernel, sizes, sides, wide_x, wide_y),
        "pack_back_z",
        [rim_message] * sides,
        [*back_xs, *own_rims],
        [VMEM] * (2 + sides),
    )
    late_rims, own_rims = lax.optimization_barrier((rims, own_rims))
    other_rims = swap_sides(own_rims, sizes)
    field_x = run(
        bind(fold_x_kernel, sizes, wide_x, wide_y),
        "fold_x",
        [field],
        [*back_xs, local],
        [VMEM] * 3,
        flops=beside,
    )[0]
    scale_block = pltpu.VMEM((planes, ext_y + 16, depth), F32)
    *weights, fixed = run(
        bind(weights_kernel, sizes, sides),
        "weights",
        [shape([ext_x + 1, ext_y, depth]), shape([ext_x, ext_y + 8, depth]), block, block, shape([1, LANES])],
        [axes_row, right, scale, *back_xs, *ys, *late_rims],
        [VMEM] * (7 + sides),
        [scale_block],
        flops=beside,
    )
    *faces, low, high = run(
        bind(pack_back_y_kernel, sides, wide_x, wide_y),
        "pack_back_y",
        [rim_message] * sides + [shape([(planes + groups * sides) * RIM, depth])] * 2,
        [field_x, *own_rims, *other_rims],
        [VMEM] * (1 + 2 * sides),
    )
    back_ys = swap_ends(low, high, "gy", sizes)

    parts = [shape([planes, ext_y + 16, depth]), shape([sides * groups * ext_y, LANES]), block]
    inner = run(
        bind(inner_kernel, sizes, sides, wide_x),
        "inner",
        parts + [shape([24, depth])],
        [right, field_x, *other_rims, *faces, *weights],
        [VMEM] * (6 + 2 * sides),
        flops=beside,
    )
    values, edges, applied, sums = run(
        bind(outer_kernel, sizes, sides, wide_x),
        "outer",
        parts + [shape([count, LANES])],
        [right, *back_ys, *weights, fixed, *inner],
        [VMEM] * 12,
        [pltpu.VMEM((24, depth), F32)],
        aliases={8: 0, 9: 1, 10: 2},
    )
    sums = lax.all_to_all(sums, MESH_AXES, 0, 0, tiled=True)

    held = pltpu.VMEM(right.shape, F32)
    wx, wy, _, z_weight = weights
    return tuple(
        run(
            bind(finish_kernel, sizes),
            "finish",
            [block] * 2,
            [sums, spread, values, applied, wx, wy, z_weight, right],
            [VMEM] * 8,
            [held, held, pltpu.SemaphoreType.DMA((2, ext_x // 12))],
            out_specs=[ANY] * 2,
        )
    )


def solution(mesh):
    sizes = dict(mesh.shape)
    in_specs = (P(*MESH_AXES), P(*MESH_AXES), P(), P(), P(), P(), P(), P(), P(), P())
    out_specs = (P(*MESH_AXES), P(*MESH_AXES))
    return jax.shard_map(functools.partial(body, sizes), mesh=mesh, in_specs=in_specs, out_specs=out_specs, check_vma=False)
```

```python
import functools

import jax
import jax.numpy as jnp
from jax import lax
from jax.experimental import pallas as pl
from jax.experimental.pallas import tpu as pltpu
from jax.sharding import PartitionSpec as P

SZ = 64
OV = 4
RIM = OV + 1
LANES = 128
SLOT = 8
GROUP = LANES // SLOT
F32 = jnp.float32
BF16 = jnp.bfloat16
MESH_AXES = ("gx", "gy", "gz")

VMEM = pl.BlockSpec(memory_space=pltpu.VMEM)
ANY = pl.BlockSpec(memory_space=pl.ANY)
HBM = pl.BlockSpec(memory_space=pltpu.HBM)


def call(sizes, kernel, name, outs, args, spaces, scratch=(), limit=8, out_specs=None, aliases=None, flops=0):
    size = sum(o.size * o.dtype.itemsize for o in outs) + sum(a.size * a.dtype.itemsize for a in args)

    def placed(*refs):
        return kernel(place_values(sizes), *refs)

    return pl.pallas_call(
        placed,
        out_shape=outs,
        in_specs=spaces,
        out_specs=out_specs or [VMEM] * len(outs),
        scratch_shapes=list(scratch),
        input_output_aliases=aliases or {},
        name=name,
        compiler_params=pltpu.CompilerParams(vmem_limit_bytes=limit * 2**20),
        cost_estimate=pl.CostEstimate(flops=flops, bytes_accessed=size, transcendentals=0),
    )(*args)


def shape(dims, dtype=F32):
    return jax.ShapeDtypeStruct(tuple(dims), dtype)


def halves(value):
    high = value.astype(BF16)
    return high, (value - high.astype(F32)).astype(BF16)


def dot(left, right):
    return jnp.dot(left, right, preferred_element_type=F32)


def iota(dims, axis):
    return lax.broadcasted_iota(jnp.int32, dims, axis)


IX, IY, IZ, SIDE = 0, 1, 2, 3


def place_values(sizes):
    ix, iy, iz = (lax.axis_index(a) for a in MESH_AXES)
    nz = sizes["gz"]
    if nz == 2:
        sides = [1 - iz, 1]
    else:
        sides = [1, jnp.where(iz < nz - 1, 1, 0), 0, jnp.where(iz > 0, 1, 0)]
    return [ix, iy, iz] + sides


def swap_sides(messages, sizes):
    count = sizes["gz"]
    if count == 2:
        return [lax.ppermute(messages[0], "gz", [(0, 1), (1, 0)])]
    up = [(i, (i + 1) % count) for i in range(count)]
    down = [((i + 1) % count, i) for i in range(count)]
    return [lax.ppermute(messages[1], "gz", down), lax.ppermute(messages[0], "gz", up)]


def swap_ends(first, second, axis, sizes):
    count = sizes[axis]
    received = []
    for message, start in ((first, 0), (second, 1)):
        partner = list(range(count))
        for i in range(start, count - 1, 2):
            partner[i], partner[i + 1] = i + 1, i
        received.append(lax.ppermute(message, axis, list(enumerate(partner))))
    return received


def is_even(place, axis):
    return lax.rem(place[axis], 2) == 0


def from_ends(place, axis, sizes, first, second):
    even = is_even(place, axis)
    inside_low = place[axis] > 0
    inside_high = place[axis] < sizes[MESH_AXES[axis]] - 1

    def low(at):
        return jnp.where(inside_low, jnp.where(even, second[at], first[at]), 0.0)

    def high(at):
        return jnp.where(inside_high, jnp.where(even, first[at], second[at]), 0.0)

    return low, high


def prepare_kernel(sides, cells, place, axes, xv, yv, zv, y_row, z_row, inverse, fx, bx, fy, by, wz, bz, den, spread, pad, wide, rows):
    ez = zv.shape[0]
    depth = wz.shape[0] // 4

    def stacked(value, out):
        size = out.shape[1] // 3
        high, low = (part.astype(F32) for part in halves(value[: LANES // 2]))
        spread = jnp.concatenate([high, jnp.zeros_like(high)], axis=1)
        wide_low = jnp.concatenate([low, jnp.zeros_like(low)], axis=1)
        out[...] = (spread + pltpu.roll(spread, size, 1) + pltpu.roll(wide_low, 2 * size, 1)).astype(BF16)[:, : 3 * size]

    for vectors, forward, back in ((xv, fx, bx), (yv, fy, by)):
        size = vectors.shape[0]
        pad[...] = jnp.zeros_like(pad)
        pad[0:size, 0:size] = vectors[...]
        stacked(pad[...], back)
        if vectors is yv:
            pad[0 : size - OV, 0:size] = vectors[OV:size]
            pad[size - OV : size, 0:size] = vectors[0:OV]
        stacked(pad[...].T, forward)

    wide[...] = jnp.zeros_like(wide)
    wide[0:ez, 0:ez] = zv[...]
    wide[SZ : SZ + ez, LANES : LANES + ez] = zv[...]
    middle = wide[OV : OV + depth]
    high, low = halves(middle)
    wz[0:depth] = high
    wz[depth : 2 * depth] = high
    wz[2 * depth : 3 * depth] = low
    rows[...] = jnp.zeros_like(rows)
    for side in range(sides):
        is_high = place[SIDE + 2 * side] > 0
        for k in range(OV):
            top, bottom = OV + depth + k, k
            row = jnp.where(is_high, wide[top : top + 1], wide[bottom : bottom + 1])
            row_high, row_low = halves(row)
            at = 3 * SLOT * side + k
            rows[at : at + 1] = row_high.astype(F32)
            rows[at + SLOT : at + SLOT + 1] = row_high.astype(F32)
            rows[at + 2 * SLOT : at + 2 * SLOT + 1] = row_low.astype(F32)
    wz[3 * depth :] = rows[...].astype(BF16)

    rows[...] = jnp.zeros_like(rows)
    for side in range(sides):
        is_high = place[SIDE + 2 * side] > 0
        for k in range(RIM):
            top, bottom = OV + depth - 1 + k, k
            rows[SLOT * side + k : SLOT * side + k + 1] = jnp.where(is_high, wide[top : top + 1], wide[bottom : bottom + 1])
    across = 2 * LANES
    for at, part in ((0, middle), (LANES, rows[...])):
        turned = jnp.concatenate([part[:, 0:LANES].T, part[:, LANES:].T], axis=0)
        high, low = halves(turned)
        bz[0:across, at : at + LANES] = high
        bz[across : 2 * across, at : at + LANES] = high
        bz[2 * across :, at : at + LANES] = low

    ey = yv.shape[0]
    diagonal = iota((ey, ey), 0) == iota((ey, ey), 1)
    y_column = jnp.sum(jnp.where(diagonal, y_row[...], 0.0), axis=1, keepdims=True)
    pad[...] = jnp.ones_like(pad)
    pad[0:1, 0:ez] = axes[:, 2:3] * z_row[...]
    den[...] = axes[:, 1:2] * y_column + pad[0:1]
    count, blocks = spread.shape[0], inverse.shape[0]
    member = jnp.where(iota((count, blocks), 0) // 2 == iota((count, blocks), 1), 1.0, 0.0)
    from_block = jnp.where(iota((blocks, count), 0) == iota((blocks, count), 1) // 2, 1.0, 0.0)
    exact = functools.partial(jnp.dot, preferred_element_type=F32, precision=lax.Precision.HIGHEST)
    spread[...] = exact(exact(member, inverse[...]), from_block) / cells


def pack_y_own_kernel(place, right, scale, first, second):
    ext_x, ext_y, depth = right.shape
    even = is_even(place, IY)
    base = (ext_x + 2 * OV) * OV
    for x in range(ext_x):
        low, high = right[x, 0:OV], right[x, ext_y - OV : ext_y]
        at = (x + OV) * OV
        first[at : at + OV] = jnp.where(even, high, low)
        second[at : at + OV] = jnp.where(even, low, high)
        low, high = scale[x, 0:16].astype(F32)[0:1], scale[x, ext_y - 16 : ext_y].astype(F32)[15:16]
        first[base + x : base + x + 1] = jnp.where(even, high, low)
        second[base + x : base + x + 1] = jnp.where(even, low, high)


def pack_y_rest_kernel(sizes, sides, wide_x, place, x_first, x_second, *refs):
    rims, (first, second) = refs[:sides], refs[sides + 2 :]
    ext_y = x_first.shape[1]
    even = is_even(place, IY)
    x_low, x_high = from_ends(place, IX, sizes, x_first, x_second)
    last = (wide_x - 2 * OV) * OV
    groups = (wide_x + GROUP - 1) // GROUP
    for side in range(sides):
        for group in range(groups):
            start = group * ext_y
            low, high = rims[side][start : start + OV], rims[side][start + ext_y - OV : start + ext_y]
            at = wide_x * OV + wide_x - 2 * OV + (side * groups + group) * OV
            first[at : at + OV] = jnp.where(even, high, low)
            second[at : at + OV] = jnp.where(even, low, high)
    for t in range(OV):
        for source, at in ((x_low, t * OV), (x_high, last + OV * OV + t * OV)):
            low, high = source((t, slice(0, OV))), source((t, slice(ext_y - OV, ext_y)))
            first[at : at + OV] = jnp.where(even, high, low)
            second[at : at + OV] = jnp.where(even, low, high)


def pack_z_kernel(planes, faces, sides, place, *refs):
    if faces:
        right, scale, *messages = refs
        sources = {a + OV: right.at[a] for a in range(right.shape[0])}
        ext_x, ext_y, depth = right.shape
    else:
        x_first, x_second, *messages = refs
        messages = messages[sides:]
        low, high = from_ends(place, IX, planes, x_first, x_second)
        ext_y, depth = x_first.shape[1:]
        ext_x = messages[0].shape[0] // ext_y * GROUP - 2 * OV
        ext_x = ext_x // GROUP * GROUP
        sources = {}
    lane = iota((ext_y, LANES), 1)
    for side in range(sides):
        is_high = place[SIDE + 2 * side] > 0
        start, face = jnp.where(is_high, depth - OV, 0), jnp.where(is_high, depth - 1, 0)
        for group in range(messages[side].shape[0] // ext_y):
            at = slice(group * ext_y, (group + 1) * ext_y)
            total = jnp.zeros((ext_y, LANES), F32) if faces else messages[side][at]
            for q in range(GROUP):
                a = group * GROUP + q
                if faces and a in sources:
                    cells = sources[a][...]
                elif not faces and a < OV:
                    cells = low(a)
                elif not faces and ext_x + OV <= a < ext_x + 2 * OV:
                    cells = high(a - OV - ext_x)
                else:
                    cells = None
                if cells is not None:
                    moved = pltpu.roll(cells, lax.rem(SLOT * q + depth - start, depth), 1)
                    total = jnp.where((lane >= SLOT * q) & (lane < SLOT * q + OV), moved, total)
                if faces and a < ext_x:
                    moved = pltpu.roll(scale[a].astype(F32), lax.rem(SLOT * q + OV + depth - face, depth), 1)
                    total = jnp.where(lane == SLOT * q + OV, moved, total)
            messages[side][at] = total


def rim_columns(place, sides, values, q):
    lane = iota(values[0].shape, 1)
    piece = jnp.zeros(values[0].shape, F32)
    for side in range(sides):
        value = jnp.where((lane // SLOT == q) & (place[SIDE + 2 * side + 1] > 0), values[side], 0.0)
        high = value.astype(BF16).astype(F32)
        at = LANES - SLOT * q + 3 * SLOT * side
        for number, part in enumerate((high, value - high, high)):
            shift = (at + number * SLOT) % LANES
            piece = piece + (pltpu.roll(part, shift, 1) if shift else part)
    return piece.astype(BF16)


def z_forward(cells, rims, wz):
    high, low = halves(cells)
    return dot(jnp.concatenate([high, low, high, rims], axis=1), wz[...])


def along(matrix, pair):
    value = jnp.concatenate(pair, axis=1)
    high = value.astype(BF16).astype(F32)
    stack = jnp.concatenate([high, value - high, high], axis=0).astype(BF16)
    return dot(matrix[...], stack)[0 : value.shape[0]]


def strided(pair, at, count, stride):
    return [ref[pl.ds(at, count, stride=stride), :] for ref in pair]


def solve_own_kernel(sizes, sides, place, right, x_first, x_second, *refs):
    received, (fx, wz, out_a, out_b, first_a, first_b) = refs[:sides], refs[sides:]
    ext_x, ext_y, depth = right.shape
    wide = ext_x + 2 * OV
    low, high = from_ends(place, IX, sizes, x_first, x_second)
    batch = 8
    for start in range(0, wide, batch):
        cells, rims = [], []
        for a in range(start, start + batch):
            if a < OV:
                cells.append(low(a))
            elif a < ext_x + OV:
                cells.append(right[a - OV])
            else:
                cells.append(high(a - OV - ext_x))
            at = slice(a // GROUP * ext_y, (a // GROUP + 1) * ext_y)
            rims.append(rim_columns(place, sides, [ref[at] for ref in received], a % GROUP))
        out = z_forward(jnp.concatenate(cells, axis=0), jnp.concatenate(rims, axis=0), wz)
        block = pl.ds(start * ext_y, batch * ext_y)
        first_a[block] = out[:, 0:LANES]
        first_b[block] = out[:, LANES:]
    for y in range(ext_y):
        out = along(fx, strided((first_a, first_b), y, wide, ext_y))
        out_a[y * wide : (y + 1) * wide] = out[:, 0:LANES]
        out_b[y * wide : (y + 1) * wide] = out[:, LANES:]


def solve_rest_kernel(sizes, sides, place, axes, x_values, scale, y_first, y_second, own_a, own_b, *refs):
    fx, bx, fy, by, wz, bz, den, back_a, back_b, first, second = refs[:11]
    edge_a, edge_b, halo_a, halo_b, mode_a, mode_b = refs[11:]
    wide = x_values.shape[1]
    rows = back_a.shape[0]
    wide_y = rows // wide
    ext_y = wide_y - 2 * OV
    groups = (wide + GROUP - 1) // GROUP
    low, high = from_ends(place, IY, sizes, y_first, y_second)
    both = []
    for side in range(sides):
        values = []
        for group in range(groups):
            at = wide * OV + wide - 2 * OV + (side * groups + group) * OV
            values.append(jnp.concatenate([high(slice(at, at + OV)), low(slice(at, at + OV))], axis=0))
        both.append(values)
    cells, rims = [], []
    for a in range(wide):
        part = slice(a * OV, (a + 1) * OV)
        cells.append(jnp.concatenate([high(part), low(part)], axis=0))
        rims.append(rim_columns(place, sides, [values[a // GROUP] for values in both], a % GROUP))
    out = z_forward(jnp.concatenate(cells, axis=0), jnp.concatenate(rims, axis=0), wz)
    edge_a[...] = out[:, 0:LANES]
    edge_b[...] = out[:, LANES:]
    for t in range(2 * OV):
        out = along(fx, strided((edge_a, edge_b), t, wide, 2 * OV))
        halo_a[t * wide : (t + 1) * wide] = out[:, 0:LANES]
        halo_b[t * wide : (t + 1) * wide] = out[:, LANES:]
    for i in range(wide):
        pair = []
        for inside, outside in ((own_a, halo_a), (own_b, halo_b)):
            parts = strided((inside,), i, ext_y, wide) + strided((outside,), i, 2 * OV, wide)
            pair.append(jnp.concatenate(parts, axis=0))
        out = along(fy, pair)
        inverse = 1.0 / (axes[:, 0:1] * x_values[:, i : i + 1] + den[...])
        out = along(by, [out[:, 0:LANES] * inverse, out[:, LANES:] * inverse])
        mode_a[pl.ds(i * wide_y, wide_y)] = out[:, 0:LANES]
        mode_b[pl.ds(i * wide_y, wide_y)] = out[:, LANES:]
    for y in range(wide_y):
        out = along(bx, strided((mode_a, mode_b), y, wide, wide_y))
        back_a[pl.ds(y, wide, stride=wide_y), :] = out[:, 0:LANES]
        back_b[pl.ds(y, wide, stride=wide_y), :] = out[:, LANES:]
    even = is_even(place, IX)
    ends = RIM * wide_y
    low, low_rims = z_back(sides, wide_y, back_a, back_b, bz, 0, RIM)
    high, high_rims = z_back(sides, wide_y, back_a, back_b, bz, wide - RIM, RIM)
    first[0:ends] = jnp.where(even, high, low)
    second[0:ends] = jnp.where(even, low, high)
    third = fold_rows(wide_y)
    for side in range(sides):
        low = folded(sum(low_rims[side].values()), 0)
        high = folded(sum(high_rims[side].values()), (wide - RIM) % GROUP * SLOT)
        at = ends + side * third
        first[at : at + third] = jnp.where(even, high, low)
        second[at : at + third] = jnp.where(even, low, high)
    low, high = scale[0].astype(F32), scale[scale.shape[0] - 1].astype(F32)
    at = ends + sides * third
    first[at : at + ext_y] = jnp.where(even, high, low)
    second[at : at + ext_y] = jnp.where(even, low, high)


def fold_rows(rows):
    return (rows // 3 + 7) // 8 * 8


def folded(value, start):
    third, lanes = fold_rows(value.shape[0]), RIM * SLOT
    value = pltpu.roll(value, LANES - start, 1) if start else value
    last = jnp.concatenate([value[2 * third :], jnp.zeros((3 * third - value.shape[0], LANES), F32)], axis=0)
    return value[:third] + pltpu.roll(value[third : 2 * third], lanes, 1) + pltpu.roll(last, 2 * lanes, 1)


def unfolded(value, rows, start):
    third, lanes = value.shape[0], RIM * SLOT
    parts = [value, pltpu.roll(value, LANES - lanes, 1), pltpu.roll(value, LANES - 2 * lanes, 1)[: rows - 2 * third]]
    whole = jnp.concatenate(parts, axis=0)
    whole = pltpu.roll(whole, start, 1) if start else whole
    lane = iota(whole.shape, 1)
    return jnp.where((lane >= start) & (lane < start + lanes), whole, 0.0)


def z_back(sides, wide_y, back_a, back_b, bz, start, count):
    lane = iota((wide_y, LANES), 1)
    block = pl.ds(start * wide_y, count * wide_y)
    high_a, low_a = halves(back_a[block])
    high_b, low_b = halves(back_b[block])
    out = dot(jnp.concatenate([high_a, high_b, low_a, low_b, high_a, high_b], axis=1), bz[...])
    rims = [{} for _ in range(sides)]
    for a in range(start, start + count):
        group, q = a // GROUP, a % GROUP
        value = out[(a - start) * wide_y : (a - start + 1) * wide_y, LANES:]
        for side in range(sides):
            own = value if sides == 1 else jnp.where(lane // SLOT == side, value, 0.0)
            at = (SLOT * q + LANES - SLOT * side) % LANES
            moved = pltpu.roll(own, at, 1) if at else own
            rims[side][group] = rims[side][group] + moved if group in rims[side] else moved
    return out[:, 0:LANES], rims


def solve_tail_kernel(sides, wide, place, back_a, back_b, bz, local, *rims):
    wide_y = back_a.shape[0] // wide
    for side in range(sides):
        rims[side][...] = jnp.zeros_like(rims[side])
    count = 10
    for start in range(OV - 1, wide - OV + 1, count):
        out, more = z_back(sides, wide_y, back_a, back_b, bz, start, count)
        at = start - OV + 1
        local[at * wide_y : (at + count) * wide_y] = out
        for side in range(sides):
            for group, value in more[side].items():
                rims[side][group * wide_y : (group + 1) * wide_y] += value


def placed_rims(place, sides, received, a, rows):
    total = None
    for side in range(sides):
        is_high, valid = place[SIDE + 2 * side] > 0, place[SIDE + 2 * side + 1] > 0
        start = jnp.where(is_high, LANES - OV, 0)
        shift = lax.rem(jnp.where(is_high, LANES - OV, LANES - 1) + LANES - SLOT * (a % GROUP), LANES)
        value = received[side][rows]
        lane = iota(value.shape, 1)
        value = jnp.where((lane >= start) & (lane < start + OV) & valid, pltpu.roll(value, shift, 1), 0.0)
        total = value if total is None else total + value
    return total


def pack_back_z_kernel(sizes, sides, wide, wide_y, place, x_first, x_second, *refs):
    own, out = refs[:sides], refs[sides:]
    _, faces = x_received(sizes, wide, wide_y, place, x_first, x_second)
    for side in range(sides):
        for group in range((wide + GROUP - 1) // GROUP):
            part = slice(group * wide_y, (group + 1) * wide_y)
            more = faces(side, group)
            out[side][part] = own[side][part] if more is None else own[side][part] + more


def fold_x_kernel(sizes, wide, wide_y, place, x_first, x_second, local, out):
    plane, _ = x_received(sizes, wide, wide_y, place, x_first, x_second)
    for p in range(wide - 2 * OV + 2):
        part = slice(p * wide_y, (p + 1) * wide_y)
        more = plane(p + OV - 1, slice(0, wide_y))
        out[part] = local[part] if more is None else local[part] + more


def pack_back_y_kernel(sides, wide, wide_y, place, field, *refs):
    own, received = refs[:sides], refs[sides : 2 * sides]
    faces, (first, second) = refs[2 * sides : 3 * sides], refs[3 * sides :]
    groups = (wide + GROUP - 1) // GROUP
    planes = wide - 2 * OV + 2
    even = is_even(place, IY)

    def put(at, low, high):
        first[at : at + RIM] = jnp.where(even, high, low)
        second[at : at + RIM] = jnp.where(even, low, high)

    lane = iota((groups * wide_y, LANES), 1)
    for side in range(sides):
        is_high, valid = place[SIDE + 2 * side] > 0, place[SIDE + 2 * side + 1] > 0
        other = pltpu.roll(received[side][...], jnp.where(is_high, LANES - OV, 0), 1)
        mine = pltpu.roll(own[side][...], jnp.where(is_high, LANES - 1, LANES - OV + 1), 1)
        faces[side][...] = jnp.where((lax.rem(lane, SLOT) == 0) & valid, other + mine, 0.0)
        for group in range(groups):
            low = faces[side][group * wide_y : group * wide_y + 8]
            high = faces[side][(group + 1) * wide_y - 8 : (group + 1) * wide_y]
            put(planes * RIM + (side * groups + group) * RIM, low[0:RIM], high[8 - RIM :])
    for p in range(planes):
        a = p + OV - 1
        ends = []
        for start in (0, wide_y - 8):
            at = a // GROUP * wide_y + start
            value = placed_rims(place, sides, received, a, slice(at, at + 8))
            ends.append(field[p * wide_y + start : p * wide_y + start + 8] + value)
        put(p * RIM, ends[0][0:RIM], ends[1][8 - RIM :])


def x_received(sizes, wide, wide_y, place, x_first, x_second):
    low, high = from_ends(place, IX, sizes, x_first, x_second)
    high_lane = (wide - 2 * OV) % GROUP * SLOT

    def plane(a, rows):
        if OV - 1 <= a < OV - 1 + RIM:
            at, source = (a - OV + 1) * wide_y, low
        elif wide - 2 * OV <= a < wide - 2 * OV + RIM:
            at, source = (a - wide + 2 * OV) * wide_y, high
        else:
            return None
        return source(slice(at + rows.start, at + rows.stop))

    def faces(side, group):
        third = fold_rows(wide_y)
        rows = slice(RIM * wide_y + side * third, RIM * wide_y + (side + 1) * third)
        if group == 0:
            return unfolded(low(rows), wide_y, (OV - 1) * SLOT)
        if group == (wide + GROUP - 1) // GROUP - 1:
            return unfolded(high(rows), wide_y, high_lane)
        return None

    return plane, faces


def weights_kernel(sizes, sides, place, axes, right, scale, x_first, x_second, y_first, y_second, *refs):
    scale_faces = refs[:sides]
    wx, wy, wz, z_weight, sums, scales = refs[sides:]
    ext_x, ext_y, depth = right.shape
    core = slice(8, 8 + ext_y)
    x_low, x_high = from_ends(place, IX, sizes, x_first, x_second)
    y_low, y_high = from_ends(place, IY, sizes, y_first, y_second)
    y_rows = (ext_x + 2 * OV) * OV
    x_rows = slice(x_first.shape[0] - ext_y, x_first.shape[0])
    scales[0, core] = x_low(x_rows)
    scales[ext_x + 1, core] = x_high(x_rows)
    for x in range(ext_x):
        scales[x + 1, core] = scale[x].astype(F32)
        part = slice(y_rows + x, y_rows + x + 1)
        scales[x + 1, 7:8] = y_low(part)
        scales[x + 1, 8 + ext_y : 9 + ext_y] = y_high(part)
    hx, hy, hz = (0.5 * axes[:, d : d + 1] for d in range(3))
    lane = iota((8, depth), 1)
    ends = (lane == 0) | (lane == depth - 1)
    zero = jnp.zeros((8, depth), F32)
    sum_right, sum_z = zero, zero
    for x in range(ext_x + 1):
        wx[x] = hx * (scales[x, core] + scales[x + 1, core])
    for x in range(ext_x):
        wy[x, 0 : ext_y + 1] = hy * (scales[x + 1, 7 : 8 + ext_y] + scales[x + 1, 8 : 9 + ext_y])
        for row in range(0, ext_y, 8):
            own = scales[x + 1, 8 + row : 16 + row]
            edge = zero
            for side in range(sides):
                is_high, valid = place[SIDE + 2 * side] > 0, place[SIDE + 2 * side + 1] > 0
                target = jnp.where(is_high, depth - 1, 0)
                at = x // GROUP * ext_y + row
                shift = lax.rem(target + depth - (x % GROUP * SLOT + OV), depth)
                edge = jnp.where((lane == target) & valid, pltpu.roll(scale_faces[side][at : at + 8], shift, 1), edge)
            wz[x, row : row + 8] = hz * (own + jnp.where(lane == 0, edge, pltpu.roll(own, 1, 1)))
            end_weight = jnp.where(ends, hz * (own + edge), 0.0)
            z_weight[x, row : row + 8] = end_weight
            sum_z = sum_z + end_weight
            sum_right = sum_right + right[x, row : row + 8]

    def whole(value):
        return jnp.sum(jnp.sum(value, axis=0, keepdims=True), axis=1, keepdims=True)

    def y_sum(row):
        total = jnp.zeros((1, depth), F32)
        for x in range(ext_x):
            total = total + wy[x, row : row + 1]
        return whole(total)

    x_high_sum, y_high_sum = whole(wx[ext_x]), y_sum(ext_y)
    z_high_sum = whole(jnp.where(lane == depth - 1, sum_z, 0.0))
    faces_sum = whole(wx[0]) + x_high_sum + y_sum(0) + y_high_sum + whole(sum_z)
    columns = {
        0: whole(sum_right),
        4: faces_sum,
        5: jnp.where(place[IX] < sizes["gx"] - 1, x_high_sum, 0.0),
        6: jnp.where(place[IY] < sizes["gy"] - 1, y_high_sum, 0.0),
        7: jnp.where(place[IZ] < sizes["gz"] - 1, z_high_sum, 0.0),
    }
    sums[...] = in_columns(columns, jnp.zeros((1, LANES), F32))


def in_columns(columns, row):
    at = iota((1, LANES), 1)
    for number, value in columns.items():
        row = jnp.where(at == number, value, row)
    return row


def operator_tile(place, sides, groups, values, edges, wx, wy, wz, z_weight, block, inner, row):
    depth = values.shape[2]
    ext_y = z_weight.shape[1]
    lane = iota((8, depth), 1)
    at = slice(8 + row, 16 + row)
    x = block * GROUP + inner
    mid = values[x + 1, at]
    total = wx[x, row : row + 8] * (mid - values[x, at]) + wx[x + 1, row : row + 8] * (mid - values[x + 2, at])
    total = total + wy[x, row : row + 8] * (mid - values[x + 1, 7 + row : 15 + row])
    total = total + wy[x, row + 1 : row + 9] * (mid - values[x + 1, 9 + row : 17 + row])
    edge = jnp.zeros((8, depth), F32)
    for side in range(sides):
        is_high, valid = place[SIDE + 2 * side] > 0, place[SIDE + 2 * side + 1] > 0
        target = jnp.where(is_high, depth - 1, 0)
        start = (side * groups + block + (inner + OV) // GROUP) * ext_y + row
        moved = edges[pl.ds(pl.multiple_of(start, 8), 8)]
        q = (inner + OV) % GROUP
        if q:
            moved = pltpu.roll(moved, depth - q * SLOT, 1)
        edge = jnp.where((lane == target) & valid, moved, edge)
    flux = wz[x, row : row + 8] * (mid - jnp.where(lane == 0, edge, pltpu.roll(mid, 1, 1)))
    above = z_weight[x, row : row + 8] * (mid - edge)
    total = total + flux + jnp.where(lane == depth - 1, above, -pltpu.roll(flux, depth - 1, 1))
    return mid, total


def operator_tiles(place, sides, groups, right, values, edges, weights, applied, sums, rows):
    def several(block, totals):
        product, energy, whole = totals
        for inner in range(GROUP):
            x = block * GROUP + inner
            for row in rows:
                mid, total = operator_tile(place, sides, groups, values, edges, *weights, block, inner, row)
                applied[x, row : row + 8] = total
                product = product + right[x, row : row + 8] * mid
                energy = energy + mid * total
                whole = whole + total
        return product, energy, whole

    totals = lax.fori_loop(0, right.shape[0] // GROUP, several, (jnp.zeros((8, values.shape[2]), F32),) * 3)
    for number, value in enumerate(totals):
        sums[number * 8 : (number + 1) * 8] = value


def to_face(place, side, value):
    return pltpu.roll(value, jnp.where(place[SIDE + 2 * side] > 0, LANES - 1, 0), 1)


def inner_kernel(sizes, sides, wide, place, right, field, *refs):
    received, faces, weights = refs[:sides], refs[sides : 2 * sides], refs[2 * sides : 2 * sides + 4]
    values, edges, applied, sums = refs[2 * sides + 4 :]
    ext_x, ext_y, depth = right.shape
    wide_y = ext_y + 2 * OV
    groups = (wide + GROUP - 1) // GROUP
    inside_low, inside_high = place[IX] > 0, place[IX] < sizes["gx"] - 1
    for p in range(ext_x + 2):
        a = p + OV - 1
        at = a // GROUP * wide_y
        value = placed_rims(place, sides, received, a, slice(at, at + wide_y))
        value = value + field[p * wide_y : (p + 1) * wide_y]
        if p == 0:
            value = jnp.where(inside_low, value, 0.0)
        if p == ext_x + 1:
            value = jnp.where(inside_high, value, 0.0)
        values[p, 8 - OV : 8 - OV + wide_y] = value
    for side in range(sides):
        for group in range(groups):
            value = faces[side][group * wide_y : (group + 1) * wide_y]
            at = (side * groups + group) * ext_y
            edges[at : at + ext_y] = to_face(place, side, value)[OV : OV + ext_y]
    operator_tiles(place, sides, groups, right, values, edges, weights, applied, sums, range(8, ext_y - 8, 8))


def outer_kernel(sizes, sides, wide, place, right, y_first, y_second, *refs):
    weights, fixed, refs = refs[:4], refs[4], refs[5:]
    inner_sums, refs = refs[3], refs[4:]
    values, edges, applied, out, sums = refs
    ext_x, ext_y, depth = right.shape
    wide_y = ext_y + 2 * OV
    groups = (wide + GROUP - 1) // GROUP
    low, high = from_ends(place, IY, sizes, y_first, y_second)
    inside_low, inside_high = place[IY] > 0, place[IY] < sizes["gy"] - 1
    for p in range(ext_x + 2):
        part = slice(p * RIM, (p + 1) * RIM)
        low_rows, high_rows = low(part), high(part)
        if p == 0 or p == ext_x + 1:
            inside = place[IX] > 0 if p == 0 else place[IX] < sizes["gx"] - 1
            low_rows, high_rows = (jnp.where(inside, rows, 0.0) for rows in (low_rows, high_rows))
        values[p, 7 : 7 + RIM] += low_rows
        values[p, 4 + ext_y : 4 + ext_y + RIM] += high_rows
        values[p, 7:8] = jnp.where(inside_low, values[p, 7:8], 0.0)
        values[p, 8 + ext_y : 9 + ext_y] = jnp.where(inside_high, values[p, 8 + ext_y : 9 + ext_y], 0.0)
    for number in range(sides * groups):
        at = (ext_x + 2 + number) * RIM
        start = number * ext_y
        side = number // groups
        edges[start : start + OV] += to_face(place, side, low(slice(at, at + RIM)))[1:]
        edges[start + ext_y - OV : start + ext_y] += to_face(place, side, high(slice(at, at + RIM)))[:OV]
    operator_tiles(place, sides, groups, right, values, edges, weights, applied, sums, (0, ext_y - 8))
    columns = {}
    for number in range(3):
        part = slice(number * 8, (number + 1) * 8)
        value = inner_sums[part] + sums[part]
        columns[number + 1] = jnp.sum(jnp.sum(value, axis=0, keepdims=True), axis=1, keepdims=True)
    out[...] = jnp.broadcast_to(in_columns(columns, fixed[...]), out.shape)


def finish_kernel(sizes, place, sums, spread, values, applied, wx, wy, z_weight, right, solution, residual, held_s, held_r, sems):
    ext_x, ext_y, depth = right.shape
    nx, ny, nz = (sizes[a] for a in MESH_AXES)
    count = nx * ny * nz
    table = sums[...]
    part = [table[:, k : k + 1] for k in range(8)]
    from_device = iota((count, count), 0) == iota((count, count), 1)
    sums_row = jnp.sum(jnp.where(from_device, part[0], 0.0), axis=0, keepdims=True)
    level = jnp.sum(spread[...] * sums_row, axis=1, keepdims=True)

    def shifted(by):
        return jnp.concatenate([level[by:], level[:by]], axis=0)

    def whole(value):
        return jnp.sum(value, axis=0, keepdims=True)

    product = whole(part[1] + level * part[0])
    neighbours = part[5] * shifted(ny * nz) + part[6] * shifted(nz) + part[7] * shifted(1)
    curvature = whole(part[2] + 2.0 * level * part[3] + level * (level * part[4] - 2.0 * neighbours))
    step = product / curvature
    device = iota((count, 1), 0)
    mine = (place[IX] * ny + place[IY]) * nz + place[IZ]

    def level_at(number, inside):
        return whole(jnp.where((device == number) & inside, level, 0.0))

    own = level_at(mine, True)
    drops = []
    for axis, stride, size in ((IX, ny * nz, nx), (IY, nz, ny), (IZ, 1, nz)):
        drops.append(step * (own - level_at(mine - stride, place[axis] > 0)))
        drops.append(step * (own - level_at(mine + stride, place[axis] < size - 1)))
    z_drop = jnp.where(iota((1, depth), 1) < depth // 2, drops[4], drops[5])
    chunk = 12
    for x in range(ext_x):
        held_s[x] = step * (values[x + 1, 8 : 8 + ext_y] + own)
        value = right[x] - step * applied[x] - z_drop * z_weight[x]
        if x == 0:
            value = value - drops[0] * wx[0]
        if x == ext_x - 1:
            value = value - drops[1] * wx[ext_x]
        held_r[x] = value
        held_r[x, 0:1] = value[0:1] - drops[2] * wy[x, 0:1]
        held_r[x, ext_y - 1 : ext_y] = value[ext_y - 1 : ext_y] - drops[3] * wy[x, ext_y : ext_y + 1]
        if (x + 1) % chunk == 0:
            part_x = pl.ds(x + 1 - chunk, chunk)
            number = (x + 1) // chunk - 1
            pltpu.make_async_copy(held_s.at[part_x], solution.at[part_x], sems.at[0, number]).start()
            pltpu.make_async_copy(held_r.at[part_x], residual.at[part_x], sems.at[1, number]).start()
    for number in range(ext_x // chunk):
        part_x = pl.ds(number * chunk, chunk)
        pltpu.make_async_copy(held_s.at[part_x], solution.at[part_x], sems.at[0, number]).wait()
        pltpu.make_async_copy(held_r.at[part_x], residual.at[part_x], sems.at[1, number]).wait()


def body(sizes, right, scale, axes, xv, yv, zv, x_values, y_values, z_values, inverse):
    ext_x, ext_y, depth = right.shape
    wide_x, wide_y = xv.shape[0], yv.shape[0]
    sides = 1 if sizes["gz"] == 2 else 2
    groups = (wide_x + GROUP - 1) // GROUP
    count = sizes["gx"] * sizes["gy"] * sizes["gz"]
    bind = functools.partial
    run = bind(call, sizes)
    block = shape(right.shape)
    axes_row = axes.reshape(1, -1)
    beside = 2 * 10**9

    up = lax.rem(lax.axis_index("gx"), 2) == 0
    starts = jnp.where(up, ext_x - OV, 0), jnp.where(up, 0, ext_x - OV)
    xs = [lax.dynamic_slice_in_dim(right, start, OV, 0) for start in starts]
    xs = swap_ends(*xs, "gx", sizes)

    rim_message = [shape([groups * ext_y, LANES])] * sides
    rims = run(
        bind(pack_z_kernel, None, True, sides),
        "pack_z_own",
        rim_message,
        [right, scale],
        [VMEM] * 2,
        flops=beside,
    )
    y_message = [shape([wide_x * OV + ext_x + sides * groups * OV, depth])] * 2
    ys = run(pack_y_own_kernel, "pack_y_own", y_message, [right, scale], [VMEM] * 2, flops=beside)
    rims, ys = lax.optimization_barrier((rims, ys))
    rims = run(
        bind(pack_z_kernel, sizes, False, sides),
        "pack_z_rest",
        rim_message,
        [*xs, *rims],
        [VMEM] * (2 + sides),
        aliases={2 + k: k for k in range(sides)},
    )
    rims, late_zv = lax.optimization_barrier((rims, zv))
    rims = swap_sides(rims, sizes)
    thin = [shape([LANES // 2, 3 * size], BF16) for size in (wide_x, wide_x, wide_y, wide_y)]
    *mats, spread = run(
        bind(prepare_kernel, sides, 2.0 * ext_x * ext_y * depth),
        "prepare",
        thin + [shape([4 * depth, 2 * LANES], BF16), shape([6 * LANES, 2 * LANES], BF16), shape([wide_y, LANES]), shape([count, count])],
        [axes_row, xv, yv, late_zv, y_values.reshape(1, -1), z_values.reshape(1, -1), inverse],
        [VMEM] * 7,
        [pltpu.VMEM((LANES, LANES), F32), pltpu.VMEM((depth + 2 * OV, 2 * LANES), F32), pltpu.VMEM((LANES, 2 * LANES), F32)],
        flops=beside,
    )

    ys = run(
        bind(pack_y_rest_kernel, sizes, sides, wide_x),
        "pack_y_rest",
        y_message,
        [*xs, *rims, *ys],
        [VMEM] * (4 + sides),
        aliases={2 + sides: 0, 3 + sides: 1},
    )
    ys = swap_ends(*ys, "gy", sizes)

    fx, _, _, _, wz, _, _ = mats
    tall = pltpu.VMEM((wide_x * wide_y, LANES), F32)
    core = pltpu.VMEM((wide_x * ext_y, LANES), F32)
    owns = run(
        bind(solve_own_kernel, sizes, sides),
        "solve_own",
        [shape([wide_x * ext_y, LANES])] * 2,
        [right, *xs, *rims, fx, wz],
        [VMEM] * (5 + sides),
        [core] * 2,
        limit=16,
        flops=2 * beside,
    )
    field = shape([wide_x * wide_y, depth])
    rim_message = shape([groups * wide_y, LANES])
    edge = pltpu.VMEM((wide_x * 2 * OV, LANES), F32)
    *back, low, high = run(
        bind(solve_rest_kernel, sizes, sides),
        "solve_rest",
        [field] * 2 + [shape([RIM * wide_y + sides * fold_rows(wide_y) + ext_y, depth])] * 2,
        [axes_row, x_values.reshape(1, -1), scale, *ys, *owns, *mats],
        [VMEM] * (7 + len(mats)),
        [edge] * 4 + [tall] * 2,
        limit=20,
    )
    back_xs = swap_ends(low, high, "gx", sizes)

    planes = ext_x + 2
    field = shape([planes * wide_y, depth])
    local, *own_rims = run(
        bind(solve_tail_kernel, sides, wide_x),
        "solve_tail",
        [field] + [rim_message] * sides,
        [*back, mats[5]],
        [VMEM] * 3,
        flops=beside,
    )
    own_rims = run(
        bind(pack_back_z_kernel, sizes, sides, wide_x, wide_y),
        "pack_back_z",
        [rim_message] * sides,
        [*back_xs, *own_rims],
        [VMEM] * (2 + sides),
    )
    other_rims = swap_sides(own_rims, sizes)
    field_x = run(
        bind(fold_x_kernel, sizes, wide_x, wide_y),
        "fold_x",
        [field],
        [*back_xs, local],
        [VMEM] * 3,
        flops=beside,
    )[0]
    *faces, low, high = run(
        bind(pack_back_y_kernel, sides, wide_x, wide_y),
        "pack_back_y",
        [rim_message] * sides + [shape([(planes + groups * sides) * RIM, depth])] * 2,
        [field_x, *own_rims, *other_rims],
        [VMEM] * (1 + 2 * sides),
    )
    back_ys = swap_ends(low, high, "gy", sizes)

    faces, late_rims = lax.optimization_barrier((faces, rims))
    scale_block = pltpu.VMEM((planes, ext_y + 16, depth), F32)
    *weights, fixed = run(
        bind(weights_kernel, sizes, sides),
        "weights",
        [shape([ext_x + 1, ext_y, depth]), shape([ext_x, ext_y + 8, depth]), block, block, shape([1, LANES])],
        [axes_row, right, scale, *back_xs, *ys, *late_rims],
        [VMEM] * (7 + sides),
        [scale_block],
        flops=beside,
    )

    parts = [shape([planes, ext_y + 16, depth]), shape([sides * groups * ext_y, LANES]), block]
    inner = run(
        bind(inner_kernel, sizes, sides, wide_x),
        "inner",
        parts + [shape([24, depth])],
        [right, field_x, *other_rims, *faces, *weights],
        [VMEM] * (6 + 2 * sides),
        flops=beside,
    )
    values, edges, applied, sums = run(
        bind(outer_kernel, sizes, sides, wide_x),
        "outer",
        parts + [shape([count, LANES])],
        [right, *back_ys, *weights, fixed, *inner],
        [VMEM] * 12,
        [pltpu.VMEM((24, depth), F32)],
        aliases={8: 0, 9: 1, 10: 2},
    )
    sums = lax.all_to_all(sums, MESH_AXES, 0, 0, tiled=True)

    held = pltpu.VMEM(right.shape, F32)
    wx, wy, _, z_weight = weights
    return tuple(
        run(
            bind(finish_kernel, sizes),
            "finish",
            [block] * 2,
            [sums, spread, values, applied, wx, wy, z_weight, right],
            [VMEM] * 8,
            [held, held, pltpu.SemaphoreType.DMA((2, ext_x // 12))],
            out_specs=[ANY] * 2,
        )
    )


def solution(mesh):
    sizes = dict(mesh.shape)
    in_specs = (P(*MESH_AXES), P(*MESH_AXES), P(), P(), P(), P(), P(), P(), P(), P())
    out_specs = (P(*MESH_AXES), P(*MESH_AXES))
    return jax.shard_map(functools.partial(body, sizes), mesh=mesh, in_specs=in_specs, out_specs=out_specs, check_vma=False)
```
